256 devices in a mesh: dp: 64 (over z, y, core), mp: 4 (over x).
Axes of the slice: x: 4, y: 4, z: 8, core: 2. Of those that a mesh axis runs over, the one named last changes fastest.
Arguments:
- gradient: bfloat16 [2048, 16384], P('dp', 'mp')
- block_owner: int32 [4, 32], replicated, may hold values from 0 to 63, as said below
- prev_left: float32 [4, 64, 2, 512, 512], P('mp', 'dp'), as said below
- prev_right: float32 [4, 64, 2, 512, 512], P('mp', 'dp'), as said below
Outputs:
- update_out: bfloat16 [2048, 16384], P('dp', 'mp')
- new_left: float32 [4, 64, 2, 512, 512], P('mp', 'dp')
- new_right: float32 [4, 64, 2, 512, 512], P('mp', 'dp')
The draws below stay inside these ranges and needn't reach their ends.
Inputs may be any that keep to these rules, and one draw needn't show every extreme that they name: `block_owner`: within each column shard of 8 column blocks, each owner holds at most 2 blocks, and some owner holds exactly 2; no owner holds two blocks of the same row block of one column shard. `prev_left`: each slot is symmetric positive definite. `prev_right`: each slot is symmetric positive definite.
All inputs are finite; a program needn't handle non-finite values.
Results may differ from the reference program's by a relative error of at most 0.001.
Values may be sent and summed in bfloat16 or wider, within the bound.
No kernel may reach another device: no remote copies, remote signals or barrier semaphores. Data moves between devices by JAX's collectives and lax.ppermute only.
A program may use at most 128 MiB of HBM per device.

```python
import math
import jax
import jax.numpy as jnp
from jax import lax

BLOCK = 512
COLS = 16384
ROWS = 2048
ITERS = 2
ROW_BLOCKS = 4
COL_BLOCKS = 32
SHARDS = 4
SHARD_BLOCKS = 8
OWNERS = 64
SLOTS = 2


def draw_gradient(key, part):
    key = jax.random.fold_in(key, 5)
    sub_keys = jax.random.split(key, 3)
    position = jnp.arange(ROWS, dtype=jnp.float32)[:, None]
    row_scale = jnp.exp(jax.random.uniform(sub_keys[0], (ROWS, 1), jnp.float32, math.log(0.5), math.log(1.5))) * (1.0 + 2.0 * position / ROWS)
    col_scale = jnp.exp(jax.random.uniform(sub_keys[1], (1, COLS), jnp.float32, math.log(0.3), math.log(3.0)))
    noise_field = jax.random.normal(sub_keys[2], (ROWS, COLS), jnp.float32)
    return (noise_field * row_scale * col_scale).astype(jnp.bfloat16)


def draw_block_owner(key, part):
    key = jax.random.fold_in(key, 11)
    cell_count = ROW_BLOCKS * SHARD_BLOCKS
    spread = (cell_count + SLOTS - 1) // SLOTS
    tables = []
    for shard_index in range(SHARDS):
        sub_key = jax.random.fold_in(key, shard_index)
        holders = jax.random.permutation(jax.random.fold_in(sub_key, 2), OWNERS).astype(jnp.int32)
        row_tables = []
        for row_index in range(ROW_BLOCKS):
            order = jax.random.permutation(jax.random.fold_in(sub_key, 100 + row_index), SHARD_BLOCKS).astype(jnp.int32)
            numbers = row_index * SHARD_BLOCKS + order
            row_tables.append(holders[numbers % spread])
        tables.append(jnp.stack(row_tables))
    return jnp.concatenate(tables, axis=1).astype(jnp.int32)


def stat_draw(key, lowest, highest, ratio_low, ratio_high):
    sub_keys = jax.random.split(key, 2)
    scales = jnp.sqrt(jnp.exp(jax.random.uniform(sub_keys[0], (SHARDS, OWNERS, SLOTS, BLOCK, 1), jnp.float32, math.log(lowest), math.log(highest))))
    kernel_ratio = jax.random.uniform(sub_keys[1], (SHARDS, OWNERS, SLOTS, 1, 1), jnp.float32, ratio_low, ratio_high)
    position = jnp.arange(BLOCK, dtype=jnp.float32)
    distance = jnp.abs(position[:, None] - position[None, :])
    return scales * jnp.swapaxes(scales, -1, -2) * jnp.exp(distance * jnp.log(kernel_ratio))


def draw_prev_left(key, part):
    key = jax.random.fold_in(key, 7)
    return stat_draw(key, 64.0, 1024.0, 0.5, 0.85)


def draw_prev_right(key, part):
    key = jax.random.fold_in(key, 9)
    return stat_draw(key, 64.0, 1024.0, 0.5, 0.85)


def setup_inputs(seed: int = 0) -> dict:
    keys = jax.random.split(jax.random.key(seed), 5)
    gradient = draw_gradient(jax.random.fold_in(keys[4], 71), 0)
    block_owner = draw_block_owner(jax.random.fold_in(keys[4], 71), 0)
    prev_left = draw_prev_left(jax.random.fold_in(keys[4], 71), 0)
    prev_right = draw_prev_right(jax.random.fold_in(keys[4], 71), 0)
    return {"gradient": gradient, "block_owner": block_owner, "prev_left": prev_left, "prev_right": prev_right}


EPS_DAMP = 1.0
BETA = 0.95

def multiply(left_mat, right_mat):
    return jnp.matmul(left_mat, right_mat, precision=lax.Precision.HIGHEST)

def inverse_root(statistic):
    identity = jnp.eye(BLOCK, dtype=jnp.float32)
    damped = statistic + EPS_DAMP * identity
    scaling = 0.25 * jnp.sqrt(jnp.sum(damped * damped))
    current = damped / scaling
    factor = 1.25 * identity - 0.25 * current
    product = factor
    for iteration in range(1, ITERS):
        square = multiply(factor, factor)
        current = multiply(square, multiply(square, current))
        factor = 1.25 * identity - 0.25 * current
        product = multiply(product, factor)
    return product * lax.rsqrt(jnp.sqrt(scaling))

def table_ranks(block_owner):
    cell_count = ROW_BLOCKS * SHARD_BLOCKS
    shard_tables = block_owner.reshape(ROW_BLOCKS, SHARDS, SHARD_BLOCKS).transpose(1, 0, 2).reshape(SHARDS, cell_count)
    position = jnp.arange(cell_count, dtype=jnp.int32)
    matched = shard_tables[:, :, None] == shard_tables[:, None, :]
    earlier = position[None, :] < position[:, None]
    slot_ranks = lax.optimization_barrier(jnp.sum(jnp.where(matched & earlier[None], 1, 0), axis=2)).astype(jnp.int32)
    return slot_ranks.reshape(SHARDS, ROW_BLOCKS, SHARD_BLOCKS).transpose(1, 0, 2).reshape(ROW_BLOCKS, COL_BLOCKS)

def reference(gradient, block_owner, prev_left, prev_right):
    slot_ranks = table_ranks(block_owner)
    block_index = jnp.arange(ROW_BLOCKS * COL_BLOCKS, dtype=jnp.int32)
    block_row = block_index // COL_BLOCKS
    block_col = block_index % COL_BLOCKS
    shard_of = (block_col // SHARD_BLOCKS).astype(jnp.int32)
    holder = block_owner[block_row, block_col]
    slot_of = slot_ranks[block_row, block_col]

    def one_block(block_entry):
        row_index, col_index, shard_index, holder_index, slot_place = block_entry
        block_piece = lax.dynamic_slice(gradient, (row_index * BLOCK, col_index * BLOCK), (BLOCK, BLOCK))
        left_stat = BETA * prev_left[shard_index, holder_index, slot_place] + jnp.dot(block_piece, block_piece.T, preferred_element_type=jnp.float32)
        right_stat = BETA * prev_right[shard_index, holder_index, slot_place] + jnp.dot(block_piece.T, block_piece, preferred_element_type=jnp.float32)
        raw_update = multiply(multiply(inverse_root(left_stat), block_piece.astype(jnp.float32)), inverse_root(right_stat))
        return (raw_update, left_stat, right_stat)
    updates, left_stats, right_stats = lax.map(one_block, (block_row, block_col, shard_of, holder, slot_of))
    grad_total = jnp.sum(jnp.square(gradient.astype(jnp.float32)))
    update_total = jnp.sum(jnp.square(updates))
    cell_count = ROWS * COLS
    graft = jnp.sqrt(grad_total / cell_count) * lax.rsqrt(update_total / cell_count + 1e-06)
    scaled = (updates * graft).astype(jnp.bfloat16)
    update_out = scaled.reshape(ROW_BLOCKS, COL_BLOCKS, BLOCK, BLOCK).transpose(0, 2, 1, 3).reshape(ROWS, COLS)
    new_left = (BETA * prev_left).at[shard_of, holder, slot_of].set(left_stats)
    new_right = (BETA * prev_right).at[shard_of, holder, slot_of].set(right_stats)
    return (update_out, new_left, new_right)
```

```python
import jax
import jax.numpy as jnp
from jax import lax
from jax.experimental import pallas as pl
from jax.experimental.pallas import tpu as pltpu
from jax.sharding import PartitionSpec as P

EPS_DAMP = 1.0
BETA = 0.95
BLOCK = 512
GROUPS = 4
MEMBERS = 16
PER_SHARD = 8
OWNERS = 64
SLOTS = 2
ROWS_DEV = 32
PIECE = 128
CELLS = 2048 * 16384

WHOLE = pl.BlockSpec(memory_space=pltpu.VMEM)
SMEM = pl.BlockSpec(memory_space=pltpu.SMEM)


def rank_table(owner_ref, where_ref, count_ref, place_ref):
    base = where_ref[0] * PER_SHARD

    def clear(o, _):
        count_ref[o] = 0
        return 0

    lax.fori_loop(0, OWNERS, clear, 0)

    def step(b, _):
        owner = owner_ref[b // PER_SHARD, base + b % PER_SHARD]
        slot = count_ref[owner]
        count_ref[owner] = slot + 1
        place_ref[b] = owner * SLOTS + slot
        return 0

    lax.fori_loop(0, GROUPS * PER_SHARD, step, 0)


def spread_kernel(where_ref, grad_ref, *out_refs):
    group = where_ref[1]
    for shift in range(GROUPS):
        chunk = lax.rem(group + shift, GROUPS)
        for j in range(PER_SHARD):
            columns = pl.ds(pl.multiple_of(j * BLOCK + chunk * PIECE, PIECE), PIECE)
            out_refs[shift][j] = grad_ref[:, columns]


def route_kernel(where_ref, owner_ref, *refs):
    in_refs, (out_ref, count_ref, place_ref) = refs[:GROUPS], refs[GROUPS:]
    rank_table(owner_ref, where_ref, count_ref, place_ref)
    group = where_ref[1]
    for shift in range(GROUPS):
        row = lax.rem(group + GROUPS - shift, GROUPS)
        for j in range(PER_SHARD):
            out_ref[place_ref[row * PER_SHARD + j]] = in_refs[shift][j]


def collect_kernel(where_ref, owner_ref, in_ref, *refs):
    out_refs, (count_ref, place_ref) = refs[:GROUPS], refs[GROUPS:]
    rank_table(owner_ref, where_ref, count_ref, place_ref)
    group = where_ref[1]
    for shift in range(GROUPS):
        row = lax.rem(group + shift, GROUPS)
        for j in range(PER_SHARD):
            out_refs[shift][j] = in_ref[place_ref[row * PER_SHARD + j]]


def place_kernel(where_ref, *refs):
    in_refs, out_ref = refs[:GROUPS], refs[GROUPS]
    group = where_ref[1]
    for shift in range(GROUPS):
        chunk = lax.rem(group + GROUPS - shift, GROUPS)
        for j in range(PER_SHARD):
            columns = pl.ds(pl.multiple_of(j * BLOCK + chunk * PIECE, PIECE), PIECE)
            out_ref[:, columns] = in_refs[shift][j]


def dot(a, b):
    return jnp.dot(a, b, preferred_element_type=jnp.float32)


def split(x):
    high = x.astype(jnp.bfloat16)
    return high, (x - high.astype(jnp.float32)).astype(jnp.bfloat16)


def dot3(a, b):
    return dot(a[0], b[0]) + (dot(a[0], b[1]) + dot(a[1], b[0]))


def root(stat, eye):
    damped = stat + EPS_DAMP * eye
    total = jnp.sum(damped * damped, keepdims=True)
    norm = jnp.sqrt(total)
    n = damped * (1.0 / norm)
    n_split = split(n)
    n2 = dot3(n_split, n_split)
    q = split(1.5625 * eye - 2.5 * n + n2)
    h = split(1.25 * n - n2)
    r = split(dot3(q, q))
    product = 1.5625 * eye - 1.25 * n - dot3(h, r)
    return product * lax.rsqrt(jnp.sqrt(0.25 * norm))


def owner_kernel(where_ref, owner_ref, got_ref, left_ref, right_ref, new_left_ref, new_right_ref,
                 raw_ref, sums_ref, block_ref):
    slot = pl.program_id(0)
    base = where_ref[0] * PER_SHARD
    me = where_ref[2]

    def step(b, held):
        return held + jnp.where(owner_ref[b // PER_SHARD, base + b % PER_SHARD] == me, 1, 0)

    held = lax.fori_loop(0, GROUPS * PER_SHARD, step, jnp.int32(0))
    used = held > slot
    for chunk in range(GROUPS):
        for member in range(MEMBERS):
            piece = got_ref[chunk * MEMBERS + member, 0]
            block_ref[pl.ds(member * ROWS_DEV, ROWS_DEV), pl.ds(chunk * PIECE, PIECE)] = jnp.where(
                used, piece, jnp.zeros_like(piece)
            )
    block = block_ref[...]
    turned = block.T
    rows = lax.broadcasted_iota(jnp.int32, (BLOCK, BLOCK), 0)
    columns = lax.broadcasted_iota(jnp.int32, (BLOCK, BLOCK), 1)
    eye = jnp.where(rows == columns, 1.0, 0.0).astype(jnp.float32)
    left = BETA * left_ref[0] + dot(block, turned)
    new_left_ref[0] = left
    right = BETA * right_ref[0] + dot(turned, block)
    new_right_ref[0] = right
    left_root = split(root(left, eye))
    half = split(dot(left_root[0], block) + dot(left_root[1], block))
    raw = dot3(half, split(root(right, eye)))
    raw_ref[0] = raw
    wide = block.astype(jnp.float32)
    grad_sq = jnp.sum(wide * wide, keepdims=True)
    update_sq = jnp.sum(raw * raw, keepdims=True)
    line = lax.broadcasted_iota(jnp.int32, (8, 128), 0)
    sums = jnp.where(line == 0, grad_sq, update_sq)

    @pl.when(slot == 0)
    def _():
        sums_ref[...] = sums

    @pl.when(slot > 0)
    def _():
        sums_ref[...] += sums


def scale_kernel(sums_ref, raw_ref, out_ref):
    grad_total = sums_ref[0:1, 0:1]
    update_total = sums_ref[1:2, 0:1]
    graft = jnp.sqrt(grad_total / CELLS) * lax.rsqrt(update_total / CELLS + 1e-06)
    for chunk in range(GROUPS):
        for member in range(MEMBERS):
            for slot in range(SLOTS):
                piece = raw_ref[slot, pl.ds(member * ROWS_DEV, ROWS_DEV), pl.ds(chunk * PIECE, PIECE)]
                out_ref[(chunk * MEMBERS + member) * SLOTS + slot] = (piece * graft).astype(jnp.bfloat16)


def between_groups(arrays):
    moved = [arrays[0]]
    for shift in range(1, GROUPS):
        pairs = [(d, (d + shift * MEMBERS) % OWNERS) for d in range(OWNERS)]
        moved.append(lax.ppermute(arrays[shift], "dp", pairs))
    return moved


def sum_everywhere(x):
    stages = [
        ("mp", [[(d, (d + s) % 4) for d in range(4)] for s in (1, 2, 3)]),
        ("dp", [[(d, d // 8 * 8 + (d + s) % 8) for d in range(OWNERS)] for s in (2, 4, 6)]),
        ("dp", [[(d, d ^ s) for d in range(OWNERS)] for s in (8, 16, 24)]),
        ("dp", [[(d, d ^ s) for d in range(OWNERS)] for s in (1, 32, 33)]),
    ]
    for axis, perms in stages:
        got = [lax.ppermute(x, axis, perm) for perm in perms]
        x = (x + got[0]) + (got[1] + got[2])
    return x


def shards(gradient, block_owner, prev_left, prev_right):
    my_index = lax.axis_index("dp")
    where = jnp.stack([lax.axis_index("mp"), my_index // MEMBERS, my_index]).astype(jnp.int32)
    piece_set = jax.ShapeDtypeStruct((PER_SHARD, ROWS_DEV, PIECE), jnp.bfloat16)
    rank_scratch = [pltpu.SMEM((OWNERS,), jnp.int32), pltpu.SMEM((GROUPS * PER_SHARD,), jnp.int32)]
    routed_shape = (OWNERS * SLOTS, ROWS_DEV, PIECE)

    pieces = pl.pallas_call(
        spread_kernel,
        out_shape=[piece_set] * GROUPS,
        in_specs=[SMEM, WHOLE],
        out_specs=[WHOLE] * GROUPS,
        name="spread",
    )(where, gradient)
    pieces = between_groups(pieces)
    routed = pl.pallas_call(
        route_kernel,
        out_shape=jax.ShapeDtypeStruct(routed_shape, jnp.bfloat16),
        in_specs=[SMEM, SMEM] + [WHOLE] * GROUPS,
        out_specs=WHOLE,
        scratch_shapes=rank_scratch,
        name="route",
    )(where, block_owner, *pieces)
    got = lax.all_to_all(
        routed.reshape(OWNERS, SLOTS, ROWS_DEV, PIECE), "dp", split_axis=0, concat_axis=0, tiled=True
    )

    stat_spec = pl.BlockSpec((1, BLOCK, BLOCK), lambda k: (k, 0, 0))
    stat_shape = jax.ShapeDtypeStruct((SLOTS, BLOCK, BLOCK), jnp.float32)
    new_left, new_right, raw, sums = pl.pallas_call(
        owner_kernel,
        grid=(SLOTS,),
        out_shape=[stat_shape, stat_shape, stat_shape, jax.ShapeDtypeStruct((8, 128), jnp.float32)],
        in_specs=[
            SMEM,
            SMEM,
            pl.BlockSpec((OWNERS, 1, ROWS_DEV, PIECE), lambda k: (0, k, 0, 0)),
            stat_spec,
            stat_spec,
        ],
        out_specs=[stat_spec, stat_spec, stat_spec, pl.BlockSpec((8, 128), lambda k: (0, 0))],
        scratch_shapes=[pltpu.VMEM((BLOCK, BLOCK), jnp.bfloat16)],
        compiler_params=pltpu.CompilerParams(vmem_limit_bytes=48 * 1024 * 1024),
        cost_estimate=pl.CostEstimate(
            flops=50 * 2 * BLOCK**3, bytes_accessed=12 * 1024 * 1024, transcendentals=0
        ),
        name="owner",
    )(where, block_owner, got, prev_left[0, 0], prev_right[0, 0])

    totals = sum_everywhere(sums)
    sending = pl.pallas_call(
        scale_kernel,
        out_shape=jax.ShapeDtypeStruct(routed_shape, jnp.bfloat16),
        in_specs=[WHOLE, WHOLE],
        out_specs=WHOLE,
        name="scale",
    )(totals, raw)
    returned = lax.all_to_all(
        sending.reshape(OWNERS, SLOTS, ROWS_DEV, PIECE), "dp", split_axis=0, concat_axis=0, tiled=True
    )
    back = pl.pallas_call(
        collect_kernel,
        out_shape=[piece_set] * GROUPS,
        in_specs=[SMEM, SMEM, WHOLE],
        out_specs=[WHOLE] * GROUPS,
        scratch_shapes=rank_scratch,
        name="collect",
    )(where, block_owner, returned.reshape(routed_shape))
    back = between_groups(back)
    update_out = pl.pallas_call(
        place_kernel,
        out_shape=jax.ShapeDtypeStruct(gradient.shape, jnp.bfloat16),
        in_specs=[SMEM] + [WHOLE] * GROUPS,
        out_specs=WHOLE,
        name="place",
    )(where, *back)
    return (update_out, new_left[None, None], new_right[None, None])


def solution(mesh):
    in_specs = (
        P("dp", "mp"),
        P(),
        P("mp", "dp", None, None, None),
        P("mp", "dp", None, None, None),
    )
    out_specs = (P("dp", "mp"), P("mp", "dp", None, None, None), P("mp", "dp", None, None, None))
    return jax.shard_map(shards, mesh=mesh, in_specs=in_specs, out_specs=out_specs, check_vma=False)
```

```python
import jax
import jax.numpy as jnp
from jax import lax
from jax.experimental import pallas as pl
from jax.experimental.pallas import tpu as pltpu
from jax.sharding import Mesh
from jax.sharding import PartitionSpec as P

EPS_DAMP = 1.0
BETA = 0.95
BLOCK = 512
SHARDS = 4
GROUPS = 4
MEMBERS = 16
PER_SHARD = 8
OWNERS = 64
SLOTS = 2
ROWS_DEV = 32
PIECE = 128
CELLS = 2048 * 16384

WHOLE = pl.BlockSpec(memory_space=pltpu.VMEM)
SMEM = pl.BlockSpec(memory_space=pltpu.SMEM)


def place_table_kernel(shard_ref, owner_ref, place_ref, count_ref):
    base = shard_ref[0] * PER_SHARD

    def clear(o, _):
        count_ref[o] = 0
        return 0

    lax.fori_loop(0, OWNERS, clear, 0, unroll=8)
    for b in range(GROUPS * PER_SHARD):
        owner = owner_ref[b // PER_SHARD, base + b % PER_SHARD]
        slot = count_ref[owner]
        count_ref[owner] = slot + 1
        place_ref[b] = owner * SLOTS + slot


def spread_kernel(grad_ref, out_ref):
    for chunk in range(GROUPS):
        for j in range(PER_SHARD):
            out_ref[chunk, j] = grad_ref[:, pl.ds(j * BLOCK + chunk * PIECE, PIECE)]


def route_kernel(place_ref, in_ref, out_ref):
    for row in range(GROUPS):
        for j in range(PER_SHARD):
            out_ref[place_ref[row * PER_SHARD + j]] = in_ref[row, j]


def collect_kernel(place_ref, in_ref, out_ref):
    for row in range(GROUPS):
        for j in range(PER_SHARD):
            out_ref[row, j] = in_ref[place_ref[row * PER_SHARD + j]]


def place_kernel(in_ref, out_ref):
    for chunk in range(GROUPS):
        for j in range(PER_SHARD):
            out_ref[:, pl.ds(j * BLOCK + chunk * PIECE, PIECE)] = in_ref[chunk, j]


def dot(a, b):
    return jnp.dot(a, b, preferred_element_type=jnp.float32)


def split(x):
    high = x.astype(jnp.bfloat16)
    return high, (x - high.astype(jnp.float32)).astype(jnp.bfloat16)


def dot3(a, b):
    return dot(a[0], b[0]) + (dot(a[0], b[1]) + dot(a[1], b[0]))


def root(stat, eye):
    damped = stat + EPS_DAMP * eye
    total = jnp.sum(damped * damped, keepdims=True)
    norm = jnp.sqrt(total)
    n = damped * (1.0 / norm)
    n_split = split(n)
    n2 = dot3(n_split, n_split)
    q = split(1.5625 * eye - 2.5 * n + n2)
    h = split(1.25 * n - n2)
    r = split(dot3(q, q))
    product = 1.5625 * eye - 1.25 * n - dot3(h, r)
    return product * lax.rsqrt(jnp.sqrt(0.25 * norm))


def owner_kernel(me_ref, place_ref, got_ref, left_ref, right_ref, new_left_ref, new_right_ref,
                 raw_ref, sums_ref, block_ref):
    slot = pl.program_id(0)
    wanted = me_ref[0] * SLOTS + slot
    used = place_ref[0] == wanted
    for b in range(1, GROUPS * PER_SHARD):
        used = used | (place_ref[b] == wanted)
    for chunk in range(GROUPS):
        for member in range(MEMBERS):
            piece = got_ref[chunk * MEMBERS + member, 0]
            block_ref[pl.ds(member * ROWS_DEV, ROWS_DEV), pl.ds(chunk * PIECE, PIECE)] = jnp.where(
                used, piece, jnp.zeros_like(piece)
            )
    block = block_ref[...]
    turned = block.T
    rows = lax.broadcasted_iota(jnp.int32, (BLOCK, BLOCK), 0)
    columns = lax.broadcasted_iota(jnp.int32, (BLOCK, BLOCK), 1)
    eye = jnp.where(rows == columns, 1.0, 0.0).astype(jnp.float32)
    left = BETA * left_ref[0] + dot(block, turned)
    new_left_ref[0] = left
    right = BETA * right_ref[0] + dot(turned, block)
    new_right_ref[0] = right
    left_root = split(root(left, eye))
    half = split(dot(left_root[0], block) + dot(left_root[1], block))
    raw = dot3(half, split(root(right, eye)))
    raw_ref[0] = raw
    wide = block.astype(jnp.float32)
    grad_sq = jnp.sum(wide * wide, keepdims=True)
    update_sq = jnp.sum(raw * raw, keepdims=True)
    line = lax.broadcasted_iota(jnp.int32, (GROUPS * SHARDS, 8, 128), 1)
    sums = jnp.where(line == 0, grad_sq[None], update_sq[None])

    @pl.when(slot == 0)
    def _():
        sums_ref[...] = sums

    @pl.when(slot > 0)
    def _():
        sums_ref[...] += sums


def scale_kernel(sums_ref, raw_ref, out_ref):
    totals = jnp.sum(sums_ref[...], axis=0)
    grad_total = totals[0:1, 0:1]
    update_total = totals[1:2, 0:1]
    graft = jnp.sqrt(grad_total / CELLS) * lax.rsqrt(update_total / CELLS + 1e-06)
    for chunk in range(GROUPS):
        for member in range(MEMBERS):
            for slot in range(SLOTS):
                piece = raw_ref[slot, pl.ds(member * ROWS_DEV, ROWS_DEV), pl.ds(chunk * PIECE, PIECE)]
                out_ref[(chunk * MEMBERS + member) * SLOTS + slot] = (piece * graft).astype(jnp.bfloat16)


def exchange(x, axes):
    return lax.all_to_all(x, axes, split_axis=0, concat_axis=0, tiled=True)


def shards(gradient, block_owner, prev_left, prev_right):
    shard = jnp.reshape(lax.axis_index("mp"), (1,)).astype(jnp.int32)
    me = jnp.reshape(lax.axis_index(("g", "r")), (1,)).astype(jnp.int32)
    spread_shape = jax.ShapeDtypeStruct((GROUPS, PER_SHARD, ROWS_DEV, PIECE), jnp.bfloat16)
    routed_shape = jax.ShapeDtypeStruct((OWNERS * SLOTS, ROWS_DEV, PIECE), jnp.bfloat16)
    sums_shape = (GROUPS * SHARDS, 8, 128)

    places = pl.pallas_call(
        place_table_kernel,
        out_shape=jax.ShapeDtypeStruct((GROUPS * PER_SHARD,), jnp.int32),
        in_specs=[SMEM, SMEM],
        out_specs=SMEM,
        scratch_shapes=[pltpu.SMEM((OWNERS,), jnp.int32)],
        cost_estimate=pl.CostEstimate(flops=1000, bytes_accessed=1000, transcendentals=0),
        name="places",
    )(shard, block_owner)
    pieces = pl.pallas_call(
        spread_kernel, out_shape=spread_shape, in_specs=[WHOLE], out_specs=WHOLE, name="spread"
    )(gradient)
    pieces = exchange(pieces, "g")
    routed = pl.pallas_call(
        route_kernel, out_shape=routed_shape, in_specs=[SMEM, WHOLE], out_specs=WHOLE, name="route"
    )(places, pieces)
    got = exchange(routed, ("g", "r")).reshape(OWNERS, SLOTS, ROWS_DEV, PIECE)

    stat_spec = pl.BlockSpec((1, BLOCK, BLOCK), lambda k: (k, 0, 0))
    stat_shape = jax.ShapeDtypeStruct((SLOTS, BLOCK, BLOCK), jnp.float32)
    new_left, new_right, raw, sums = pl.pallas_call(
        owner_kernel,
        grid=(SLOTS,),
        out_shape=[stat_shape, stat_shape, stat_shape, jax.ShapeDtypeStruct(sums_shape, jnp.float32)],
        in_specs=[
            SMEM,
            SMEM,
            pl.BlockSpec((OWNERS, 1, ROWS_DEV, PIECE), lambda k: (0, k, 0, 0)),
            stat_spec,
            stat_spec,
        ],
        out_specs=[stat_spec, stat_spec, stat_spec, pl.BlockSpec(sums_shape, lambda k: (0, 0, 0))],
        scratch_shapes=[pltpu.VMEM((BLOCK, BLOCK), jnp.bfloat16)],
        compiler_params=pltpu.CompilerParams(vmem_limit_bytes=48 * 1024 * 1024),
        cost_estimate=pl.CostEstimate(
            flops=50 * 2 * BLOCK**3, bytes_accessed=12 * 1024 * 1024, transcendentals=0
        ),
        name="owner",
    )(me, places, got, prev_left[0, 0], prev_right[0, 0])

    sums = jnp.sum(exchange(sums, ("g", "mp")), axis=0, keepdims=True)
    sums = exchange(jnp.broadcast_to(sums, (MEMBERS, 8, 128)), "r")
    sending = pl.pallas_call(
        scale_kernel, out_shape=routed_shape, in_specs=[WHOLE, WHOLE], out_specs=WHOLE, name="scale"
    )(sums, raw)
    returned = exchange(sending, ("g", "r"))
    back = pl.pallas_call(
        collect_kernel, out_shape=spread_shape, in_specs=[SMEM, WHOLE], out_specs=WHOLE, name="collect"
    )(places, returned)
    back = exchange(back, "g")
    update_out = pl.pallas_call(
        place_kernel,
        out_shape=jax.ShapeDtypeStruct(gradient.shape, jnp.bfloat16),
        in_specs=[WHOLE],
        out_specs=WHOLE,
        name="place",
    )(back)
    return (update_out, new_left[None, None], new_right[None, None])


def solution(mesh):
    fine = Mesh(mesh.devices.reshape(GROUPS, MEMBERS, SHARDS), ("g", "r", "mp"))
    grad_spec = P(("g", "r"), "mp")
    stat_spec = P("mp", ("g", "r"), None, None, None)
    return jax.shard_map(
        shards,
        mesh=fine,
        in_specs=(grad_spec, P(), stat_spec, stat_spec),
        out_specs=(grad_spec, stat_spec, stat_spec),
        check_vma=False,
    )
```

```python
import jax
import jax.numpy as jnp
from jax import lax
from jax.experimental import pallas as pl
from jax.experimental.pallas import tpu as pltpu
from jax.sharding import Mesh
from jax.sharding import PartitionSpec as P

EPS_DAMP = 1.0
BETA = 0.95
BLOCK = 512
SHARDS = 4
GROUPS = 4
MEMBERS = 16
PER_SHARD = 8
BLOCKS = GROUPS * PER_SHARD
OWNERS = 64
SLOTS = 2
LINES = 8
CELLS = 2048 * 16384
MIB = 1024 * 1024

WHOLE = pl.BlockSpec(memory_space=pltpu.VMEM)
SMEM = pl.BlockSpec(memory_space=pltpu.SMEM)


def params(mib):
    return pltpu.CompilerParams(vmem_limit_bytes=mib * MIB)


def place_table_kernel(shard_ref, owner_ref, place_ref, count_ref):
    base = shard_ref[0] * PER_SHARD

    def clear(o, _):
        count_ref[o] = 0
        return 0

    lax.fori_loop(0, OWNERS, clear, 0, unroll=8)
    for b in range(BLOCKS):
        owner = owner_ref[b // PER_SHARD, base + b % PER_SHARD]
        slot = count_ref[owner]
        count_ref[owner] = slot + 1
        place_ref[b] = (lax.rem(owner, MEMBERS) * GROUPS + owner // MEMBERS) * SLOTS + slot


def route_kernel(place_ref, in_ref, out_ref):
    for row in range(GROUPS):
        for j in range(PER_SHARD):
            place = place_ref[row * PER_SHARD + j]
            columns = pl.ds(pl.multiple_of(lax.rem(place, SLOTS) * BLOCK, BLOCK), BLOCK)
            out_ref[place // SLOTS, :, columns] = in_ref[row, :, pl.ds(j * BLOCK, BLOCK)]


def collect_kernel(place_ref, sums_ref, in_ref, out_ref):
    grad_total = sums_ref[0:1, 0:1]
    update_total = sums_ref[1:2, 0:1]
    graft = jnp.sqrt(grad_total / CELLS) * lax.rsqrt(update_total / CELLS + 1e-06)
    for row in range(GROUPS):
        for j in range(PER_SHARD):
            place = place_ref[row * PER_SHARD + j]
            slot = lax.rem(place, SLOTS)
            columns = pl.ds(pl.multiple_of(slot * BLOCK, BLOCK), BLOCK)
            coded = in_ref[place // SLOTS, :, columns].astype(jnp.int32).astype(jnp.float32)
            steps = jnp.exp2(
                in_ref[place // SLOTS, :, pl.ds(SLOTS * BLOCK, 128)].astype(jnp.int32).astype(jnp.float32)
            )
            step = jnp.where(slot == 0, steps[:, 0:1], steps[:, 64:65])
            out_ref[row, :, pl.ds(j * BLOCK, BLOCK)] = (coded * (step * graft)).astype(jnp.bfloat16)


def dot(a, b):
    return jnp.dot(a, b, preferred_element_type=jnp.float32)


def split(x):
    high = x.astype(jnp.bfloat16)
    return high, (x - high.astype(jnp.float32)).astype(jnp.bfloat16)


def dot3(a, b):
    return dot(a[0], b[0]) + (dot(a[0], b[1]) + dot(a[1], b[0]))


def root(stat, eye):
    damped = stat + EPS_DAMP * eye
    total = jnp.sum(damped * damped, keepdims=True)
    norm = jnp.sqrt(total)
    n = damped * (1.0 / norm)
    n_split = split(n)
    n2 = dot3(n_split, n_split)
    q = split(1.5625 * eye - 2.5 * n + n2)
    h = split(1.25 * n - n2)
    r = split(dot3(q, q))
    product = 1.5625 * eye - 1.25 * n - dot3(h, r)
    return product * lax.rsqrt(jnp.sqrt(0.25 * norm))


def owner_kernel(me_ref, place_ref, got_ref, left_ref, right_ref, new_left_ref, new_right_ref, coded_ref,
                 sums_ref, power_ref):
    slot = pl.program_id(0)
    wanted = me_ref[0] * SLOTS + slot
    used = place_ref[0] == wanted
    for b in range(1, BLOCKS):
        used = used | (place_ref[b] == wanted)
    block = got_ref[...]
    block = jnp.where(used, block, jnp.zeros_like(block))
    turned = block.T
    rows = lax.broadcasted_iota(jnp.int32, (BLOCK, BLOCK), 0)
    columns = lax.broadcasted_iota(jnp.int32, (BLOCK, BLOCK), 1)
    eye = jnp.where(rows == columns, 1.0, 0.0).astype(jnp.float32)
    left = BETA * left_ref[0] + dot(block, turned)
    new_left_ref[0] = left
    right = BETA * right_ref[0] + dot(turned, block)
    new_right_ref[0] = right
    left_root = split(root(left, eye))
    half = split(dot(left_root[0], block) + dot(left_root[1], block))
    raw = dot3(half, split(root(right, eye)))
    wide = block.astype(jnp.float32)
    grad_sq = jnp.sum(wide * wide, keepdims=True)
    update_sq = jnp.sum(raw * raw, keepdims=True)
    line = lax.broadcasted_iota(jnp.int32, sums_ref.shape, 0)
    sums = jnp.where(line == 0, grad_sq, update_sq)
    largest = jnp.max(jnp.abs(raw), axis=1, keepdims=True)
    power = jnp.ceil(jnp.log2(jnp.maximum(largest, 1e-30)) + 0.001) - 15.0
    coded = jnp.round(raw * jnp.exp2(-power)).astype(jnp.int32)
    place = pl.ds(pl.multiple_of(slot * BLOCK, BLOCK), BLOCK)
    for p in range(OWNERS):
        coded_ref[p, :, place] = coded[p * LINES : (p + 1) * LINES].astype(jnp.int16)

    @pl.when(slot == 0)
    def _():
        sums_ref[...] = sums
        power_ref[...] = jnp.broadcast_to(power, power_ref.shape)

    @pl.when(slot > 0)
    def _():
        sums_ref[...] += sums
        lane = lax.broadcasted_iota(jnp.int32, power_ref.shape, 1)
        powers = jnp.where(lane < 64, power_ref[...], power).astype(jnp.int32)
        for p in range(OWNERS):
            coded_ref[p, :, pl.ds(SLOTS * BLOCK, 128)] = powers[p * LINES : (p + 1) * LINES].astype(jnp.int16)


def exchange(x, axes):
    return lax.all_to_all(x, axes, split_axis=0, concat_axis=0, tiled=True)


def sum_everywhere(x):
    stages = [
        ("mp", [[(d, (d + s) % SHARDS) for d in range(SHARDS)] for s in (1, 2, 3)]),
        ("r", [[(d, d // 8 * 8 + (d + s) % 8) for d in range(MEMBERS)] for s in (2, 4, 6)]),
        ("r", [[(d, d ^ s) for d in range(MEMBERS)] for s in (1, 8, 9)]),
        ("g", [[(d, (d + s) % GROUPS) for d in range(GROUPS)] for s in (1, 2, 3)]),
    ]
    for axis, perms in stages:
        got = [lax.ppermute(x, axis, perm) for perm in perms]
        x = (x + got[0]) + (got[1] + got[2])
    return x


def shards(gradient, block_owner, prev_left, prev_right):
    shard = jnp.reshape(lax.axis_index("mp"), (1,)).astype(jnp.int32)
    me = jnp.reshape(lax.axis_index(("r", "g")), (1,)).astype(jnp.int32)
    spread_shape = (GROUPS, LINES, PER_SHARD * BLOCK)

    places = pl.pallas_call(
        place_table_kernel,
        out_shape=jax.ShapeDtypeStruct((BLOCKS,), jnp.int32),
        in_specs=[SMEM, SMEM],
        out_specs=SMEM,
        scratch_shapes=[pltpu.SMEM((OWNERS,), jnp.int32)],
        compiler_params=params(4),
        cost_estimate=pl.CostEstimate(flops=1000, bytes_accessed=1000, transcendentals=0),
        name="places",
    )(shard, block_owner)
    pieces = exchange(gradient.reshape(spread_shape), "g")
    routed = pl.pallas_call(
        route_kernel,
        out_shape=jax.ShapeDtypeStruct((OWNERS, LINES, SLOTS * BLOCK), jnp.bfloat16),
        in_specs=[SMEM, WHOLE],
        out_specs=WHOLE,
        compiler_params=params(4),
        name="route",
    )(places, pieces)
    got = exchange(routed, ("r", "g")).reshape(BLOCK, SLOTS * BLOCK)

    stat_spec = pl.BlockSpec((1, BLOCK, BLOCK), lambda k: (k, 0, 0))
    stat_shape = jax.ShapeDtypeStruct((SLOTS, BLOCK, BLOCK), jnp.float32)
    coded_shape = (OWNERS, LINES, SLOTS * BLOCK + 128)
    new_left, new_right, coded, sums = pl.pallas_call(
        owner_kernel,
        grid=(SLOTS,),
        out_shape=[
            stat_shape,
            stat_shape,
            jax.ShapeDtypeStruct(coded_shape, jnp.int16),
            jax.ShapeDtypeStruct((8, 128), jnp.float32),
        ],
        in_specs=[SMEM, SMEM, pl.BlockSpec((BLOCK, BLOCK), lambda k: (0, k)), stat_spec, stat_spec],
        out_specs=[
            stat_spec,
            stat_spec,
            pl.BlockSpec(coded_shape, lambda k: (0, 0, 0)),
            pl.BlockSpec((8, 128), lambda k: (0, 0)),
        ],
        scratch_shapes=[pltpu.VMEM((BLOCK, 128), jnp.float32)],
        compiler_params=params(40),
        cost_estimate=pl.CostEstimate(
            flops=50 * 2 * BLOCK**3, bytes_accessed=12 * MIB, transcendentals=0
        ),
        name="owner",
    )(me, places, got, prev_left[0, 0], prev_right[0, 0])

    returned = exchange(coded, ("r", "g"))
    sums = sum_everywhere(sums)
    back = pl.pallas_call(
        collect_kernel,
        out_shape=jax.ShapeDtypeStruct(spread_shape, jnp.bfloat16),
        in_specs=[SMEM, WHOLE, WHOLE],
        out_specs=WHOLE,
        compiler_params=params(8),
        name="collect",
    )(places, sums, returned)
    update_out = exchange(back, "g").reshape(gradient.shape)
    return (update_out, new_left[None, None], new_right[None, None])


def solution(mesh):
    fine = Mesh(mesh.devices.reshape(GROUPS, MEMBERS, SHARDS), ("g", "r", "mp"))
    grad_spec = P(("g", "r"), "mp")
    stat_spec = P("mp", ("g", "r"), None, None, None)
    return jax.shard_map(
        shards,
        mesh=fine,
        in_specs=(grad_spec, P(), stat_spec, stat_spec),
        out_specs=(grad_spec, stat_spec, stat_spec),
        check_vma=False,
    )
```

```python
import jax
import jax.numpy as jnp
from jax import lax
from jax.experimental import pallas as pl
from jax.experimental.pallas import tpu as pltpu
from jax.sharding import Mesh
from jax.sharding import PartitionSpec as P

EPS_DAMP = 1.0
BETA = 0.95
BLOCK = 512
SHARDS = 4
GROUPS = 4
MEMBERS = 16
PER_SHARD = 8
BLOCKS = GROUPS * PER_SHARD
OWNERS = 64
SLOTS = 2
LINES = 8
CELLS = 2048 * 16384
MIB = 1024 * 1024

WHOLE = pl.BlockSpec(memory_space=pltpu.VMEM)
SMEM = pl.BlockSpec(memory_space=pltpu.SMEM)


def params(mib):
    return pltpu.CompilerParams(vmem_limit_bytes=mib * MIB)


def place_table_kernel(shard_ref, owner_ref, place_ref, count_ref):
    base = shard_ref[0] * PER_SHARD

    def clear(o, _):
        count_ref[o] = 0
        return 0

    lax.fori_loop(0, OWNERS, clear, 0, unroll=8)
    for b in range(BLOCKS):
        owner = owner_ref[b // PER_SHARD, base + b % PER_SHARD]
        slot = count_ref[owner]
        count_ref[owner] = slot + 1
        place_ref[b] = (lax.rem(owner, MEMBERS) * GROUPS + owner // MEMBERS) * SLOTS + slot


def route_kernel(place_ref, in_ref, out_ref):
    for row in range(GROUPS):
        for j in range(PER_SHARD):
            place = place_ref[row * PER_SHARD + j]
            columns = pl.ds(pl.multiple_of(lax.rem(place, SLOTS) * BLOCK, BLOCK), BLOCK)
            out_ref[place // SLOTS, :, columns] = in_ref[row, :, pl.ds(j * BLOCK, BLOCK)]


def collect_kernel(place_ref, sums_ref, in_ref, out_ref):
    grad_total = sums_ref[0:1, 0:1]
    update_total = sums_ref[1:2, 0:1]
    graft = jnp.sqrt(grad_total / CELLS) * lax.rsqrt(update_total / CELLS + 1e-06)
    for row in range(GROUPS):
        for j in range(PER_SHARD):
            place = place_ref[row * PER_SHARD + j]
            slot = lax.rem(place, SLOTS)
            columns = pl.ds(pl.multiple_of(slot * BLOCK, BLOCK), BLOCK)
            coded = in_ref[place // SLOTS, :, columns].astype(jnp.int32).astype(jnp.float32)
            steps = jnp.exp2(
                in_ref[place // SLOTS, :, pl.ds(SLOTS * BLOCK, 128)].astype(jnp.int32).astype(jnp.float32)
            )
            step = jnp.where(slot == 0, steps[:, 0:1], steps[:, 64:65])
            out_ref[row, :, pl.ds(j * BLOCK, BLOCK)] = (coded * (step * graft)).astype(jnp.bfloat16)


def dot(a, b):
    return jnp.dot(a, b, preferred_element_type=jnp.float32)


def split(x):
    high = x.astype(jnp.bfloat16)
    return high, (x - high.astype(jnp.float32)).astype(jnp.bfloat16)


def dot3(a, b):
    return dot(
        jnp.concatenate([a[0], a[0], a[1]], axis=1), jnp.concatenate([b[0], b[1], b[0]], axis=0)
    )


def roots(stats, eye):
    damped = [stat + EPS_DAMP * eye for stat in stats]
    norms = [jnp.sqrt(jnp.sum(a * a, keepdims=True)) for a in damped]
    ns = [a * (1.0 / norm) for a, norm in zip(damped, norms)]
    n_splits = [split(n) for n in ns]
    n2s = [dot3(n, n) for n in n_splits]
    qs = [split(1.5625 * eye - 2.5 * n + n2) for n, n2 in zip(ns, n2s)]
    hs = [split(1.25 * n - n2) for n, n2 in zip(ns, n2s)]
    rs = [split(dot3(q, q)) for q in qs]
    products = [1.5625 * eye - 1.25 * n - dot3(h, r) for n, h, r in zip(ns, hs, rs)]
    return [p * lax.rsqrt(jnp.sqrt(0.25 * norm)) for p, norm in zip(products, norms)]


def owner_kernel(me_ref, place_ref, got_ref, left_ref, right_ref, new_left_ref, new_right_ref, coded_ref,
                 sums_ref, power_ref):
    slot = pl.program_id(0)
    wanted = me_ref[0] * SLOTS + slot
    used = place_ref[0] == wanted
    for b in range(1, BLOCKS):
        used = used | (place_ref[b] == wanted)
    block = got_ref[...]
    block = jnp.where(used, block, jnp.zeros_like(block))
    turned = block.T
    rows = lax.broadcasted_iota(jnp.int32, (BLOCK, BLOCK), 0)
    columns = lax.broadcasted_iota(jnp.int32, (BLOCK, BLOCK), 1)
    eye = jnp.where(rows == columns, 1.0, 0.0).astype(jnp.float32)
    left = BETA * left_ref[0] + dot(block, turned)
    new_left_ref[0] = left
    right = BETA * right_ref[0] + dot(turned, block)
    new_right_ref[0] = right
    left_root, right_root = (split(p) for p in roots((left, right), eye))
    half = split(dot(left_root[0], block) + dot(left_root[1], block))
    raw = dot3(half, right_root)
    wide = block.astype(jnp.float32)
    grad_sq = jnp.sum(wide * wide, keepdims=True)
    update_sq = jnp.sum(raw * raw, keepdims=True)
    line = lax.broadcasted_iota(jnp.int32, sums_ref.shape, 0)
    sums = jnp.where(line == 0, grad_sq, update_sq)
    largest = jnp.max(jnp.abs(raw), axis=1, keepdims=True)
    power = jnp.ceil(jnp.log2(jnp.maximum(largest, 1e-30)) + 0.001) - 15.0
    coded = jnp.round(raw * jnp.exp2(-power)).astype(jnp.int32)
    place = pl.ds(pl.multiple_of(slot * BLOCK, BLOCK), BLOCK)
    for p in range(OWNERS):
        coded_ref[p, :, place] = coded[p * LINES : (p + 1) * LINES].astype(jnp.int16)

    @pl.when(slot == 0)
    def _():
        sums_ref[...] = sums
        power_ref[...] = jnp.broadcast_to(power, power_ref.shape)

    @pl.when(slot > 0)
    def _():
        sums_ref[...] += sums
        lane = lax.broadcasted_iota(jnp.int32, power_ref.shape, 1)
        powers = jnp.where(lane < 64, power_ref[...], power).astype(jnp.int32)
        for p in range(OWNERS):
            coded_ref[p, :, pl.ds(SLOTS * BLOCK, 128)] = powers[p * LINES : (p + 1) * LINES].astype(jnp.int16)


def exchange(x, axes):
    return lax.all_to_all(x, axes, split_axis=0, concat_axis=0, tiled=True)


def add_permuted(x, axis, perms):
    return sum([lax.ppermute(x, axis, perm) for perm in perms], x)


def sum_everywhere(x):
    x = add_permuted(x, "mp", [[(d, (d + s) % SHARDS) for d in range(SHARDS)] for s in range(1, 4)])
    x = add_permuted(x, "r", [[(d, d ^ s) for d in range(MEMBERS)] for s in range(1, 8)])
    x = add_permuted(x, ("g", "r"), [[(d, d ^ (8 * s)) for d in range(OWNERS)] for s in range(1, 8)])
    return x


def shards(gradient, block_owner, prev_left, prev_right):
    shard = jnp.reshape(lax.axis_index("mp"), (1,)).astype(jnp.int32)
    me = jnp.reshape(lax.axis_index(("r", "g")), (1,)).astype(jnp.int32)
    spread_shape = (GROUPS, LINES, PER_SHARD * BLOCK)

    places = pl.pallas_call(
        place_table_kernel,
        out_shape=jax.ShapeDtypeStruct((BLOCKS,), jnp.int32),
        in_specs=[SMEM, SMEM],
        out_specs=SMEM,
        scratch_shapes=[pltpu.SMEM((OWNERS,), jnp.int32)],
        compiler_params=params(4),
        cost_estimate=pl.CostEstimate(flops=1000, bytes_accessed=1000, transcendentals=0),
        name="places",
    )(shard, block_owner)
    pieces = exchange(gradient.reshape(spread_shape), "g")
    routed = pl.pallas_call(
        route_kernel,
        out_shape=jax.ShapeDtypeStruct((OWNERS, LINES, SLOTS * BLOCK), jnp.bfloat16),
        in_specs=[SMEM, WHOLE],
        out_specs=WHOLE,
        compiler_params=params(4),
        name="route",
    )(places, pieces)
    got = exchange(routed, ("r", "g")).reshape(BLOCK, SLOTS * BLOCK)

    stat_spec = pl.BlockSpec((1, BLOCK, BLOCK), lambda k: (k, 0, 0))
    stat_shape = jax.ShapeDtypeStruct((SLOTS, BLOCK, BLOCK), jnp.float32)
    coded_shape = (OWNERS, LINES, SLOTS * BLOCK + 128)
    new_left, new_right, coded, sums = pl.pallas_call(
        owner_kernel,
        grid=(SLOTS,),
        out_shape=[
            stat_shape,
            stat_shape,
            jax.ShapeDtypeStruct(coded_shape, jnp.int16),
            jax.ShapeDtypeStruct((8, 128), jnp.float32),
        ],
        in_specs=[SMEM, SMEM, pl.BlockSpec((BLOCK, BLOCK), lambda k: (0, k)), stat_spec, stat_spec],
        out_specs=[
            stat_spec,
            stat_spec,
            pl.BlockSpec(coded_shape, lambda k: (0, 0, 0)),
            pl.BlockSpec((8, 128), lambda k: (0, 0)),
        ],
        scratch_shapes=[pltpu.VMEM((BLOCK, 128), jnp.float32)],
        compiler_params=params(58),
        cost_estimate=pl.CostEstimate(
            flops=50 * 2 * BLOCK**3, bytes_accessed=12 * MIB, transcendentals=0
        ),
        name="owner",
    )(me, places, got, prev_left[0, 0], prev_right[0, 0])

    returned = exchange(coded, ("r", "g"))
    sums = sum_everywhere(sums)
    back = pl.pallas_call(
        collect_kernel,
        out_shape=jax.ShapeDtypeStruct(spread_shape, jnp.bfloat16),
        in_specs=[SMEM, WHOLE, WHOLE],
        out_specs=WHOLE,
        compiler_params=params(8),
        name="collect",
    )(places, sums, returned)
    update_out = exchange(back, "g").reshape(gradient.shape)
    return (update_out, new_left[None, None], new_right[None, None])


def solution(mesh):
    fine = Mesh(mesh.devices.reshape(GROUPS, MEMBERS, SHARDS), ("g", "r", "mp"))
    grad_spec = P(("g", "r"), "mp")
    stat_spec = P("mp", ("g", "r"), None, None, None)
    return jax.shard_map(
        shards,
        mesh=fine,
        in_specs=(grad_spec, P(), stat_spec, stat_spec),
        out_specs=(grad_spec, stat_spec, stat_spec),
        check_vma=False,
    )
```

```python
import jax
import jax.numpy as jnp
from jax import lax
from jax.experimental import pallas as pl
from jax.experimental.pallas import tpu as pltpu
from jax.sharding import Mesh
from jax.sharding import PartitionSpec as P

EPS_DAMP = 1.0
BETA = 0.95
BLOCK = 512
SHARDS = 4
GROUPS = 4
MEMBERS = 16
PER_SHARD = 8
BLOCKS = GROUPS * PER_SHARD
OWNERS = 64
SLOTS = 2
LINES = 8
CELLS = 2048 * 16384
MIB = 1024 * 1024

WHOLE = pl.BlockSpec(memory_space=pltpu.VMEM)
SMEM = pl.BlockSpec(memory_space=pltpu.SMEM)


def params(mib):
    return pltpu.CompilerParams(vmem_limit_bytes=mib * MIB)


def place_table_kernel(shard_ref, owner_ref, place_ref, count_ref):
    base = shard_ref[0] * PER_SHARD

    def clear(o, _):
        count_ref[o] = 0
        return 0

    lax.fori_loop(0, OWNERS, clear, 0, unroll=8)
    for b in range(BLOCKS):
        owner = owner_ref[b // PER_SHARD, base + b % PER_SHARD]
        slot = count_ref[owner]
        count_ref[owner] = slot + 1
        place_ref[b] = (lax.rem(owner, MEMBERS) * GROUPS + owner // MEMBERS) * SLOTS + slot


def route_kernel(place_ref, in_ref, out_ref):
    for row in range(GROUPS):
        for j in range(PER_SHARD):
            place = place_ref[row * PER_SHARD + j]
            columns = pl.ds(pl.multiple_of(lax.rem(place, SLOTS) * BLOCK, BLOCK), BLOCK)
            out_ref[place // SLOTS, :, columns] = in_ref[row, :, pl.ds(j * BLOCK, BLOCK)]


def collect_kernel(place_ref, sums_ref, in_ref, out_ref):
    grad_total = sums_ref[0:1, 0:1]
    update_total = sums_ref[1:2, 0:1]
    graft = jnp.sqrt(grad_total / CELLS) * lax.rsqrt(update_total / CELLS + 1e-06)
    for row in range(GROUPS):
        for j in range(PER_SHARD):
            place = place_ref[row * PER_SHARD + j]
            slot = lax.rem(place, SLOTS)
            columns = pl.ds(pl.multiple_of(slot * BLOCK, BLOCK), BLOCK)
            coded = in_ref[place // SLOTS, :, columns].astype(jnp.int32).astype(jnp.float32)
            steps = jnp.exp2(
                in_ref[place // SLOTS, :, pl.ds(SLOTS * BLOCK, 128)].astype(jnp.int32).astype(jnp.float32)
            )
            step = jnp.where(slot == 0, steps[:, 0:1], steps[:, 64:65])
            out_ref[row, :, pl.ds(j * BLOCK, BLOCK)] = (coded * (step * graft)).astype(jnp.bfloat16)


def dot(a, b):
    return jnp.dot(a, b, preferred_element_type=jnp.float32)


def split(x):
    high = x.astype(jnp.bfloat16)
    return high, (x - high.astype(jnp.float32)).astype(jnp.bfloat16)


def dot3(a, b, columns):
    return dot(
        jnp.concatenate([a[0][...], a[0][...], a[1][...]], axis=1),
        jnp.concatenate([b[0][:, columns], b[1][:, columns], b[0][:, columns]], axis=0),
    )


def put(pair, columns, x):
    pair[0][:, columns], pair[1][:, columns] = split(x)


def owner_kernel(me_ref, place_ref, got_ref, left_ref, right_ref, new_left_ref, new_right_ref, coded_ref,
                 sums_ref, power_ref, prev_ref, new_ref, n_ref, raw_ref, n_parts_ref, q_parts_ref,
                 h_parts_ref, r_parts_ref, got_sem, new_sem):
    slot = pl.program_id(0)

    def fetch(side, k):
        source = (left_ref, right_ref)[side]
        return pltpu.make_async_copy(source.at[k], prev_ref.at[side, k], got_sem.at[side, k])

    def write(side, k):
        target = (new_left_ref, new_right_ref)[side]
        return pltpu.make_async_copy(new_ref.at[side, k], target.at[k], new_sem.at[side, k])

    @pl.when(slot == 0)
    def _():
        for k in range(SLOTS):
            for side in range(2):
                fetch(side, k).start()

    wanted = me_ref[0] * SLOTS + slot
    used = place_ref[0] == wanted
    for b in range(1, BLOCKS):
        used = used | (place_ref[b] == wanted)
    block = got_ref[...]
    block = jnp.where(used, block, jnp.zeros_like(block))
    turned = block.T
    halves = [pl.ds(0, BLOCK // 2), pl.ds(BLOCK // 2, BLOCK // 2)]
    steps = [(columns, side) for columns in halves for side in range(2)]

    def eye(columns, value):
        rows = lax.broadcasted_iota(jnp.int32, (BLOCK, columns.size), 0)
        lanes = lax.broadcasted_iota(jnp.int32, (BLOCK, columns.size), 1) + columns.start
        return jnp.where(rows == lanes, jnp.float32(value), jnp.float32(0))

    def pair(ref, side):
        return ref.at[side, 0], ref.at[side, 1]

    norms = []
    for side in range(2):
        gram = dot(block, turned) if side == 0 else dot(turned, block)
        fetch(side, slot).wait()
        stat = BETA * prev_ref[side, slot] + gram
        new_ref[side, slot] = stat
        write(side, slot).start()
        damped = stat + eye(pl.ds(0, BLOCK), EPS_DAMP)
        norm = jnp.sqrt(jnp.sum(damped * damped, keepdims=True))
        n = damped * (1.0 / norm)
        n_ref[side] = n
        put(pair(n_parts_ref, side), slice(None), n)
        norms.append(norm)
    for columns, side in steps:
        n = n_ref[side, :, columns]
        n_parts = pair(n_parts_ref, side)
        n2 = dot3(n_parts, n_parts, columns)
        put(pair(q_parts_ref, side), columns, eye(columns, 1.5625) - 2.5 * n + n2)
        put(pair(h_parts_ref, side), columns, 1.25 * n - n2)
    for columns, side in steps:
        q_parts = pair(q_parts_ref, side)
        put(pair(r_parts_ref, side), columns, dot3(q_parts, q_parts, columns))
    for columns, side in steps:
        product = dot3(pair(h_parts_ref, side), pair(r_parts_ref, side), columns)
        product = eye(columns, 1.5625) - 1.25 * n_ref[side, :, columns] - product
        put(pair(n_parts_ref, side), columns, product * lax.rsqrt(jnp.sqrt(0.25 * norms[side])))
    left_root = jnp.concatenate([n_parts_ref[0, 0], n_parts_ref[0, 1]], axis=1)
    for columns in halves:
        part = block[:, columns.start : columns.start + columns.size]
        put(pair(q_parts_ref, 0), columns, dot(left_root, jnp.concatenate([part, part], axis=0)))
    update_sq = jnp.zeros((1, 1), jnp.float32)
    for columns in halves:
        raw = dot3(pair(q_parts_ref, 0), pair(n_parts_ref, 1), columns)
        raw_ref[:, columns] = raw
        update_sq += jnp.sum(raw * raw, keepdims=True)
    wide = block.astype(jnp.float32)
    grad_sq = jnp.sum(wide * wide, keepdims=True)
    line = lax.broadcasted_iota(jnp.int32, sums_ref.shape, 0)
    sums = jnp.where(line == 0, grad_sq, update_sq)
    raw = raw_ref[...]
    largest = jnp.max(jnp.abs(raw), axis=1, keepdims=True)
    power = jnp.ceil(jnp.log2(jnp.maximum(largest, 1e-30)) + 0.001) - 15.0
    coded = jnp.round(raw * jnp.exp2(-power)).astype(jnp.int32)
    place = pl.ds(pl.multiple_of(slot * BLOCK, BLOCK), BLOCK)
    for p in range(OWNERS):
        coded_ref[p, :, place] = coded[p * LINES : (p + 1) * LINES].astype(jnp.int16)

    @pl.when(slot == 0)
    def _():
        sums_ref[...] = sums
        power_ref[...] = jnp.broadcast_to(power, power_ref.shape)

    @pl.when(slot == SLOTS - 1)
    def _():
        sums_ref[...] += sums
        lane = lax.broadcasted_iota(jnp.int32, power_ref.shape, 1)
        powers = jnp.where(lane < 64, power_ref[...], power).astype(jnp.int32)
        for p in range(OWNERS):
            coded_ref[p, :, pl.ds(SLOTS * BLOCK, 128)] = powers[p * LINES : (p + 1) * LINES].astype(jnp.int16)
        for k in range(SLOTS):
            for side in range(2):
                write(side, k).wait()


def exchange(x, axes):
    return lax.all_to_all(x, axes, split_axis=0, concat_axis=0, tiled=True)


def add_permuted(x, axis, perms):
    return sum([lax.ppermute(x, axis, perm) for perm in perms], x)


def sum_everywhere(x):
    x = add_permuted(x, "mp", [[(d, (d + s) % SHARDS) for d in range(SHARDS)] for s in range(1, 4)])
    x = add_permuted(x, "r", [[(d, d ^ s) for d in range(MEMBERS)] for s in range(1, 8)])
    x = add_permuted(x, ("g", "r"), [[(d, d ^ (8 * s)) for d in range(OWNERS)] for s in range(1, 4)])
    x = add_permuted(x, "g", [[(d, d ^ 2) for d in range(GROUPS)]])
    return x


def shards(gradient, block_owner, prev_left, prev_right):
    shard = jnp.reshape(lax.axis_index("mp"), (1,)).astype(jnp.int32)
    me = jnp.reshape(lax.axis_index(("r", "g")), (1,)).astype(jnp.int32)
    spread_shape = (GROUPS, LINES, PER_SHARD * BLOCK)

    places = pl.pallas_call(
        place_table_kernel,
        out_shape=jax.ShapeDtypeStruct((BLOCKS,), jnp.int32),
        in_specs=[SMEM, SMEM],
        out_specs=SMEM,
        scratch_shapes=[pltpu.SMEM((OWNERS,), jnp.int32)],
        compiler_params=params(4),
        cost_estimate=pl.CostEstimate(flops=1000, bytes_accessed=1000, transcendentals=0),
        name="places",
    )(shard, block_owner)
    pieces = exchange(gradient.reshape(spread_shape), "g")
    routed = pl.pallas_call(
        route_kernel,
        out_shape=jax.ShapeDtypeStruct((OWNERS, LINES, SLOTS * BLOCK), jnp.bfloat16),
        in_specs=[SMEM, WHOLE],
        out_specs=WHOLE,
        compiler_params=params(4),
        name="route",
    )(places, pieces)
    got = exchange(routed, ("r", "g")).reshape(BLOCK, SLOTS * BLOCK)

    stat_spec = pl.BlockSpec(memory_space=pl.ANY)
    parts = pltpu.VMEM((2, 2, BLOCK, BLOCK), jnp.bfloat16)
    stat_shape = jax.ShapeDtypeStruct((SLOTS, BLOCK, BLOCK), jnp.float32)
    coded_shape = (OWNERS, LINES, SLOTS * BLOCK + 128)
    new_left, new_right, coded, sums = pl.pallas_call(
        owner_kernel,
        grid=(SLOTS,),
        out_shape=[
            stat_shape,
            stat_shape,
            jax.ShapeDtypeStruct(coded_shape, jnp.int16),
            jax.ShapeDtypeStruct((8, 128), jnp.float32),
        ],
        in_specs=[SMEM, SMEM, pl.BlockSpec((BLOCK, BLOCK), lambda k: (0, k)), stat_spec, stat_spec],
        out_specs=[
            stat_spec,
            stat_spec,
            pl.BlockSpec(coded_shape, lambda k: (0, 0, 0)),
            pl.BlockSpec((8, 128), lambda k: (0, 0)),
        ],
        scratch_shapes=[
            pltpu.VMEM((BLOCK, 128), jnp.float32),
            pltpu.VMEM((2, SLOTS, BLOCK, BLOCK), jnp.float32),
            pltpu.VMEM((2, SLOTS, BLOCK, BLOCK), jnp.float32),
            pltpu.VMEM((2, BLOCK, BLOCK), jnp.float32),
            pltpu.VMEM((BLOCK, BLOCK), jnp.float32),
            parts,
            parts,
            parts,
            parts,
            pltpu.SemaphoreType.DMA((2, SLOTS)),
            pltpu.SemaphoreType.DMA((2, SLOTS)),
        ],
        compiler_params=params(48),
        cost_estimate=pl.CostEstimate(
            flops=50 * 2 * BLOCK**3, bytes_accessed=12 * MIB, transcendentals=0
        ),
        name="owner",
    )(me, places, got, prev_left[0, 0], prev_right[0, 0])

    returned = exchange(coded, ("r", "g"))
    sums = sum_everywhere(sums)
    back = pl.pallas_call(
        collect_kernel,
        out_shape=jax.ShapeDtypeStruct(spread_shape, jnp.bfloat16),
        in_specs=[SMEM, WHOLE, WHOLE],
        out_specs=WHOLE,
        compiler_params=params(8),
        name="collect",
    )(places, sums, returned)
    update_out = exchange(back, "g").reshape(gradient.shape)
    return (update_out, new_left[None, None], new_right[None, None])


def solution(mesh):
    fine = Mesh(mesh.devices.reshape(GROUPS, MEMBERS, SHARDS), ("g", "r", "mp"))
    grad_spec = P(("g", "r"), "mp")
    stat_spec = P("mp", ("g", "r"), None, None, None)
    return jax.shard_map(
        shards,
        mesh=fine,
        in_specs=(grad_spec, P(), stat_spec, stat_spec),
        out_specs=(grad_spec, stat_spec, stat_spec),
        check_vma=False,
    )
```

```python
import jax
import jax.numpy as jnp
from jax import lax
from jax.experimental import pallas as pl
from jax.experimental.pallas import tpu as pltpu
from jax.sharding import Mesh
from jax.sharding import PartitionSpec as P

EPS_DAMP = 1.0
BETA = 0.95
BLOCK = 512
SHARDS = 4
GROUPS = 4
MEMBERS = 16
PER_SHARD = 8
BLOCKS = GROUPS * PER_SHARD
OWNERS = 64
SLOTS = 2
LINES = 8
CELLS = 2048 * 16384
MIB = 1024 * 1024

WHOLE = pl.BlockSpec(memory_space=pltpu.VMEM)
SMEM = pl.BlockSpec(memory_space=pltpu.SMEM)


def params(mib):
    return pltpu.CompilerParams(vmem_limit_bytes=mib * MIB)


def place_table_kernel(shard_ref, owner_ref, place_ref, count_ref):
    base = shard_ref[0] * PER_SHARD

    def clear(o, _):
        count_ref[o] = 0
        return 0

    lax.fori_loop(0, OWNERS, clear, 0, unroll=8)
    for b in range(BLOCKS):
        owner = owner_ref[b // PER_SHARD, base + b % PER_SHARD]
        slot = count_ref[owner]
        count_ref[owner] = slot + 1
        place_ref[b] = (lax.rem(owner, MEMBERS) * GROUPS + owner // MEMBERS) * SLOTS + slot


def route_kernel(place_ref, in_ref, out_ref):
    for row in range(GROUPS):
        for j in range(PER_SHARD):
            place = place_ref[row * PER_SHARD + j]
            columns = pl.ds(pl.multiple_of(lax.rem(place, SLOTS) * BLOCK, BLOCK), BLOCK)
            out_ref[place // SLOTS, :, columns] = in_ref[row, :, pl.ds(j * BLOCK, BLOCK)]


def collect_kernel(place_ref, sums_ref, in_ref, out_ref):
    grad_total = sums_ref[0:1, 0:1]
    update_total = sums_ref[1:2, 0:1]
    graft = jnp.sqrt(grad_total / CELLS) * lax.rsqrt(update_total / CELLS + 1e-06)
    for row in range(GROUPS):
        for j in range(PER_SHARD):
            place = place_ref[row * PER_SHARD + j]
            slot = lax.rem(place, SLOTS)
            columns = pl.ds(pl.multiple_of(slot * BLOCK, BLOCK), BLOCK)
            coded = in_ref[place // SLOTS, :, columns].astype(jnp.int32).astype(jnp.float32)
            steps = jnp.exp2(
                in_ref[place // SLOTS, :, pl.ds(SLOTS * BLOCK, 128)].astype(jnp.int32).astype(jnp.float32)
            )
            step = jnp.where(slot == 0, steps[:, 0:1], steps[:, 64:65])
            out_ref[row, :, pl.ds(j * BLOCK, BLOCK)] = (coded * (step * graft)).astype(jnp.bfloat16)


def dot(a, b):
    return jnp.dot(a, b, preferred_element_type=jnp.float32)


def split(x):
    high = x.astype(jnp.bfloat16)
    return high, (x - high.astype(jnp.float32)).astype(jnp.bfloat16)


HALF = BLOCK // 2
ALL = slice(0, BLOCK)
LOW = slice(0, HALF)
HIGH = slice(HALF, BLOCK)


def dot3(a, b, rows, columns):
    return dot(
        jnp.concatenate([a[0][rows], a[0][rows], a[1][rows]], axis=1),
        jnp.concatenate([b[0][:, columns], b[1][:, columns], b[0][:, columns]], axis=0),
    )


def put(pair, rows, columns, x):
    pair[0][rows, columns], pair[1][rows, columns] = split(x)


def mirror(pair):
    for part in pair:
        part[LOW, HIGH] = part[HIGH, LOW].T


def owner_kernel(me_ref, place_ref, got_ref, left_ref, right_ref, new_left_ref, new_right_ref, coded_ref,
                 sums_ref, power_ref, prev_ref, new_ref, n_ref, raw_ref, n_parts_ref, q_parts_ref,
                 h_parts_ref, r_parts_ref, got_sem, new_sem):
    slot = pl.program_id(0)

    def fetch(side, k):
        source = (left_ref, right_ref)[side]
        return pltpu.make_async_copy(source.at[k], prev_ref.at[side, k], got_sem.at[side, k])

    def write(side, k):
        target = (new_left_ref, new_right_ref)[side]
        return pltpu.make_async_copy(new_ref.at[side, k], target.at[k], new_sem.at[side, k])

    @pl.when(slot == 0)
    def _():
        for k in range(SLOTS):
            for side in range(2):
                fetch(side, k).start()

    wanted = me_ref[0] * SLOTS + slot
    used = place_ref[0] == wanted
    for b in range(1, BLOCKS):
        used = used | (place_ref[b] == wanted)
    block = got_ref[...]
    block = jnp.where(used, block, jnp.zeros_like(block))
    turned = block.T
    steps = [(rows, columns, side) for rows, columns in ((ALL, LOW), (HIGH, HIGH)) for side in range(2)]

    def eye(rows, columns, value):
        shape = (rows.stop - rows.start, columns.stop - columns.start)
        down = lax.broadcasted_iota(jnp.int32, shape, 0) + rows.start
        across = lax.broadcasted_iota(jnp.int32, shape, 1) + columns.start
        return jnp.where(down == across, jnp.float32(value), jnp.float32(0))

    def pair(ref, side):
        return ref.at[side, 0], ref.at[side, 1]

    norms = []
    for side in range(2):
        gram = dot(block, turned) if side == 0 else dot(turned, block)
        fetch(side, slot).wait()
        stat = BETA * prev_ref[side, slot] + gram
        new_ref[side, slot] = stat
        write(side, slot).start()
        damped = stat + eye(ALL, ALL, EPS_DAMP)
        norm = jnp.sqrt(jnp.sum(damped * damped, keepdims=True))
        n = damped * (1.0 / norm)
        n_ref[side] = n
        put(pair(n_parts_ref, side), ALL, ALL, n)
        norms.append(norm)
    for rows, columns, side in steps:
        n = n_ref[side, rows, columns]
        n_parts = pair(n_parts_ref, side)
        n2 = dot3(n_parts, n_parts, rows, columns)
        put(pair(q_parts_ref, side), rows, columns, eye(rows, columns, 1.5625) - 2.5 * n + n2)
        put(pair(h_parts_ref, side), rows, columns, 1.25 * n - n2)
        if columns == LOW:
            mirror(pair(q_parts_ref, side))
            mirror(pair(h_parts_ref, side))
    for rows, columns, side in steps:
        q_parts = pair(q_parts_ref, side)
        put(pair(r_parts_ref, side), rows, columns, dot3(q_parts, q_parts, rows, columns))
        if columns == LOW:
            mirror(pair(r_parts_ref, side))
    for rows, columns, side in steps:
        product = dot3(pair(h_parts_ref, side), pair(r_parts_ref, side), rows, columns)
        product = eye(rows, columns, 1.5625) - 1.25 * n_ref[side, rows, columns] - product
        product = product * lax.rsqrt(jnp.sqrt(0.25 * norms[side]))
        put(pair(n_parts_ref, side), rows, columns, product)
        if columns == LOW:
            mirror(pair(n_parts_ref, side))
    left_root = jnp.concatenate([n_parts_ref[0, 0], n_parts_ref[0, 1]], axis=1)
    for columns in (LOW, HIGH):
        part = block[:, columns]
        put(pair(q_parts_ref, 0), ALL, columns, dot(left_root, jnp.concatenate([part, part], axis=0)))
    update_sq = jnp.zeros((1, 1), jnp.float32)
    for columns in (LOW, HIGH):
        raw = dot3(pair(q_parts_ref, 0), pair(n_parts_ref, 1), ALL, columns)
        raw_ref[:, columns] = raw
        update_sq += jnp.sum(raw * raw, keepdims=True)
    wide = block.astype(jnp.float32)
    grad_sq = jnp.sum(wide * wide, keepdims=True)
    line = lax.broadcasted_iota(jnp.int32, sums_ref.shape, 0)
    sums = jnp.where(line == 0, grad_sq, update_sq)
    raw = raw_ref[...]
    largest = jnp.max(jnp.abs(raw), axis=1, keepdims=True)
    power = jnp.ceil(jnp.log2(jnp.maximum(largest, 1e-30)) + 0.001) - 15.0
    coded = jnp.round(raw * jnp.exp2(-power)).astype(jnp.int32)
    place = pl.ds(pl.multiple_of(slot * BLOCK, BLOCK), BLOCK)
    for p in range(OWNERS):
        coded_ref[p, :, place] = coded[p * LINES : (p + 1) * LINES].astype(jnp.int16)

    @pl.when(slot == 0)
    def _():
        sums_ref[...] = sums
        power_ref[...] = jnp.broadcast_to(power, power_ref.shape)

    @pl.when(slot == SLOTS - 1)
    def _():
        sums_ref[...] += sums
        lane = lax.broadcasted_iota(jnp.int32, power_ref.shape, 1)
        powers = jnp.where(lane < 64, power_ref[...], power).astype(jnp.int32)
        for p in range(OWNERS):
            coded_ref[p, :, pl.ds(SLOTS * BLOCK, 128)] = powers[p * LINES : (p + 1) * LINES].astype(jnp.int16)
        for k in range(SLOTS):
            for side in range(2):
                write(side, k).wait()


def exchange(x, axes):
    return lax.all_to_all(x, axes, split_axis=0, concat_axis=0, tiled=True)


def add_permuted(x, axis, perms):
    return sum([lax.ppermute(x, axis, perm) for perm in perms], x)


def sum_everywhere(x):
    ends = [[(d, (d ^ t) // 4 * 4 + (d + s) % 4) for d in range(16)] for t in (0, 8) for s in range(4)]
    x = add_permuted(x, ("g", "mp"), ends[1:])
    x = add_permuted(x, "r", [[(d, d ^ s) for d in range(MEMBERS)] for s in range(1, 8)])
    x = add_permuted(x, ("g", "r"), [[(d, d ^ (8 * s)) for d in range(OWNERS)] for s in range(1, 4)])
    return x


def shards(gradient, block_owner, prev_left, prev_right):
    shard = jnp.reshape(lax.axis_index("mp"), (1,)).astype(jnp.int32)
    me = jnp.reshape(lax.axis_index(("r", "g")), (1,)).astype(jnp.int32)
    spread_shape = (GROUPS, LINES, PER_SHARD * BLOCK)

    places = pl.pallas_call(
        place_table_kernel,
        out_shape=jax.ShapeDtypeStruct((BLOCKS,), jnp.int32),
        in_specs=[SMEM, SMEM],
        out_specs=SMEM,
        scratch_shapes=[pltpu.SMEM((OWNERS,), jnp.int32)],
        compiler_params=params(4),
        cost_estimate=pl.CostEstimate(flops=1000, bytes_accessed=1000, transcendentals=0),
        name="places",
    )(shard, block_owner)
    pieces = exchange(gradient.reshape(spread_shape), "g")
    routed = pl.pallas_call(
        route_kernel,
        out_shape=jax.ShapeDtypeStruct((OWNERS, LINES, SLOTS * BLOCK), jnp.bfloat16),
        in_specs=[SMEM, WHOLE],
        out_specs=WHOLE,
        compiler_params=params(4),
        name="route",
    )(places, pieces)
    got = exchange(routed, ("r", "g")).reshape(BLOCK, SLOTS * BLOCK)

    stat_spec = pl.BlockSpec(memory_space=pl.ANY)
    parts = pltpu.VMEM((2, 2, BLOCK, BLOCK), jnp.bfloat16)
    stat_shape = jax.ShapeDtypeStruct((SLOTS, BLOCK, BLOCK), jnp.float32)
    coded_shape = (OWNERS, LINES, SLOTS * BLOCK + 128)
    new_left, new_right, coded, sums = pl.pallas_call(
        owner_kernel,
        grid=(SLOTS,),
        out_shape=[
            stat_shape,
            stat_shape,
            jax.ShapeDtypeStruct(coded_shape, jnp.int16),
            jax.ShapeDtypeStruct((8, 128), jnp.float32),
        ],
        in_specs=[SMEM, SMEM, pl.BlockSpec((BLOCK, BLOCK), lambda k: (0, k)), stat_spec, stat_spec],
        out_specs=[
            stat_spec,
            stat_spec,
            pl.BlockSpec(coded_shape, lambda k: (0, 0, 0)),
            pl.BlockSpec((8, 128), lambda k: (0, 0)),
        ],
        scratch_shapes=[
            pltpu.VMEM((BLOCK, 128), jnp.float32),
            pltpu.VMEM((2, SLOTS, BLOCK, BLOCK), jnp.float32),
            pltpu.VMEM((2, SLOTS, BLOCK, BLOCK), jnp.float32),
            pltpu.VMEM((2, BLOCK, BLOCK), jnp.float32),
            pltpu.VMEM((BLOCK, BLOCK), jnp.float32),
            parts,
            parts,
            parts,
            parts,
            pltpu.SemaphoreType.DMA((2, SLOTS)),
            pltpu.SemaphoreType.DMA((2, SLOTS)),
        ],
        compiler_params=params(48),
        cost_estimate=pl.CostEstimate(
            flops=50 * 2 * BLOCK**3, bytes_accessed=12 * MIB, transcendentals=0
        ),
        name="owner",
    )(me, places, got, prev_left[0, 0], prev_right[0, 0])

    returned = exchange(coded, ("r", "g"))
    sums = sum_everywhere(sums)
    back = pl.pallas_call(
        collect_kernel,
        out_shape=jax.ShapeDtypeStruct(spread_shape, jnp.bfloat16),
        in_specs=[SMEM, WHOLE, WHOLE],
        out_specs=WHOLE,
        compiler_params=params(8),
        name="collect",
    )(places, sums, returned)
    update_out = exchange(back, "g").reshape(gradient.shape)
    return (update_out, new_left[None, None], new_right[None, None])


def solution(mesh):
    fine = Mesh(mesh.devices.reshape(GROUPS, MEMBERS, SHARDS), ("g", "r", "mp"))
    grad_spec = P(("g", "r"), "mp")
    stat_spec = P("mp", ("g", "r"), None, None, None)
    return jax.shard_map(
        shards,
        mesh=fine,
        in_specs=(grad_spec, P(), stat_spec, stat_spec),
        out_specs=(grad_spec, stat_spec, stat_spec),
        check_vma=False,
    )
```

```python
import jax
import jax.numpy as jnp
from jax import lax
from jax.experimental import pallas as pl
from jax.experimental.pallas import tpu as pltpu
from jax.sharding import Mesh
from jax.sharding import PartitionSpec as P

EPS_DAMP = 1.0
BETA = 0.95
BLOCK = 512
SHARDS = 4
GROUPS = 4
MEMBERS = 16
PER_SHARD = 8
BLOCKS = GROUPS * PER_SHARD
OWNERS = 64
SLOTS = 2
LINES = 8
CELLS = 2048 * 16384
MIB = 1024 * 1024

WHOLE = pl.BlockSpec(memory_space=pltpu.VMEM)
SMEM = pl.BlockSpec(memory_space=pltpu.SMEM)


def params(mib):
    return pltpu.CompilerParams(vmem_limit_bytes=mib * MIB)


def place_table_kernel(shard_ref, owner_ref, place_ref, count_ref):
    base = shard_ref[0] * PER_SHARD

    def clear(o, _):
        count_ref[o] = 0
        return 0

    lax.fori_loop(0, OWNERS, clear, 0, unroll=8)
    for b in range(BLOCKS):
        owner = owner_ref[b // PER_SHARD, base + b % PER_SHARD]
        slot = count_ref[owner]
        count_ref[owner] = slot + 1
        place_ref[b] = (lax.rem(owner, MEMBERS) * GROUPS + owner // MEMBERS) * SLOTS + slot


def route_kernel(place_ref, in_ref, out_ref):
    for row in range(GROUPS):
        for j in range(PER_SHARD):
            place = place_ref[row * PER_SHARD + j]
            columns = pl.ds(pl.multiple_of(lax.rem(place, SLOTS) * BLOCK, BLOCK), BLOCK)
            out_ref[place // SLOTS, :, columns] = in_ref[row, :, pl.ds(j * BLOCK, BLOCK)]


def collect_kernel(place_ref, in_ref, out_ref):
    lane = lax.broadcasted_iota(jnp.int32, (LINES, 128), 1)
    for row in range(GROUPS):
        powers = jnp.zeros((LINES, 128), jnp.int32)
        for j in range(PER_SHARD):
            place = place_ref[row * PER_SHARD + j]
            position, slot = place // SLOTS, lax.rem(place, SLOTS)
            columns = pl.ds(pl.multiple_of(slot * BLOCK, BLOCK), BLOCK)
            out_ref[row, :, pl.ds(j * BLOCK, BLOCK)] = in_ref[position, :, columns]
            both = in_ref[position, :, pl.ds(SLOTS * BLOCK, 128)].astype(jnp.int32)
            powers = jnp.where(lane == j, jnp.where(slot == 0, both[:, 0:1], both[:, 64:65]), powers)
        out_ref[row, :, pl.ds(PER_SHARD * BLOCK, 128)] = powers.astype(jnp.int16)


def finish_kernel(sums_ref, in_ref, out_ref):
    grad_total = sums_ref[0:1, 0:1]
    update_total = sums_ref[1:2, 0:1]
    graft = jnp.sqrt(grad_total / CELLS) * lax.rsqrt(update_total / CELLS + 1e-06)
    for chunk in range(GROUPS):
        powers = in_ref[chunk, :, pl.ds(PER_SHARD * BLOCK, 128)].astype(jnp.int32).astype(jnp.float32)
        steps = jnp.exp2(powers) * graft
        for j in range(PER_SHARD):
            columns = pl.ds(j * BLOCK, BLOCK)
            coded = in_ref[chunk, :, columns].astype(jnp.int32).astype(jnp.float32)
            out_ref[chunk, :, columns] = (coded * steps[:, j : j + 1]).astype(jnp.bfloat16)


def dot(a, b):
    return jnp.dot(a, b, preferred_element_type=jnp.float32)


def split(x):
    high = x.astype(jnp.bfloat16)
    return high, (x - high.astype(jnp.float32)).astype(jnp.bfloat16)


HALF = BLOCK // 2
ALL = slice(0, BLOCK)
LOW = slice(0, HALF)
HIGH = slice(HALF, BLOCK)


def dot3(a, b, rows, columns):
    return dot(
        jnp.concatenate([a[0][rows], a[0][rows], a[1][rows]], axis=1),
        jnp.concatenate([b[0][:, columns], b[1][:, columns], b[0][:, columns]], axis=0),
    )


def put(pair, rows, columns, x):
    pair[0][rows, columns], pair[1][rows, columns] = split(x)


def mirror(pair):
    for part in pair:
        part[LOW, HIGH] = part[HIGH, LOW].T


def owner_kernel(me_ref, place_ref, got_ref, left_ref, right_ref, new_left_ref, new_right_ref, coded_ref,
                 sums_ref, power_ref, prev_ref, new_ref, n_ref, raw_ref, n_parts_ref, q_parts_ref,
                 h_parts_ref, r_parts_ref, got_sem, new_sem):
    slot = pl.program_id(0)

    def fetch(side, k):
        source = (left_ref, right_ref)[side]
        return pltpu.make_async_copy(source.at[k], prev_ref.at[side, k], got_sem.at[side, k])

    def write(side, k):
        target = (new_left_ref, new_right_ref)[side]
        return pltpu.make_async_copy(new_ref.at[side, k], target.at[k], new_sem.at[side, k])

    @pl.when(slot == 0)
    def _():
        for k in range(SLOTS):
            for side in range(2):
                fetch(side, k).start()

    wanted = me_ref[0] * SLOTS + slot
    used = place_ref[0] == wanted
    for b in range(1, BLOCKS):
        used = used | (place_ref[b] == wanted)
    block = got_ref[...]
    block = jnp.where(used, block, jnp.zeros_like(block))
    turned = block.T
    steps = [(rows, columns, side) for rows, columns in ((ALL, LOW), (HIGH, HIGH)) for side in range(2)]

    def eye(rows, columns, value):
        shape = (rows.stop - rows.start, columns.stop - columns.start)
        down = lax.broadcasted_iota(jnp.int32, shape, 0) + rows.start
        across = lax.broadcasted_iota(jnp.int32, shape, 1) + columns.start
        return jnp.where(down == across, jnp.float32(value), jnp.float32(0))

    def pair(ref, side):
        return ref.at[side, 0], ref.at[side, 1]

    norms = []
    for side in range(2):
        gram = dot(block, turned) if side == 0 else dot(turned, block)
        fetch(side, slot).wait()
        stat = BETA * prev_ref[side, slot] + gram
        new_ref[side, slot] = stat
        write(side, slot).start()
        damped = stat + eye(ALL, ALL, EPS_DAMP)
        norm = jnp.sqrt(jnp.sum(damped * damped, keepdims=True))
        n = damped * (1.0 / norm)
        n_ref[side] = n
        put(pair(n_parts_ref, side), ALL, ALL, n)
        norms.append(norm)
    for rows, columns, side in steps:
        n = n_ref[side, rows, columns]
        n_parts = pair(n_parts_ref, side)
        n2 = dot3(n_parts, n_parts, rows, columns)
        put(pair(q_parts_ref, side), rows, columns, eye(rows, columns, 1.5625) - 2.5 * n + n2)
        put(pair(h_parts_ref, side), rows, columns, 1.25 * n - n2)
        if columns == LOW:
            mirror(pair(q_parts_ref, side))
            mirror(pair(h_parts_ref, side))
    for rows, columns, side in steps:
        q_parts = pair(q_parts_ref, side)
        put(pair(r_parts_ref, side), rows, columns, dot3(q_parts, q_parts, rows, columns))
        if columns == LOW:
            mirror(pair(r_parts_ref, side))
    for rows, columns, side in steps:
        product = dot3(pair(h_parts_ref, side), pair(r_parts_ref, side), rows, columns)
        product = eye(rows, columns, 1.5625) - 1.25 * n_ref[side, rows, columns] - product
        product = product * lax.rsqrt(jnp.sqrt(0.25 * norms[side]))
        put(pair(n_parts_ref, side), rows, columns, product)
        if columns == LOW:
            mirror(pair(n_parts_ref, side))
    left_root = jnp.concatenate([n_parts_ref[0, 0], n_parts_ref[0, 1]], axis=1)
    for columns in (LOW, HIGH):
        part = block[:, columns]
        put(pair(q_parts_ref, 0), ALL, columns, dot(left_root, jnp.concatenate([part, part], axis=0)))
    update_sq = jnp.zeros((1, 1), jnp.float32)
    for columns in (LOW, HIGH):
        raw = dot3(pair(q_parts_ref, 0), pair(n_parts_ref, 1), ALL, columns)
        raw_ref[:, columns] = raw
        update_sq += jnp.sum(raw * raw, keepdims=True)
    wide = block.astype(jnp.float32)
    grad_sq = jnp.sum(wide * wide, keepdims=True)
    line = lax.broadcasted_iota(jnp.int32, sums_ref.shape, 0)
    sums = jnp.where(line == 0, grad_sq, update_sq)
    raw = raw_ref[...]
    largest = jnp.max(jnp.abs(raw), axis=1, keepdims=True)
    power = jnp.ceil(jnp.log2(jnp.maximum(largest, 1e-30)) + 0.001) - 15.0
    coded = jnp.round(raw * jnp.exp2(-power)).astype(jnp.int32)
    place = pl.ds(pl.multiple_of(slot * BLOCK, BLOCK), BLOCK)
    for p in range(OWNERS):
        coded_ref[p, :, place] = coded[p * LINES : (p + 1) * LINES].astype(jnp.int16)

    @pl.when(slot == 0)
    def _():
        sums_ref[...] = sums
        power_ref[...] = jnp.broadcast_to(power, power_ref.shape)

    @pl.when(slot == SLOTS - 1)
    def _():
        sums_ref[...] += sums
        lane = lax.broadcasted_iota(jnp.int32, power_ref.shape, 1)
        powers = jnp.where(lane < 64, power_ref[...], power).astype(jnp.int32)
        for p in range(OWNERS):
            coded_ref[p, :, pl.ds(SLOTS * BLOCK, 128)] = powers[p * LINES : (p + 1) * LINES].astype(jnp.int16)
        for k in range(SLOTS):
            for side in range(2):
                write(side, k).wait()


def exchange(x, axes):
    return lax.all_to_all(x, axes, split_axis=0, concat_axis=0, tiled=True)


def add_permuted(x, axis, perms):
    return sum([lax.ppermute(x, axis, perm) for perm in perms], x)


def sum_near(x):
    x = add_permuted(x, "mp", [[(d, (d + s) % SHARDS) for d in range(SHARDS)] for s in range(1, 4)])
    x = add_permuted(x, "r", [[(d, d ^ s) for d in range(MEMBERS)] for s in range(1, 8)])
    return add_permuted(x, ("g", "r"), [[(d, d ^ (8 * s)) for d in range(OWNERS)] for s in range(1, 4)])


def sum_far(x):
    return add_permuted(x, "g", [[(d, d ^ 2) for d in range(GROUPS)]])


def shards(gradient, block_owner, prev_left, prev_right):
    shard = jnp.reshape(lax.axis_index("mp"), (1,)).astype(jnp.int32)
    me = jnp.reshape(lax.axis_index(("r", "g")), (1,)).astype(jnp.int32)
    spread_shape = (GROUPS, LINES, PER_SHARD * BLOCK)

    places = pl.pallas_call(
        place_table_kernel,
        out_shape=jax.ShapeDtypeStruct((BLOCKS,), jnp.int32),
        in_specs=[SMEM, SMEM],
        out_specs=SMEM,
        scratch_shapes=[pltpu.SMEM((OWNERS,), jnp.int32)],
        compiler_params=params(4),
        cost_estimate=pl.CostEstimate(flops=1000, bytes_accessed=1000, transcendentals=0),
        name="places",
    )(shard, block_owner)
    pieces = exchange(gradient.reshape(spread_shape), "g")
    routed = pl.pallas_call(
        route_kernel,
        out_shape=jax.ShapeDtypeStruct((OWNERS, LINES, SLOTS * BLOCK), jnp.bfloat16),
        in_specs=[SMEM, WHOLE],
        out_specs=WHOLE,
        compiler_params=params(4),
        name="route",
    )(places, pieces)
    got = exchange(routed, ("r", "g")).reshape(BLOCK, SLOTS * BLOCK)

    stat_spec = pl.BlockSpec(memory_space=pl.ANY)
    parts = pltpu.VMEM((2, 2, BLOCK, BLOCK), jnp.bfloat16)
    stat_shape = jax.ShapeDtypeStruct((SLOTS, BLOCK, BLOCK), jnp.float32)
    coded_shape = (OWNERS, LINES, SLOTS * BLOCK + 128)
    new_left, new_right, coded, sums = pl.pallas_call(
        owner_kernel,
        grid=(SLOTS,),
        out_shape=[
            stat_shape,
            stat_shape,
            jax.ShapeDtypeStruct(coded_shape, jnp.int16),
            jax.ShapeDtypeStruct((8, 128), jnp.float32),
        ],
        in_specs=[SMEM, SMEM, pl.BlockSpec((BLOCK, BLOCK), lambda k: (0, k)), stat_spec, stat_spec],
        out_specs=[
            stat_spec,
            stat_spec,
            pl.BlockSpec(coded_shape, lambda k: (0, 0, 0)),
            pl.BlockSpec((8, 128), lambda k: (0, 0)),
        ],
        scratch_shapes=[
            pltpu.VMEM((BLOCK, 128), jnp.float32),
            pltpu.VMEM((2, SLOTS, BLOCK, BLOCK), jnp.float32),
            pltpu.VMEM((2, SLOTS, BLOCK, BLOCK), jnp.float32),
            pltpu.VMEM((2, BLOCK, BLOCK), jnp.float32),
            pltpu.VMEM((BLOCK, BLOCK), jnp.float32),
            parts,
            parts,
            parts,
            parts,
            pltpu.SemaphoreType.DMA((2, SLOTS)),
            pltpu.SemaphoreType.DMA((2, SLOTS)),
        ],
        compiler_params=params(48),
        cost_estimate=pl.CostEstimate(
            flops=50 * 2 * BLOCK**3, bytes_accessed=12 * MIB, transcendentals=0
        ),
        name="owner",
    )(me, places, got, prev_left[0, 0], prev_right[0, 0])

    returned = exchange(coded, ("r", "g"))
    sums = sum_near(sums)
    back = pl.pallas_call(
        collect_kernel,
        out_shape=jax.ShapeDtypeStruct((GROUPS, LINES, PER_SHARD * BLOCK + 128), jnp.int16),
        in_specs=[SMEM, WHOLE],
        out_specs=WHOLE,
        compiler_params=params(8),
        name="collect",
    )(places, returned)
    sums, back = lax.optimization_barrier((sums, back))
    back = exchange(back, "g")
    update_out = pl.pallas_call(
        finish_kernel,
        out_shape=jax.ShapeDtypeStruct(spread_shape, jnp.bfloat16),
        in_specs=[WHOLE, WHOLE],
        out_specs=WHOLE,
        compiler_params=params(8),
        name="finish",
    )(sum_far(sums), back).reshape(gradient.shape)
    return (update_out, new_left[None, None], new_right[None, None])


def solution(mesh):
    fine = Mesh(mesh.devices.reshape(GROUPS, MEMBERS, SHARDS), ("g", "r", "mp"))
    grad_spec = P(("g", "r"), "mp")
    stat_spec = P("mp", ("g", "r"), None, None, None)
    return jax.shard_map(
        shards,
        mesh=fine,
        in_specs=(grad_spec, P(), stat_spec, stat_spec),
        out_specs=(grad_spec, stat_spec, stat_spec),
        check_vma=False,
    )
```

```python
import jax
import jax.numpy as jnp
from jax import lax
from jax.experimental import pallas as pl
from jax.experimental.pallas import tpu as pltpu
from jax.sharding import Mesh
from jax.sharding import PartitionSpec as P

EPS_DAMP = 1.0
BETA = 0.95
BLOCK = 512
SHARDS = 4
GROUPS = 4
MEMBERS = 16
PER_SHARD = 8
BLOCKS = GROUPS * PER_SHARD
OWNERS = 64
SLOTS = 2
LINES = 8
CELLS = 2048 * 16384
MIB = 1024 * 1024

WHOLE = pl.BlockSpec(memory_space=pltpu.VMEM)
SMEM = pl.BlockSpec(memory_space=pltpu.SMEM)


def params(mib):
    return pltpu.CompilerParams(vmem_limit_bytes=mib * MIB)


def place_table_kernel(shard_ref, owner_ref, place_ref, count_ref):
    base = shard_ref[0] * PER_SHARD

    def clear(o, _):
        count_ref[o] = 0
        return 0

    lax.fori_loop(0, OWNERS, clear, 0, unroll=8)
    for b in range(BLOCKS):
        owner = owner_ref[b // PER_SHARD, base + b % PER_SHARD]
        slot = count_ref[owner]
        count_ref[owner] = slot + 1
        place_ref[b] = (lax.rem(owner, MEMBERS) * GROUPS + owner // MEMBERS) * SLOTS + slot


def route_kernel(group_ref, place_ref, in_ref, out_ref):
    for row in range(GROUPS):
        for j in range(PER_SHARD):
            place = place_ref[row * PER_SHARD + j]
            position = place // SLOTS

            @pl.when(lax.rem(position, GROUPS) == group_ref[0])
            def _():
                columns = pl.ds(pl.multiple_of(lax.rem(place, SLOTS) * BLOCK, BLOCK), BLOCK)
                out_ref[position // GROUPS, :, columns] = in_ref[row, :, pl.ds(j * BLOCK, BLOCK)]


def collect_kernel(place_ref, in_ref, out_ref):
    lane = lax.broadcasted_iota(jnp.int32, (LINES, 128), 1)
    for row in range(GROUPS):
        powers = jnp.zeros((LINES, 128), jnp.int32)
        for j in range(PER_SHARD):
            place = place_ref[row * PER_SHARD + j]
            position, slot = place // SLOTS, lax.rem(place, SLOTS)
            columns = pl.ds(pl.multiple_of(slot * BLOCK, BLOCK), BLOCK)
            out_ref[row, :, pl.ds(j * BLOCK, BLOCK)] = in_ref[position, :, columns]
            both = in_ref[position, :, pl.ds(SLOTS * BLOCK, 128)].astype(jnp.int32)
            powers = jnp.where(lane == j + 64 * slot, both, powers)
        out_ref[row, :, pl.ds(PER_SHARD * BLOCK, 128)] = powers.astype(jnp.int16)


def finish_kernel(sums_ref, in_ref, out_ref):
    grad_total = sums_ref[0:1, 0:1]
    update_total = sums_ref[1:2, 0:1]
    graft = jnp.sqrt(grad_total / CELLS) * lax.rsqrt(update_total / CELLS + 1e-06)
    for chunk in range(GROUPS):
        powers = in_ref[chunk, :, pl.ds(PER_SHARD * BLOCK, 128)].astype(jnp.int32).astype(jnp.float32)
        steps = jnp.exp2(powers + pltpu.roll(powers, 64, 1)) * graft
        for j in range(PER_SHARD):
            columns = pl.ds(j * BLOCK, BLOCK)
            coded = in_ref[chunk, :, columns].astype(jnp.int32).astype(jnp.float32)
            out_ref[chunk, :, columns] = (coded * steps[:, j : j + 1]).astype(jnp.bfloat16)


def dot(a, b):
    return jnp.dot(a, b, preferred_element_type=jnp.float32)


def split(x):
    high = x.astype(jnp.bfloat16)
    return high, (x - high.astype(jnp.float32)).astype(jnp.bfloat16)


HALF = BLOCK // 2
ALL = slice(0, BLOCK)
LOW = slice(0, HALF)
HIGH = slice(HALF, BLOCK)


def dot3(a, b, rows, columns):
    return dot(
        jnp.concatenate([a[0][rows], a[0][rows], a[1][rows]], axis=1),
        jnp.concatenate([b[0][:, columns], b[1][:, columns], b[0][:, columns]], axis=0),
    )


def put(pair, rows, columns, x):
    pair[0][rows, columns], pair[1][rows, columns] = split(x)


def mirror(pair):
    for part in pair:
        part[LOW, HIGH] = part[HIGH, LOW].T


def owner_kernel(me_ref, place_ref, got_ref, left_ref, right_ref, new_left_ref, new_right_ref, coded_ref,
                 sums_ref, power_ref, prev_ref, new_ref, n_ref, raw_ref, n_parts_ref, q_parts_ref,
                 h_parts_ref, r_parts_ref, got_sem, new_sem):
    slot = pl.program_id(0)

    def fetch(side, k):
        source = (left_ref, right_ref)[side]
        return pltpu.make_async_copy(source.at[k], prev_ref.at[side, k], got_sem.at[side, k])

    def write(side, k):
        target = (new_left_ref, new_right_ref)[side]
        return pltpu.make_async_copy(new_ref.at[side, k], target.at[k], new_sem.at[side, k])

    @pl.when(slot == 0)
    def _():
        for k in range(SLOTS):
            for side in range(2):
                fetch(side, k).start()

    wanted = me_ref[0] * SLOTS + slot
    used = place_ref[0] == wanted
    for b in range(1, BLOCKS):
        used = used | (place_ref[b] == wanted)
    block = got_ref[...]
    block = jnp.where(used, block, jnp.zeros_like(block))
    turned = block.T
    steps = [(rows, columns, side) for rows, columns in ((ALL, LOW), (HIGH, HIGH)) for side in range(2)]

    def eye(rows, columns, value):
        shape = (rows.stop - rows.start, columns.stop - columns.start)
        down = lax.broadcasted_iota(jnp.int32, shape, 0) + rows.start
        across = lax.broadcasted_iota(jnp.int32, shape, 1) + columns.start
        return jnp.where(down == across, jnp.float32(value), jnp.float32(0))

    def pair(ref, side):
        return ref.at[side, 0], ref.at[side, 1]

    norms = []
    for side in range(2):
        gram = dot(block, turned) if side == 0 else dot(turned, block)
        fetch(side, slot).wait()
        stat = BETA * prev_ref[side, slot] + gram
        new_ref[side, slot] = stat
        write(side, slot).start()
        damped = stat + eye(ALL, ALL, EPS_DAMP)
        norm = jnp.sqrt(jnp.sum(damped * damped, keepdims=True))
        n = damped * (1.0 / norm)
        n_ref[side] = n
        put(pair(n_parts_ref, side), ALL, ALL, n)
        norms.append(norm)
    for rows, columns, side in steps:
        n = n_ref[side, rows, columns]
        n_parts = pair(n_parts_ref, side)
        n2 = dot3(n_parts, n_parts, rows, columns)
        put(pair(q_parts_ref, side), rows, columns, eye(rows, columns, 1.5625) - 2.5 * n + n2)
        put(pair(h_parts_ref, side), rows, columns, 1.25 * n - n2)
        if columns == LOW:
            mirror(pair(q_parts_ref, side))
            mirror(pair(h_parts_ref, side))
    for rows, columns, side in steps:
        q_parts = pair(q_parts_ref, side)
        put(pair(r_parts_ref, side), rows, columns, dot3(q_parts, q_parts, rows, columns))
        if columns == LOW:
            mirror(pair(r_parts_ref, side))
    for rows, columns, side in steps:
        product = dot3(pair(h_parts_ref, side), pair(r_parts_ref, side), rows, columns)
        product = eye(rows, columns, 1.5625) - 1.25 * n_ref[side, rows, columns] - product
        product = product * lax.rsqrt(jnp.sqrt(0.25 * norms[side]))
        put(pair(n_parts_ref, side), rows, columns, product)
        if columns == LOW:
            mirror(pair(n_parts_ref, side))
    left_root = jnp.concatenate([n_parts_ref[0, 0], n_parts_ref[0, 1]], axis=1)
    for columns in (LOW, HIGH):
        part = block[:, columns]
        put(pair(q_parts_ref, 0), ALL, columns, dot(left_root, jnp.concatenate([part, part], axis=0)))
    update_sq = jnp.zeros((1, 1), jnp.float32)
    for columns in (LOW, HIGH):
        raw = dot3(pair(q_parts_ref, 0), pair(n_parts_ref, 1), ALL, columns)
        raw_ref[:, columns] = raw
        update_sq += jnp.sum(raw * raw, keepdims=True)
    wide = block.astype(jnp.float32)
    grad_sq = jnp.sum(wide * wide, keepdims=True)
    line = lax.broadcasted_iota(jnp.int32, sums_ref.shape, 0)
    sums = jnp.where(line == 0, grad_sq, update_sq)
    raw = raw_ref[...]
    largest = jnp.max(jnp.abs(raw), axis=1, keepdims=True)
    power = jnp.ceil(jnp.log2(jnp.maximum(largest, 1e-30)) + 0.001) - 15.0
    coded = jnp.round(raw * jnp.exp2(-power)).astype(jnp.int32)
    place = pl.ds(pl.multiple_of(slot * BLOCK, BLOCK), BLOCK)
    for p in range(OWNERS):
        coded_ref[p, :, place] = coded[p * LINES : (p + 1) * LINES].astype(jnp.int16)

    @pl.when(slot == 0)
    def _():
        sums_ref[...] = sums
        power_ref[...] = jnp.broadcast_to(power, power_ref.shape)

    @pl.when(slot == SLOTS - 1)
    def _():
        sums_ref[...] += sums
        lane = lax.broadcasted_iota(jnp.int32, power_ref.shape, 1)
        powers = jnp.where(lane < 64, power_ref[...], power).astype(jnp.int32)
        for p in range(OWNERS):
            coded_ref[p, :, pl.ds(SLOTS * BLOCK, 128)] = powers[p * LINES : (p + 1) * LINES].astype(jnp.int16)
        for k in range(SLOTS):
            for side in range(2):
                write(side, k).wait()


def exchange(x, axes):
    return lax.all_to_all(x, axes, split_axis=0, concat_axis=0, tiled=True)


def add_permuted(x, axis, perms):
    return sum([lax.ppermute(x, axis, perm) for perm in perms], x)


def sum_dp(x):
    x = add_permuted(x, "r", [[(d, d ^ s) for d in range(MEMBERS)] for s in range(1, 8)])
    x = add_permuted(x, ("g", "r"), [[(d, d ^ (8 * s)) for d in range(OWNERS)] for s in range(1, 4)])
    return add_permuted(x, "g", [[(d, d ^ 2) for d in range(GROUPS)]])


def sum_mp(x):
    return add_permuted(x, "mp", [[(d, (d + s) % SHARDS) for d in range(SHARDS)] for s in range(1, 4)])


def shards(gradient, block_owner, prev_left, prev_right):
    shard = jnp.reshape(lax.axis_index("mp"), (1,)).astype(jnp.int32)
    me = jnp.reshape(lax.axis_index(("r", "g")), (1,)).astype(jnp.int32)
    spread_shape = (GROUPS, LINES, PER_SHARD * BLOCK)

    places = pl.pallas_call(
        place_table_kernel,
        out_shape=jax.ShapeDtypeStruct((BLOCKS,), jnp.int32),
        in_specs=[SMEM, SMEM],
        out_specs=SMEM,
        scratch_shapes=[pltpu.SMEM((OWNERS,), jnp.int32)],
        compiler_params=params(4),
        cost_estimate=pl.CostEstimate(flops=1000, bytes_accessed=1000, transcendentals=0),
        name="places",
    )(shard, block_owner)
    group = jnp.reshape(lax.axis_index("g"), (1,)).astype(jnp.int32)
    rows = lax.all_gather(gradient, "g", axis=0)
    routed = pl.pallas_call(
        route_kernel,
        out_shape=jax.ShapeDtypeStruct((MEMBERS, BLOCK // MEMBERS, SLOTS * BLOCK), jnp.bfloat16),
        in_specs=[SMEM, SMEM, WHOLE],
        out_specs=WHOLE,
        compiler_params=params(8),
        name="route",
    )(group, places, rows)
    got = exchange(routed, "r").reshape(BLOCK, SLOTS * BLOCK)

    stat_spec = pl.BlockSpec(memory_space=pl.ANY)
    parts = pltpu.VMEM((2, 2, BLOCK, BLOCK), jnp.bfloat16)
    stat_shape = jax.ShapeDtypeStruct((SLOTS, BLOCK, BLOCK), jnp.float32)
    coded_shape = (OWNERS, LINES, SLOTS * BLOCK + 128)
    new_left, new_right, coded, sums = pl.pallas_call(
        owner_kernel,
        grid=(SLOTS,),
        out_shape=[
            stat_shape,
            stat_shape,
            jax.ShapeDtypeStruct(coded_shape, jnp.int16),
            jax.ShapeDtypeStruct((8, 128), jnp.float32),
        ],
        in_specs=[SMEM, SMEM, pl.BlockSpec((BLOCK, BLOCK), lambda k: (0, k)), stat_spec, stat_spec],
        out_specs=[
            stat_spec,
            stat_spec,
            pl.BlockSpec(coded_shape, lambda k: (0, 0, 0)),
            pl.BlockSpec((8, 128), lambda k: (0, 0)),
        ],
        scratch_shapes=[
            pltpu.VMEM((BLOCK, 128), jnp.float32),
            pltpu.VMEM((2, SLOTS, BLOCK, BLOCK), jnp.float32),
            pltpu.VMEM((2, SLOTS, BLOCK, BLOCK), jnp.float32),
            pltpu.VMEM((2, BLOCK, BLOCK), jnp.float32),
            pltpu.VMEM((BLOCK, BLOCK), jnp.float32),
            parts,
            parts,
            parts,
            parts,
            pltpu.SemaphoreType.DMA((2, SLOTS)),
            pltpu.SemaphoreType.DMA((2, SLOTS)),
        ],
        compiler_params=params(48),
        cost_estimate=pl.CostEstimate(
            flops=50 * 2 * BLOCK**3, bytes_accessed=12 * MIB, transcendentals=0
        ),
        name="owner",
    )(me, places, got, prev_left[0, 0], prev_right[0, 0])

    returned = exchange(coded, ("r", "g"))
    sums = sum_dp(sums)
    back = pl.pallas_call(
        collect_kernel,
        out_shape=jax.ShapeDtypeStruct((GROUPS, LINES, PER_SHARD * BLOCK + 128), jnp.int16),
        in_specs=[SMEM, WHOLE],
        out_specs=WHOLE,
        compiler_params=params(8),
        name="collect",
    )(places, returned)
    sums, back = lax.optimization_barrier((sums, back))
    back = exchange(back, "g")
    update_out = pl.pallas_call(
        finish_kernel,
        out_shape=jax.ShapeDtypeStruct(spread_shape, jnp.bfloat16),
        in_specs=[WHOLE, WHOLE],
        out_specs=WHOLE,
        compiler_params=params(8),
        name="finish",
    )(sum_mp(sums), back).reshape(gradient.shape)
    return (update_out, new_left[None, None], new_right[None, None])


def solution(mesh):
    fine = Mesh(mesh.devices.reshape(GROUPS, MEMBERS, SHARDS), ("g", "r", "mp"))
    grad_spec = P(("g", "r"), "mp")
    stat_spec = P("mp", ("g", "r"), None, None, None)
    return jax.shard_map(
        shards,
        mesh=fine,
        in_specs=(grad_spec, P(), stat_spec, stat_spec),
        out_specs=(grad_spec, stat_spec, stat_spec),
        check_vma=False,
    )
```

```python
import jax
import jax.numpy as jnp
from jax import lax
from jax.experimental import pallas as pl
from jax.experimental.pallas import tpu as pltpu
from jax.sharding import Mesh
from jax.sharding import PartitionSpec as P

EPS_DAMP = 1.0
BETA = 0.95
BLOCK = 512
SHARDS = 4
GROUPS = 4
MEMBERS = 16
PER_SHARD = 8
BLOCKS = GROUPS * PER_SHARD
OWNERS = 64
SLOTS = 2
LINES = 8
CELLS = 2048 * 16384
MIB = 1024 * 1024
SUM_ROWS = 8

WHOLE = pl.BlockSpec(memory_space=pltpu.VMEM)
SMEM = pl.BlockSpec(memory_space=pltpu.SMEM)


def params(mib):
    return pltpu.CompilerParams(vmem_limit_bytes=mib * MIB)


def place_table_kernel(shard_ref, owner_ref, place_ref, count_ref):
    base = shard_ref[0] * PER_SHARD

    def clear(o, _):
        count_ref[o] = 0
        return 0

    lax.fori_loop(0, OWNERS, clear, 0, unroll=8)
    for b in range(BLOCKS):
        owner = owner_ref[b // PER_SHARD, base + b % PER_SHARD]
        slot = count_ref[owner]
        count_ref[owner] = slot + 1
        place_ref[b] = (lax.rem(owner, MEMBERS) * GROUPS + owner // MEMBERS) * SLOTS + slot


def route_kernel(place_ref, in_ref, out_ref):
    for row in range(GROUPS):
        for j in range(PER_SHARD):
            place = place_ref[row * PER_SHARD + j]
            columns = pl.ds(pl.multiple_of(lax.rem(place, SLOTS) * BLOCK, BLOCK), BLOCK)
            out_ref[place // SLOTS, :, columns] = in_ref[row, :, pl.ds(j * BLOCK, BLOCK)]


def collect_kernel(place_ref, in_ref, out_ref):
    for row in range(GROUPS):
        for j in range(PER_SHARD):
            place = place_ref[row * PER_SHARD + j]
            columns = pl.ds(pl.multiple_of(lax.rem(place, SLOTS) * BLOCK, BLOCK), BLOCK)
            out_ref[row, :, pl.ds(j * BLOCK, BLOCK)] = in_ref[place // SLOTS, :, columns]


def finish_kernel(me_ref, place_ref, gathered_ref, in_ref, out_ref):
    grad_total = gathered_ref[0:1, 0:1]
    update_total = gathered_ref[1:2, 0:1]
    graft = jnp.sqrt(grad_total / CELLS) * lax.rsqrt(update_total / CELLS + 1e-06)
    member, group = me_ref[0] // GROUPS, lax.rem(me_ref[0], GROUPS)
    scales = gathered_ref[pl.ds(SUM_ROWS + member * GROUPS, GROUPS), :] * graft
    lane = lax.broadcasted_iota(jnp.int32, scales.shape, 1)
    for j in range(PER_SHARD):
        place = place_ref[group * PER_SHARD + j]
        steps = jnp.sum(jnp.where(lane == place, scales, 0.0), axis=1, keepdims=True)
        columns = pl.ds(j * BLOCK, BLOCK)
        for chunk in range(GROUPS):
            coded = in_ref[chunk, :, columns].astype(jnp.int32).astype(jnp.float32)
            out_ref[chunk, :, columns] = (coded * steps[chunk : chunk + 1]).astype(jnp.bfloat16)


def dot(a, b):
    return jnp.dot(a, b, preferred_element_type=jnp.float32)


def split(x):
    high = x.astype(jnp.bfloat16)
    return high, (x - high.astype(jnp.float32)).astype(jnp.bfloat16)


HALF = BLOCK // 2
ALL = slice(0, BLOCK)
LOW = slice(0, HALF)
HIGH = slice(HALF, BLOCK)


def dot3(a, b, rows, columns):
    return dot(
        jnp.concatenate([a[0][rows], a[0][rows], a[1][rows]], axis=1),
        jnp.concatenate([b[0][:, columns], b[1][:, columns], b[0][:, columns]], axis=0),
    )


def put(pair, rows, columns, x):
    pair[0][rows, columns], pair[1][rows, columns] = split(x)


def mirror(pair):
    for part in pair:
        part[LOW, HIGH] = part[HIGH, LOW].T


def owner_kernel(me_ref, place_ref, got_ref, left_ref, right_ref, new_left_ref, new_right_ref, coded_ref,
                 sums_ref, scales_ref, prev_ref, new_ref, n_ref, raw_ref, n_parts_ref, q_parts_ref,
                 h_parts_ref, r_parts_ref, got_sem, new_sem):
    slot = pl.program_id(0)

    def fetch(side, k):
        source = (left_ref, right_ref)[side]
        return pltpu.make_async_copy(source.at[k], prev_ref.at[side, k], got_sem.at[side, k])

    def write(side, k):
        target = (new_left_ref, new_right_ref)[side]
        return pltpu.make_async_copy(new_ref.at[side, k], target.at[k], new_sem.at[side, k])

    @pl.when(slot == 0)
    def _():
        for k in range(SLOTS):
            for side in range(2):
                fetch(side, k).start()

    wanted = me_ref[0] * SLOTS + slot
    used = place_ref[0] == wanted
    for b in range(1, BLOCKS):
        used = used | (place_ref[b] == wanted)
    place = pl.ds(pl.multiple_of(slot * BLOCK, BLOCK), BLOCK)
    block = got_ref[:, place]
    block = jnp.where(used, block, jnp.zeros_like(block))
    turned = block.T
    steps = [(rows, columns, side) for rows, columns in ((ALL, LOW), (HIGH, HIGH)) for side in range(2)]

    def eye(rows, columns, value):
        shape = (rows.stop - rows.start, columns.stop - columns.start)
        down = lax.broadcasted_iota(jnp.int32, shape, 0) + rows.start
        across = lax.broadcasted_iota(jnp.int32, shape, 1) + columns.start
        return jnp.where(down == across, jnp.float32(value), jnp.float32(0))

    def pair(ref, side):
        return ref.at[side, 0], ref.at[side, 1]

    norms = []
    for side in range(2):
        gram = dot(block, turned) if side == 0 else dot(turned, block)
        fetch(side, slot).wait()
        stat = BETA * prev_ref[side, slot] + gram
        new_ref[side, slot] = stat
        write(side, slot).start()
        damped = stat + eye(ALL, ALL, EPS_DAMP)
        norm = jnp.sqrt(jnp.sum(damped * damped, keepdims=True))
        n = damped * (1.0 / norm)
        n_ref[side] = n
        put(pair(n_parts_ref, side), ALL, ALL, n)
        norms.append(norm)
    for rows, columns, side in steps:
        n = n_ref[side, rows, columns]
        n_parts = pair(n_parts_ref, side)
        n2 = dot3(n_parts, n_parts, rows, columns)
        put(pair(q_parts_ref, side), rows, columns, eye(rows, columns, 1.5625) - 2.5 * n + n2)
        put(pair(h_parts_ref, side), rows, columns, 1.25 * n - n2)
        if columns == LOW:
            mirror(pair(q_parts_ref, side))
            mirror(pair(h_parts_ref, side))
    for rows, columns, side in steps:
        q_parts = pair(q_parts_ref, side)
        put(pair(r_parts_ref, side), rows, columns, dot3(q_parts, q_parts, rows, columns))
        if columns == LOW:
            mirror(pair(r_parts_ref, side))
    for rows, columns, side in steps:
        product = dot3(pair(h_parts_ref, side), pair(r_parts_ref, side), rows, columns)
        product = eye(rows, columns, 1.5625) - 1.25 * n_ref[side, rows, columns] - product
        product = product * lax.rsqrt(jnp.sqrt(0.25 * norms[side]))
        put(pair(n_parts_ref, side), rows, columns, product)
        if columns == LOW:
            mirror(pair(n_parts_ref, side))
    left_root = jnp.concatenate([n_parts_ref[0, 0], n_parts_ref[0, 1]], axis=1)
    for columns in (LOW, HIGH):
        part = block[:, columns]
        put(pair(q_parts_ref, 0), ALL, columns, dot(left_root, jnp.concatenate([part, part], axis=0)))
    update_sq = jnp.zeros((1, 1), jnp.float32)
    for columns in (LOW, HIGH):
        raw = dot3(pair(q_parts_ref, 0), pair(n_parts_ref, 1), ALL, columns)
        raw_ref[:, columns] = raw
        update_sq += jnp.sum(raw * raw, keepdims=True)
    wide = block.astype(jnp.float32)
    grad_sq = jnp.sum(wide * wide, keepdims=True)
    line = lax.broadcasted_iota(jnp.int32, sums_ref.shape, 0)
    sums = jnp.where(line == 0, grad_sq, update_sq)
    raw = raw_ref[...].reshape(OWNERS, LINES, BLOCK)
    largest = jnp.max(jnp.max(jnp.abs(raw), axis=2, keepdims=True), axis=1, keepdims=True)
    largest = jnp.maximum(largest, 1e-30)
    coded = jnp.round(raw * (32767.0 / largest)).astype(jnp.int32)
    scales = largest * (1.0 / 32767.0)
    lane = lax.broadcasted_iota(jnp.int32, (1, 128), 1)
    for p in range(OWNERS):
        coded_ref[p, :, place] = coded[p].astype(jnp.int16)
        here = jnp.where(lane == wanted, scales[p], 0.0)
        scales_ref[pl.ds(p, 1), :] = jnp.where(slot == 0, here, scales_ref[pl.ds(p, 1), :] + here)

    @pl.when(slot == 0)
    def _():
        sums_ref[...] = sums

    @pl.when(slot == SLOTS - 1)
    def _():
        sums_ref[...] += sums
        for k in range(SLOTS):
            for side in range(2):
                write(side, k).wait()


def exchange(x, axes):
    return lax.all_to_all(x, axes, split_axis=0, concat_axis=0, tiled=True)


def add_permuted(x, axis, perms):
    return sum([lax.ppermute(x, axis, perm) for perm in perms], x)


def gather_sums(sums, scales):
    sums = add_permuted(sums, "mp", [[(d, (d + s) % SHARDS) for d in range(SHARDS)] for s in range(1, 4)])
    x = jnp.concatenate([sums, scales])
    x = add_permuted(x, "r", [[(d, d ^ s) for d in range(MEMBERS)] for s in range(1, 8)])
    return add_permuted(x, ("g", "r"), [[(d, d ^ (8 * s)) for d in range(OWNERS)] for s in range(1, 4)])


def gather_far(x):
    return add_permuted(x, "g", [[(d, d ^ 2) for d in range(GROUPS)]])


def shards(gradient, block_owner, prev_left, prev_right):
    shard = jnp.reshape(lax.axis_index("mp"), (1,)).astype(jnp.int32)
    me = jnp.reshape(lax.axis_index(("r", "g")), (1,)).astype(jnp.int32)
    spread_shape = (GROUPS, LINES, PER_SHARD * BLOCK)

    places = pl.pallas_call(
        place_table_kernel,
        out_shape=jax.ShapeDtypeStruct((BLOCKS,), jnp.int32),
        in_specs=[SMEM, SMEM],
        out_specs=SMEM,
        scratch_shapes=[pltpu.SMEM((OWNERS,), jnp.int32)],
        compiler_params=params(4),
        cost_estimate=pl.CostEstimate(flops=1000, bytes_accessed=1000, transcendentals=0),
        name="places",
    )(shard, block_owner)
    pieces = exchange(gradient.reshape(spread_shape), "g")
    routed = pl.pallas_call(
        route_kernel,
        out_shape=jax.ShapeDtypeStruct((OWNERS, LINES, SLOTS * BLOCK), jnp.bfloat16),
        in_specs=[SMEM, WHOLE],
        out_specs=WHOLE,
        compiler_params=params(4),
        name="route",
    )(places, pieces)
    got = exchange(routed, ("r", "g")).reshape(BLOCK, SLOTS * BLOCK)

    stat_spec = pl.BlockSpec(memory_space=pl.ANY)
    parts = pltpu.VMEM((2, 2, BLOCK, BLOCK), jnp.bfloat16)
    stat_shape = jax.ShapeDtypeStruct((SLOTS, BLOCK, BLOCK), jnp.float32)
    coded_shape = (OWNERS, LINES, SLOTS * BLOCK)
    new_left, new_right, coded, sums, scales = pl.pallas_call(
        owner_kernel,
        grid=(SLOTS,),
        out_shape=[
            stat_shape,
            stat_shape,
            jax.ShapeDtypeStruct(coded_shape, jnp.int16),
            jax.ShapeDtypeStruct((SUM_ROWS, 128), jnp.float32),
            jax.ShapeDtypeStruct((OWNERS, OWNERS * SLOTS), jnp.float32),
        ],
        in_specs=[SMEM, SMEM, WHOLE, stat_spec, stat_spec],
        out_specs=[
            stat_spec,
            stat_spec,
            WHOLE,
            WHOLE,
            WHOLE,
        ],
        scratch_shapes=[
            pltpu.VMEM((2, SLOTS, BLOCK, BLOCK), jnp.float32),
            pltpu.VMEM((2, SLOTS, BLOCK, BLOCK), jnp.float32),
            pltpu.VMEM((2, BLOCK, BLOCK), jnp.float32),
            pltpu.VMEM((BLOCK, BLOCK), jnp.float32),
            parts,
            parts,
            parts,
            parts,
            pltpu.SemaphoreType.DMA((2, SLOTS)),
            pltpu.SemaphoreType.DMA((2, SLOTS)),
        ],
        compiler_params=params(48),
        cost_estimate=pl.CostEstimate(
            flops=50 * 2 * BLOCK**3, bytes_accessed=12 * MIB, transcendentals=0
        ),
        name="owner",
    )(me, places, got, prev_left[0, 0], prev_right[0, 0])

    returned = exchange(coded, ("r", "g"))
    gathered = gather_sums(sums, scales)
    back = pl.pallas_call(
        collect_kernel,
        out_shape=jax.ShapeDtypeStruct(spread_shape, jnp.int16),
        in_specs=[SMEM, WHOLE],
        out_specs=WHOLE,
        compiler_params=params(8),
        name="collect",
    )(places, returned)
    gathered, back = lax.optimization_barrier((gathered, back))
    back = exchange(back, "g")
    update_out = pl.pallas_call(
        finish_kernel,
        out_shape=jax.ShapeDtypeStruct(spread_shape, jnp.bfloat16),
        in_specs=[SMEM, SMEM, WHOLE, WHOLE],
        out_specs=WHOLE,
        compiler_params=params(8),
        name="finish",
    )(me, places, gather_far(gathered), back).reshape(gradient.shape)
    return (update_out, new_left[None, None], new_right[None, None])


def solution(mesh):
    fine = Mesh(mesh.devices.reshape(GROUPS, MEMBERS, SHARDS), ("g", "r", "mp"))
    grad_spec = P(("g", "r"), "mp")
    stat_spec = P("mp", ("g", "r"), None, None, None)
    return jax.shard_map(
        shards,
        mesh=fine,
        in_specs=(grad_spec, P(), stat_spec, stat_spec),
        out_specs=(grad_spec, stat_spec, stat_spec),
        check_vma=False,
    )
```

```python
import jax
import jax.numpy as jnp
from jax import lax
from jax.experimental import pallas as pl
from jax.experimental.pallas import tpu as pltpu
from jax.sharding import Mesh
from jax.sharding import PartitionSpec as P

EPS_DAMP = 1.0
BETA = 0.95
BLOCK = 512
SHARDS = 4
GROUPS = 4
MEMBERS = 16
PER_SHARD = 8
BLOCKS = GROUPS * PER_SHARD
OWNERS = 64
SLOTS = 2
LINES = 8
CELLS = 2048 * 16384
MIB = 1024 * 1024
GRAD_LANE, UPDATE_LANE = 32, 36

WHOLE = pl.BlockSpec(memory_space=pltpu.VMEM)
SMEM = pl.BlockSpec(memory_space=pltpu.SMEM)


def params(mib):
    return pltpu.CompilerParams(vmem_limit_bytes=mib * MIB)


def place_table_kernel(shard_ref, owner_ref, place_ref, count_ref):
    base = shard_ref[0] * PER_SHARD

    def clear(o, _):
        count_ref[o] = 0
        return 0

    lax.fori_loop(0, OWNERS, clear, 0, unroll=8)
    for b in range(BLOCKS):
        owner = owner_ref[b // PER_SHARD, base + b % PER_SHARD]
        slot = count_ref[owner]
        count_ref[owner] = slot + 1
        place_ref[b] = (lax.rem(owner, MEMBERS) * GROUPS + owner // MEMBERS) * SLOTS + slot


def route_kernel(place_ref, in_ref, out_ref):
    for row in range(GROUPS):
        for j in range(PER_SHARD):
            place = place_ref[row * PER_SHARD + j]
            columns = pl.ds(pl.multiple_of(lax.rem(place, SLOTS) * BLOCK, BLOCK), BLOCK)
            out_ref[place // SLOTS, :, columns] = in_ref[row, :, pl.ds(j * BLOCK, BLOCK)]


def collect_kernel(place_ref, in_ref, out_ref, sums_ref):
    lane = lax.broadcasted_iota(jnp.int32, (LINES, 128), 1)
    line = lax.broadcasted_iota(jnp.int32, (LINES, 128), 0)
    tile = pl.ds(SLOTS * BLOCK, 128)
    for row in range(GROUPS):
        powers = jnp.zeros((LINES, 128), jnp.int32)
        for j in range(PER_SHARD):
            place = place_ref[row * PER_SHARD + j]
            position, slot = place // SLOTS, lax.rem(place, SLOTS)
            columns = pl.ds(pl.multiple_of(slot * BLOCK, BLOCK), BLOCK)
            out_ref[row, :, pl.ds(j * BLOCK, BLOCK)] = in_ref[position, :, columns]
            powers = jnp.where(lane == j + 64 * slot, in_ref[position, :, tile].astype(jnp.int32), powers)
        out_ref[row, :, pl.ds(PER_SHARD * BLOCK, 128)] = powers.astype(jnp.int16)
    sums = jnp.zeros((LINES, 128), jnp.float32)
    for first in range(0, OWNERS, LINES):
        digits = jnp.zeros((LINES, 128), jnp.int32)
        for k in range(LINES):
            digits = jnp.where(line == k, in_ref[first + k, :, tile].astype(jnp.int32), digits)
        digits = digits.astype(jnp.float32)
        value = pltpu.roll(digits, 127, 1) + pltpu.roll(digits, 126, 1) * (1.0 / 4096.0)
        here = (lane == GRAD_LANE) | (lane == UPDATE_LANE)
        sums += jnp.where(here, value * jnp.exp2(jnp.where(here, digits, 0.0)), 0.0)
    sums_ref[...] = sums


def finish_kernel(sums_ref, in_ref, out_ref):
    totals = jnp.sum(sums_ref[...], axis=0, keepdims=True)
    grad_total = totals[:, GRAD_LANE : GRAD_LANE + 1]
    update_total = totals[:, UPDATE_LANE : UPDATE_LANE + 1]
    graft = jnp.sqrt(grad_total / CELLS) * lax.rsqrt(update_total / CELLS + 1e-06)
    for chunk in range(GROUPS):
        powers = in_ref[chunk, :, pl.ds(PER_SHARD * BLOCK, 128)].astype(jnp.int32).astype(jnp.float32)
        steps = jnp.exp2(powers + pltpu.roll(powers, 64, 1)) * graft
        for j in range(PER_SHARD):
            columns = pl.ds(j * BLOCK, BLOCK)
            coded = in_ref[chunk, :, columns].astype(jnp.int32).astype(jnp.float32)
            out_ref[chunk, :, columns] = (coded * steps[:, j : j + 1]).astype(jnp.bfloat16)


def dot(a, b):
    return jnp.dot(a, b, preferred_element_type=jnp.float32)


def split(x):
    high = x.astype(jnp.bfloat16)
    return high, (x - high.astype(jnp.float32)).astype(jnp.bfloat16)


HALF = BLOCK // 2
ALL = slice(0, BLOCK)
LOW = slice(0, HALF)
HIGH = slice(HALF, BLOCK)


def dot3(a, b, rows, columns):
    return dot(
        jnp.concatenate([a[0][rows], a[0][rows], a[1][rows]], axis=1),
        jnp.concatenate([b[0][:, columns], b[1][:, columns], b[0][:, columns]], axis=0),
    )


def put(pair, rows, columns, x):
    pair[0][rows, columns], pair[1][rows, columns] = split(x)


def mirror(pair):
    for part in pair:
        part[LOW, HIGH] = part[HIGH, LOW].T


def owner_kernel(me_ref, place_ref, got_ref, left_ref, right_ref, new_left_ref, new_right_ref, coded_ref,
                 power_ref, sums_ref, prev_ref, new_ref, n_ref, raw_ref, n_parts_ref, q_parts_ref,
                 h_parts_ref, r_parts_ref, got_sem, new_sem):
    slot = pl.program_id(0)

    def fetch(side, k):
        source = (left_ref, right_ref)[side]
        return pltpu.make_async_copy(source.at[k], prev_ref.at[side, k], got_sem.at[side, k])

    def write(side, k):
        target = (new_left_ref, new_right_ref)[side]
        return pltpu.make_async_copy(new_ref.at[side, k], target.at[k], new_sem.at[side, k])

    @pl.when(slot == 0)
    def _():
        for k in range(SLOTS):
            for side in range(2):
                fetch(side, k).start()

    wanted = me_ref[0] * SLOTS + slot
    used = place_ref[0] == wanted
    for b in range(1, BLOCKS):
        used = used | (place_ref[b] == wanted)
    place = pl.ds(pl.multiple_of(slot * BLOCK, BLOCK), BLOCK)
    block = got_ref[:, place]
    block = jnp.where(used, block, jnp.zeros_like(block))
    turned = block.T
    steps = [(rows, columns, side) for rows, columns in ((ALL, LOW), (HIGH, HIGH)) for side in range(2)]

    def eye(rows, columns, value):
        shape = (rows.stop - rows.start, columns.stop - columns.start)
        down = lax.broadcasted_iota(jnp.int32, shape, 0) + rows.start
        across = lax.broadcasted_iota(jnp.int32, shape, 1) + columns.start
        return jnp.where(down == across, jnp.float32(value), jnp.float32(0))

    def pair(ref, side):
        return ref.at[side, 0], ref.at[side, 1]

    norms = []
    for side in range(2):
        gram = dot(block, turned) if side == 0 else dot(turned, block)
        fetch(side, slot).wait()
        stat = BETA * prev_ref[side, slot] + gram
        new_ref[side, slot] = stat
        write(side, slot).start()
        damped = stat + eye(ALL, ALL, EPS_DAMP)
        norm = jnp.sqrt(jnp.sum(damped * damped, keepdims=True))
        n = damped * (1.0 / norm)
        n_ref[side] = n
        put(pair(n_parts_ref, side), ALL, ALL, n)
        norms.append(norm)
    for rows, columns, side in steps:
        n = n_ref[side, rows, columns]
        n_parts = pair(n_parts_ref, side)
        n2 = dot3(n_parts, n_parts, rows, columns)
        put(pair(q_parts_ref, side), rows, columns, eye(rows, columns, 1.5625) - 2.5 * n + n2)
        put(pair(h_parts_ref, side), rows, columns, 1.25 * n - n2)
        if columns == LOW:
            mirror(pair(q_parts_ref, side))
            mirror(pair(h_parts_ref, side))
    for rows, columns, side in steps:
        q_parts = pair(q_parts_ref, side)
        put(pair(r_parts_ref, side), rows, columns, dot3(q_parts, q_parts, rows, columns))
        if columns == LOW:
            mirror(pair(r_parts_ref, side))
    for rows, columns, side in steps:
        product = dot3(pair(h_parts_ref, side), pair(r_parts_ref, side), rows, columns)
        product = eye(rows, columns, 1.5625) - 1.25 * n_ref[side, rows, columns] - product
        product = product * lax.rsqrt(jnp.sqrt(0.25 * norms[side]))
        put(pair(n_parts_ref, side), rows, columns, product)
        if columns == LOW:
            mirror(pair(n_parts_ref, side))
    left_root = jnp.concatenate([n_parts_ref[0, 0], n_parts_ref[0, 1]], axis=1)
    for columns in (LOW, HIGH):
        part = block[:, columns]
        put(pair(q_parts_ref, 0), ALL, columns, dot(left_root, jnp.concatenate([part, part], axis=0)))
    update_sq = jnp.zeros((1, 1), jnp.float32)
    for columns in (LOW, HIGH):
        raw = dot3(pair(q_parts_ref, 0), pair(n_parts_ref, 1), ALL, columns)
        raw_ref[:, columns] = raw
        update_sq += jnp.sum(raw * raw, keepdims=True)
    wide = block.astype(jnp.float32)
    grad_sq = jnp.sum(wide * wide, keepdims=True)
    lane = lax.broadcasted_iota(jnp.int32, (1, 128), 1)
    sums = jnp.where(lane < UPDATE_LANE, grad_sq, update_sq)
    raw = raw_ref[...]
    largest = jnp.max(jnp.abs(raw), axis=1, keepdims=True)
    power = jnp.ceil(jnp.log2(jnp.maximum(largest, 1e-30)) + 0.001) - 15.0
    coded = jnp.round(raw * jnp.exp2(-power)).astype(jnp.int32)
    for p in range(OWNERS):
        coded_ref[p, :, place] = coded[p * LINES : (p + 1) * LINES].astype(jnp.int16)

    @pl.when(slot == 0)
    def _():
        sums_ref[...] = sums
        power_ref[...] = jnp.broadcast_to(power, power_ref.shape)

    @pl.when(slot == SLOTS - 1)
    def _():
        total = sums_ref[...] + sums
        exponent = jnp.ceil(jnp.log2(jnp.maximum(total, 1e-30)))
        mantissa = total * jnp.exp2(12.0 - exponent)
        upper = jnp.floor(mantissa)
        lower = jnp.round((mantissa - upper) * 4096.0)
        start = jnp.where(lane < UPDATE_LANE, GRAD_LANE, UPDATE_LANE)
        digits = jnp.where(lane == start, exponent - 12.0, jnp.where(lane == start + 1, upper, lower))
        held = (lane >= GRAD_LANE) & (lane < UPDATE_LANE + 3)
        powers = jnp.where(held, digits, jnp.where(lane < 64, power_ref[...], power)).astype(jnp.int32)
        for p in range(OWNERS):
            coded_ref[p, :, pl.ds(SLOTS * BLOCK, 128)] = powers[p * LINES : (p + 1) * LINES].astype(jnp.int16)
        for k in range(SLOTS):
            for side in range(2):
                write(side, k).wait()


def exchange(x, axes):
    return lax.all_to_all(x, axes, split_axis=0, concat_axis=0, tiled=True)


def add_permuted(x, axis, perms):
    return sum([lax.ppermute(x, axis, perm) for perm in perms], x)


def sum_mp(x):
    return add_permuted(x, "mp", [[(d, (d + s) % SHARDS) for d in range(SHARDS)] for s in range(1, 4)])


def shards(gradient, block_owner, prev_left, prev_right):
    shard = jnp.reshape(lax.axis_index("mp"), (1,)).astype(jnp.int32)
    me = jnp.reshape(lax.axis_index(("r", "g")), (1,)).astype(jnp.int32)
    spread_shape = (GROUPS, LINES, PER_SHARD * BLOCK)

    places = pl.pallas_call(
        place_table_kernel,
        out_shape=jax.ShapeDtypeStruct((BLOCKS,), jnp.int32),
        in_specs=[SMEM, SMEM],
        out_specs=SMEM,
        scratch_shapes=[pltpu.SMEM((OWNERS,), jnp.int32)],
        compiler_params=params(4),
        cost_estimate=pl.CostEstimate(flops=1000, bytes_accessed=1000, transcendentals=0),
        name="places",
    )(shard, block_owner)
    pieces = exchange(gradient.reshape(spread_shape), "g")
    routed = pl.pallas_call(
        route_kernel,
        out_shape=jax.ShapeDtypeStruct((OWNERS, LINES, SLOTS * BLOCK), jnp.bfloat16),
        in_specs=[SMEM, WHOLE],
        out_specs=WHOLE,
        compiler_params=params(4),
        name="route",
    )(places, pieces)
    got = exchange(routed, ("r", "g")).reshape(BLOCK, SLOTS * BLOCK)

    stat_spec = pl.BlockSpec(memory_space=pl.ANY)
    parts = pltpu.VMEM((2, 2, BLOCK, BLOCK), jnp.bfloat16)
    stat_shape = jax.ShapeDtypeStruct((SLOTS, BLOCK, BLOCK), jnp.float32)
    coded_shape = (OWNERS, LINES, SLOTS * BLOCK + 128)
    new_left, new_right, coded = pl.pallas_call(
        owner_kernel,
        grid=(SLOTS,),
        out_shape=[
            stat_shape,
            stat_shape,
            jax.ShapeDtypeStruct(coded_shape, jnp.int16),
        ],
        in_specs=[SMEM, SMEM, WHOLE, stat_spec, stat_spec],
        out_specs=[
            stat_spec,
            stat_spec,
            WHOLE,
        ],
        scratch_shapes=[
            pltpu.VMEM((BLOCK, 128), jnp.float32),
            pltpu.VMEM((1, 128), jnp.float32),
            pltpu.VMEM((2, SLOTS, BLOCK, BLOCK), jnp.float32),
            pltpu.VMEM((2, SLOTS, BLOCK, BLOCK), jnp.float32),
            pltpu.VMEM((2, BLOCK, BLOCK), jnp.float32),
            pltpu.VMEM((BLOCK, BLOCK), jnp.float32),
            parts,
            parts,
            parts,
            parts,
            pltpu.SemaphoreType.DMA((2, SLOTS)),
            pltpu.SemaphoreType.DMA((2, SLOTS)),
        ],
        compiler_params=params(48),
        cost_estimate=pl.CostEstimate(
            flops=50 * 2 * BLOCK**3, bytes_accessed=12 * MIB, transcendentals=0
        ),
        name="owner",
    )(me, places, got, prev_left[0, 0], prev_right[0, 0])

    returned = exchange(coded, ("r", "g"))
    back, sums = pl.pallas_call(
        collect_kernel,
        out_shape=[
            jax.ShapeDtypeStruct((GROUPS, LINES, PER_SHARD * BLOCK + 128), jnp.int16),
            jax.ShapeDtypeStruct((LINES, 128), jnp.float32),
        ],
        in_specs=[SMEM, WHOLE],
        out_specs=[WHOLE, WHOLE],
        compiler_params=params(8),
        name="collect",
    )(places, returned)
    back = exchange(back, "g")
    update_out = pl.pallas_call(
        finish_kernel,
        out_shape=jax.ShapeDtypeStruct(spread_shape, jnp.bfloat16),
        in_specs=[WHOLE, WHOLE],
        out_specs=WHOLE,
        compiler_params=params(8),
        name="finish",
    )(sum_mp(sums), back).reshape(gradient.shape)
    return (update_out, new_left[None, None], new_right[None, None])


def solution(mesh):
    fine = Mesh(mesh.devices.reshape(GROUPS, MEMBERS, SHARDS), ("g", "r", "mp"))
    grad_spec = P(("g", "r"), "mp")
    stat_spec = P("mp", ("g", "r"), None, None, None)
    return jax.shard_map(
        shards,
        mesh=fine,
        in_specs=(grad_spec, P(), stat_spec, stat_spec),
        out_specs=(grad_spec, stat_spec, stat_spec),
        check_vma=False,
    )
```

```python
import jax
import jax.numpy as jnp
from jax import lax
from jax.experimental import pallas as pl
from jax.experimental.pallas import tpu as pltpu
from jax.sharding import Mesh
from jax.sharding import PartitionSpec as P

EPS_DAMP = 1.0
BETA = 0.95
BLOCK = 512
SHARDS = 4
GROUPS = 4
MEMBERS = 16
PER_SHARD = 8
BLOCKS = GROUPS * PER_SHARD
OWNERS = 64
SLOTS = 2
LINES = 8
CELLS = 2048 * 16384
MIB = 1024 * 1024
GRAD_LANE, UPDATE_LANE = 32, 36

WHOLE = pl.BlockSpec(memory_space=pltpu.VMEM)
SMEM = pl.BlockSpec(memory_space=pltpu.SMEM)


def params(mib):
    return pltpu.CompilerParams(vmem_limit_bytes=mib * MIB)


def place_table_kernel(shard_ref, owner_ref, place_ref, count_ref):
    base = shard_ref[0] * PER_SHARD

    def clear(o, _):
        count_ref[o] = 0
        return 0

    lax.fori_loop(0, OWNERS, clear, 0, unroll=8)
    for b in range(BLOCKS):
        owner = owner_ref[b // PER_SHARD, base + b % PER_SHARD]
        slot = count_ref[owner]
        count_ref[owner] = slot + 1
        place_ref[b] = (lax.rem(owner, MEMBERS) * GROUPS + owner // MEMBERS) * SLOTS + slot


def route_kernel(place_ref, in_ref, out_ref, sem):
    copies = []
    for row in range(GROUPS):
        for j in range(PER_SHARD):
            place = place_ref[row * PER_SHARD + j]
            columns = pl.ds(pl.multiple_of(lax.rem(place, SLOTS) * BLOCK, BLOCK), BLOCK)
            copy = pltpu.make_async_copy(
                in_ref.at[row, :, pl.ds(j * BLOCK, BLOCK)],
                out_ref.at[place // SLOTS, :, columns],
                sem.at[row, j],
            )
            copy.start()
            copies.append(copy)
    for copy in copies:
        copy.wait()


def collect_kernel(place_ref, in_ref, out_ref, sums_ref):
    lane = lax.broadcasted_iota(jnp.int32, (LINES, 128), 1)
    line = lax.broadcasted_iota(jnp.int32, (LINES, 128), 0)
    tile = pl.ds(SLOTS * BLOCK, 128)
    for row in range(GROUPS):
        powers = jnp.zeros((LINES, 128), jnp.int32)
        for j in range(PER_SHARD):
            place = place_ref[row * PER_SHARD + j]
            position, slot = place // SLOTS, lax.rem(place, SLOTS)
            columns = pl.ds(pl.multiple_of(slot * BLOCK, BLOCK), BLOCK)
            out_ref[row, :, pl.ds(j * BLOCK, BLOCK)] = in_ref[position, :, columns]
            powers = jnp.where(lane == j + 64 * slot, in_ref[position, :, tile].astype(jnp.int32), powers)
        out_ref[row, :, pl.ds(PER_SHARD * BLOCK, 128)] = powers.astype(jnp.int16)
    sums = jnp.zeros((LINES, 128), jnp.float32)
    for first in range(0, OWNERS, LINES):
        digits = jnp.zeros((LINES, 128), jnp.int32)
        for k in range(LINES):
            digits = jnp.where(line == k, in_ref[first + k, :, tile].astype(jnp.int32), digits)
        digits = digits.astype(jnp.float32)
        value = pltpu.roll(digits, 127, 1) + pltpu.roll(digits, 126, 1) * (1.0 / 4096.0)
        here = (lane == GRAD_LANE) | (lane == UPDATE_LANE)
        sums += jnp.where(here, value * jnp.exp2(jnp.where(here, digits, 0.0)), 0.0)
    sums_ref[...] = sums


def finish_kernel(sums_ref, in_ref, out_ref):
    totals = jnp.sum(sums_ref[...], axis=0, keepdims=True)
    grad_total = totals[:, GRAD_LANE : GRAD_LANE + 1]
    update_total = totals[:, UPDATE_LANE : UPDATE_LANE + 1]
    graft = jnp.sqrt(grad_total / CELLS) * lax.rsqrt(update_total / CELLS + 1e-06)
    for chunk in range(GROUPS):
        powers = in_ref[chunk, :, pl.ds(PER_SHARD * BLOCK, 128)].astype(jnp.int32).astype(jnp.float32)
        steps = jnp.exp2(powers + pltpu.roll(powers, 64, 1)) * graft
        for j in range(PER_SHARD):
            columns = pl.ds(j * BLOCK, BLOCK)
            coded = in_ref[chunk, :, columns].astype(jnp.int32).astype(jnp.float32)
            out_ref[chunk, :, columns] = (coded * steps[:, j : j + 1]).astype(jnp.bfloat16)


def dot(a, b):
    return jnp.dot(a, b, preferred_element_type=jnp.float32)


def split(x):
    high = x.astype(jnp.bfloat16)
    return high, (x - high.astype(jnp.float32)).astype(jnp.bfloat16)


HALF = BLOCK // 2
ALL = slice(0, BLOCK)
LOW = slice(0, HALF)
HIGH = slice(HALF, BLOCK)


def dot3(a, b, rows, columns):
    return dot(
        jnp.concatenate([a[0][rows], a[0][rows], a[1][rows]], axis=1),
        jnp.concatenate([b[0][:, columns], b[1][:, columns], b[0][:, columns]], axis=0),
    )


def put(pair, rows, columns, x):
    pair[0][rows, columns], pair[1][rows, columns] = split(x)


def mirror(pair):
    for part in pair:
        part[LOW, HIGH] = part[HIGH, LOW].T


def owner_kernel(me_ref, place_ref, got_ref, left_ref, right_ref, new_left_ref, new_right_ref, coded_ref,
                 prev_ref, new_ref, n_ref, raw_ref, n_parts_ref, q_parts_ref, h_parts_ref, r_parts_ref,
                 staged_ref, got_sem, new_sem, coded_sem):
    slots = range(SLOTS)
    both = [(slot, side) for slot in slots for side in range(2)]

    def fetch(slot, side):
        source = (left_ref, right_ref)[side]
        return pltpu.make_async_copy(source.at[slot], prev_ref.at[slot, side], got_sem.at[slot, side])

    def write(slot, side):
        target = (new_left_ref, new_right_ref)[side]
        return pltpu.make_async_copy(new_ref.at[slot, side], target.at[slot], new_sem.at[slot, side])

    def send(slot):
        last = BLOCK + 128 if slot == SLOTS - 1 else BLOCK
        columns = pl.ds(slot * BLOCK, last)
        return pltpu.make_async_copy(
            staged_ref.at[:, :, columns], coded_ref.at[:, :, columns], coded_sem.at[slot]
        )

    def eye(rows, columns, value):
        shape = (rows.stop - rows.start, columns.stop - columns.start)
        down = lax.broadcasted_iota(jnp.int32, shape, 0) + rows.start
        across = lax.broadcasted_iota(jnp.int32, shape, 1) + columns.start
        return jnp.where(down == across, jnp.float32(value), jnp.float32(0))

    def pair(ref, slot, side):
        return ref.at[slot, side, 0], ref.at[slot, side, 1]

    for slot, side in both:
        fetch(slot, side).start()
    blocks, turneds = [], []
    for slot in slots:
        wanted = me_ref[0] * SLOTS + slot
        used = place_ref[0] == wanted
        for b in range(1, BLOCKS):
            used = used | (place_ref[b] == wanted)
        block = got_ref[:, slot * BLOCK : (slot + 1) * BLOCK]
        block = jnp.where(used, block, jnp.zeros_like(block))
        blocks.append(block)
        turneds.append(block.T)

    norms = {}
    for slot, side in both:
        block, turned = blocks[slot], turneds[slot]
        gram = dot(block, turned) if side == 0 else dot(turned, block)
        fetch(slot, side).wait()
        stat = BETA * prev_ref[slot, side] + gram
        new_ref[slot, side] = stat
        write(slot, side).start()
        damped = stat + eye(ALL, ALL, EPS_DAMP)
        norm = jnp.sqrt(jnp.sum(damped * damped, keepdims=True))
        n = damped * (1.0 / norm)
        n_ref[slot, side] = n
        put(pair(n_parts_ref, slot, side), ALL, ALL, n)
        norms[slot, side] = norm

    steps = [(rows, columns, k, s) for rows, columns in ((ALL, LOW), (HIGH, HIGH)) for k, s in both]
    for rows, columns, slot, side in steps:
        n = n_ref[slot, side, rows, columns]
        n_parts, q_parts = pair(n_parts_ref, slot, side), pair(q_parts_ref, slot, side)
        h_parts = pair(h_parts_ref, slot, side)
        n2 = dot3(n_parts, n_parts, rows, columns)
        put(q_parts, rows, columns, eye(rows, columns, 1.5625) - 2.5 * n + n2)
        put(h_parts, rows, columns, 1.25 * n - n2)
        if columns == LOW:
            mirror(q_parts)
            mirror(h_parts)
    for rows, columns, slot, side in steps:
        q_parts, r_parts = pair(q_parts_ref, slot, side), pair(r_parts_ref, slot, side)
        put(r_parts, rows, columns, dot3(q_parts, q_parts, rows, columns))
        if columns == LOW:
            mirror(r_parts)
    for rows, columns, slot, side in steps:
        product = dot3(pair(h_parts_ref, slot, side), pair(r_parts_ref, slot, side), rows, columns)
        product = eye(rows, columns, 1.5625) - 1.25 * n_ref[slot, side, rows, columns] - product
        product = product * lax.rsqrt(jnp.sqrt(0.25 * norms[slot, side]))
        put(pair(n_parts_ref, slot, side), rows, columns, product)
        if columns == LOW:
            mirror(pair(n_parts_ref, slot, side))
    for columns in (LOW, HIGH):
        for slot in slots:
            high, low = pair(n_parts_ref, slot, 0)
            part = blocks[slot][:, columns]
            half = dot(jnp.concatenate([high[...], low[...]], axis=1), jnp.concatenate([part, part], axis=0))
            put(pair(q_parts_ref, slot, 0), ALL, columns, half)
    grad_sq = jnp.zeros((1, 1), jnp.float32)
    update_sq = jnp.zeros((1, 1), jnp.float32)
    for slot in slots:
        for columns in (LOW, HIGH):
            raw = dot3(pair(q_parts_ref, slot, 0), pair(n_parts_ref, slot, 1), ALL, columns)
            raw_ref[slot, :, columns] = raw
            update_sq += jnp.sum(raw * raw, keepdims=True)
        wide = blocks[slot].astype(jnp.float32)
        grad_sq += jnp.sum(wide * wide, keepdims=True)

    row_powers = []
    for slot in slots:
        raw = raw_ref[slot]
        largest = jnp.max(jnp.abs(raw), axis=1, keepdims=True)
        power = jnp.ceil(jnp.log2(jnp.maximum(largest, 1e-30)) + 0.001) - 15.0
        coded = jnp.round(raw * jnp.exp2(-power)).astype(jnp.int32)
        for p in range(OWNERS):
            staged_ref[p, :, pl.ds(slot * BLOCK, BLOCK)] = coded[p * LINES : (p + 1) * LINES].astype(jnp.int16)
        row_powers.append(power)
        if slot < SLOTS - 1:
            send(slot).start()

    lane = lax.broadcasted_iota(jnp.int32, (1, 128), 1)
    total = jnp.where(lane < UPDATE_LANE, grad_sq, update_sq)
    exponent = jnp.ceil(jnp.log2(jnp.maximum(total, 1e-30)))
    mantissa = total * jnp.exp2(12.0 - exponent)
    upper = jnp.floor(mantissa)
    lower = jnp.round((mantissa - upper) * 4096.0)
    start = jnp.where(lane < UPDATE_LANE, GRAD_LANE, UPDATE_LANE)
    digits = jnp.where(lane == start, exponent - 12.0, jnp.where(lane == start + 1, upper, lower))
    held = (lane >= GRAD_LANE) & (lane < UPDATE_LANE + 3)
    powers = jnp.where(lane < 64, row_powers[0], row_powers[1])
    powers = jnp.where(held, digits, powers).astype(jnp.int32)
    for p in range(OWNERS):
        staged_ref[p, :, pl.ds(SLOTS * BLOCK, 128)] = powers[p * LINES : (p + 1) * LINES].astype(jnp.int16)
    send(SLOTS - 1).start()
    for slot, side in both:
        write(slot, side).wait()
    for slot in slots:
        send(slot).wait()


def exchange(x, axes):
    return lax.all_to_all(x, axes, split_axis=0, concat_axis=0, tiled=True)


def add_permuted(x, axis, perms):
    return sum([lax.ppermute(x, axis, perm) for perm in perms], x)


def sum_mp(x):
    return add_permuted(x, "mp", [[(d, (d + s) % SHARDS) for d in range(SHARDS)] for s in range(1, 4)])


def shards(gradient, block_owner, prev_left, prev_right):
    shard = jnp.reshape(lax.axis_index("mp"), (1,)).astype(jnp.int32)
    me = jnp.reshape(lax.axis_index(("r", "g")), (1,)).astype(jnp.int32)
    spread_shape = (GROUPS, LINES, PER_SHARD * BLOCK)

    places = pl.pallas_call(
        place_table_kernel,
        out_shape=jax.ShapeDtypeStruct((BLOCKS,), jnp.int32),
        in_specs=[SMEM, SMEM],
        out_specs=SMEM,
        scratch_shapes=[pltpu.SMEM((OWNERS,), jnp.int32)],
        compiler_params=params(4),
        cost_estimate=pl.CostEstimate(flops=1000, bytes_accessed=1000, transcendentals=0),
        name="places",
    )(shard, block_owner)
    pieces = exchange(gradient.reshape(spread_shape), "g")
    routed = pl.pallas_call(
        route_kernel,
        out_shape=jax.ShapeDtypeStruct((OWNERS, LINES, SLOTS * BLOCK), jnp.bfloat16),
        in_specs=[SMEM, WHOLE],
        out_specs=pl.BlockSpec(memory_space=pl.ANY),
        scratch_shapes=[pltpu.SemaphoreType.DMA((GROUPS, PER_SHARD))],
        compiler_params=params(4),
        name="route",
    )(places, pieces)
    got = exchange(routed, ("r", "g")).reshape(BLOCK, SLOTS * BLOCK)

    stat_spec = pl.BlockSpec(memory_space=pl.ANY)
    stat_shape = jax.ShapeDtypeStruct((SLOTS, BLOCK, BLOCK), jnp.float32)
    coded_shape = (OWNERS, LINES, SLOTS * BLOCK + 128)
    wide = pltpu.VMEM((SLOTS, 2, BLOCK, BLOCK), jnp.float32)
    parts = pltpu.VMEM((SLOTS, 2, 2, BLOCK, BLOCK), jnp.bfloat16)
    new_left, new_right, coded = pl.pallas_call(
        owner_kernel,
        out_shape=[stat_shape, stat_shape, jax.ShapeDtypeStruct(coded_shape, jnp.int16)],
        in_specs=[SMEM, SMEM, WHOLE, stat_spec, stat_spec],
        out_specs=[stat_spec, stat_spec, stat_spec],
        scratch_shapes=[
            wide,
            wide,
            wide,
            pltpu.VMEM((SLOTS, BLOCK, BLOCK), jnp.float32),
            parts,
            parts,
            parts,
            parts,
            pltpu.VMEM(coded_shape, jnp.int16),
            pltpu.SemaphoreType.DMA((SLOTS, 2)),
            pltpu.SemaphoreType.DMA((SLOTS, 2)),
            pltpu.SemaphoreType.DMA((SLOTS,)),
        ],
        compiler_params=params(50),
        cost_estimate=pl.CostEstimate(
            flops=50 * 2 * BLOCK**3, bytes_accessed=12 * MIB, transcendentals=0
        ),
        name="owner",
    )(me, places, got, prev_left[0, 0], prev_right[0, 0])

    returned = exchange(coded, ("r", "g"))
    back, sums = pl.pallas_call(
        collect_kernel,
        out_shape=[
            jax.ShapeDtypeStruct((GROUPS, LINES, PER_SHARD * BLOCK + 128), jnp.int16),
            jax.ShapeDtypeStruct((LINES, 128), jnp.float32),
        ],
        in_specs=[SMEM, WHOLE],
        out_specs=[WHOLE, WHOLE],
        compiler_params=params(8),
        name="collect",
    )(places, returned)
    back = exchange(back, "g")
    update_out = pl.pallas_call(
        finish_kernel,
        out_shape=jax.ShapeDtypeStruct(spread_shape, jnp.bfloat16),
        in_specs=[WHOLE, WHOLE],
        out_specs=WHOLE,
        compiler_params=params(8),
        name="finish",
    )(sum_mp(sums), back).reshape(gradient.shape)
    return (update_out, new_left[None, None], new_right[None, None])


def solution(mesh):
    fine = Mesh(mesh.devices.reshape(GROUPS, MEMBERS, SHARDS), ("g", "r", "mp"))
    grad_spec = P(("g", "r"), "mp")
    stat_spec = P("mp", ("g", "r"), None, None, None)
    return jax.shard_map(
        shards,
        mesh=fine,
        in_specs=(grad_spec, P(), stat_spec, stat_spec),
        out_specs=(grad_spec, stat_spec, stat_spec),
        check_vma=False,
    )
```

```python
import jax
import jax.numpy as jnp
from jax import lax
from jax.experimental import pallas as pl
from jax.experimental.pallas import tpu as pltpu
from jax.sharding import Mesh
from jax.sharding import PartitionSpec as P

EPS_DAMP = 1.0
BETA = 0.95
BLOCK = 512
SHARDS = 4
GROUPS = 4
MEMBERS = 16
PER_SHARD = 8
BLOCKS = GROUPS * PER_SHARD
OWNERS = 64
SLOTS = 2
LINES = 8
CELLS = 2048 * 16384
MIB = 1024 * 1024
GRAD_LANE, UPDATE_LANE = 32, 36

WHOLE = pl.BlockSpec(memory_space=pltpu.VMEM)
SMEM = pl.BlockSpec(memory_space=pltpu.SMEM)


def params(mib):
    return pltpu.CompilerParams(vmem_limit_bytes=mib * MIB)


def place_table_kernel(shard_ref, owner_ref, place_ref, count_ref):
    base = shard_ref[0] * PER_SHARD

    def clear(o, _):
        count_ref[o] = 0
        return 0

    lax.fori_loop(0, OWNERS, clear, 0, unroll=8)
    for b in range(BLOCKS):
        owner = owner_ref[b // PER_SHARD, base + b % PER_SHARD]
        slot = count_ref[owner]
        count_ref[owner] = slot + 1
        place_ref[b] = (lax.rem(owner, MEMBERS) * GROUPS + owner // MEMBERS) * SLOTS + slot


def route_kernel(place_ref, in_ref, out_ref, sem):
    copies = []
    for row in range(GROUPS):
        for j in range(PER_SHARD):
            place = place_ref[row * PER_SHARD + j]
            columns = pl.ds(pl.multiple_of(lax.rem(place, SLOTS) * BLOCK, BLOCK), BLOCK)
            copy = pltpu.make_async_copy(
                in_ref.at[row, :, pl.ds(j * BLOCK, BLOCK)],
                out_ref.at[place // SLOTS, :, columns],
                sem.at[row, j],
            )
            copy.start()
            copies.append(copy)
    for copy in copies:
        copy.wait()


def collect_kernel(place_ref, in_ref, out_ref, sums_ref):
    lane = lax.broadcasted_iota(jnp.int32, (LINES, 128), 1)
    line = lax.broadcasted_iota(jnp.int32, (LINES, 128), 0)
    tile = pl.ds(SLOTS * BLOCK, 128)
    for row in range(GROUPS):
        powers = jnp.zeros((LINES, 128), jnp.int32)
        for j in range(PER_SHARD):
            place = place_ref[row * PER_SHARD + j]
            position, slot = place // SLOTS, lax.rem(place, SLOTS)
            columns = pl.ds(pl.multiple_of(slot * BLOCK, BLOCK), BLOCK)
            out_ref[row, :, pl.ds(j * BLOCK, BLOCK)] = in_ref[position, :, columns]
            powers = jnp.where(lane == j + 64 * slot, in_ref[position, :, tile].astype(jnp.int32), powers)
        out_ref[row, :, pl.ds(PER_SHARD * BLOCK, 128)] = powers.astype(jnp.int16)
    sums = jnp.zeros((LINES, 128), jnp.float32)
    for first in range(0, OWNERS, LINES):
        digits = jnp.zeros((LINES, 128), jnp.int32)
        for k in range(LINES):
            digits = jnp.where(line == k, in_ref[first + k, :, tile].astype(jnp.int32), digits)
        digits = digits.astype(jnp.float32)
        value = pltpu.roll(digits, 127, 1) + pltpu.roll(digits, 126, 1) * (1.0 / 4096.0)
        here = (lane == GRAD_LANE) | (lane == UPDATE_LANE)
        sums += jnp.where(here, value * jnp.exp2(jnp.where(here, digits, 0.0)), 0.0)
    sums_ref[...] = sums


def finish_kernel(sums_ref, in_ref, out_ref):
    totals = jnp.sum(sums_ref[...], axis=0, keepdims=True)
    grad_total = totals[:, GRAD_LANE : GRAD_LANE + 1]
    update_total = totals[:, UPDATE_LANE : UPDATE_LANE + 1]
    graft = jnp.sqrt(grad_total / CELLS) * lax.rsqrt(update_total / CELLS + 1e-06)
    for chunk in range(GROUPS):
        powers = in_ref[chunk, :, pl.ds(PER_SHARD * BLOCK, 128)].astype(jnp.int32).astype(jnp.float32)
        steps = jnp.exp2(powers + pltpu.roll(powers, 64, 1)) * graft
        for j in range(PER_SHARD):
            columns = pl.ds(j * BLOCK, BLOCK)
            coded = in_ref[chunk, :, columns].astype(jnp.int32).astype(jnp.float32)
            out_ref[chunk, :, columns] = (coded * steps[:, j : j + 1]).astype(jnp.bfloat16)


def dot(a, b):
    return jnp.dot(a, b, preferred_element_type=jnp.float32)


def split(x):
    high = x.astype(jnp.bfloat16)
    return high, (x - high.astype(jnp.float32)).astype(jnp.bfloat16)


HALF = BLOCK // 2
ALL = slice(0, BLOCK)
LOW = slice(0, HALF)
HIGH = slice(HALF, BLOCK)


def dot3(a, b, rows, columns):
    count = rows.stop - rows.start
    stacked = dot(jnp.concatenate([a[0][rows], a[1][rows]], axis=0), b[0][:, columns])
    return stacked[:count] + (stacked[count:] + dot(a[0][rows], b[1][:, columns]))


def put(pair, rows, columns, x):
    pair[0][rows, columns], pair[1][rows, columns] = split(x)


def mirror(pair):
    for part in pair:
        part[LOW, HIGH] = part[HIGH, LOW].T


def owner_kernel(me_ref, place_ref, got_ref, left_ref, right_ref, new_left_ref, new_right_ref, coded_ref,
                 prev_ref, new_ref, n_ref, raw_ref, n_parts_ref, q_parts_ref, h_parts_ref, r_parts_ref,
                 staged_ref, got_sem, new_sem, coded_sem):
    slots = range(SLOTS)
    both = [(slot, side) for slot in slots for side in range(2)]

    def fetch(slot, side):
        source = (left_ref, right_ref)[side]
        return pltpu.make_async_copy(source.at[slot], prev_ref.at[slot, side], got_sem.at[slot, side])

    def write(slot, side):
        target = (new_left_ref, new_right_ref)[side]
        return pltpu.make_async_copy(new_ref.at[slot, side], target.at[slot], new_sem.at[slot, side])

    def send(slot):
        last = BLOCK + 128 if slot == SLOTS - 1 else BLOCK
        columns = pl.ds(slot * BLOCK, last)
        return pltpu.make_async_copy(
            staged_ref.at[:, :, columns], coded_ref.at[:, :, columns], coded_sem.at[slot]
        )

    def eye(rows, columns, value):
        shape = (rows.stop - rows.start, columns.stop - columns.start)
        down = lax.broadcasted_iota(jnp.int32, shape, 0) + rows.start
        across = lax.broadcasted_iota(jnp.int32, shape, 1) + columns.start
        return jnp.where(down == across, jnp.float32(value), jnp.float32(0))

    def pair(ref, slot, side):
        return ref.at[slot, side, 0], ref.at[slot, side, 1]

    for slot, side in both:
        fetch(slot, side).start()
    blocks, turneds = [], []
    for slot in slots:
        wanted = me_ref[0] * SLOTS + slot
        used = place_ref[0] == wanted
        for b in range(1, BLOCKS):
            used = used | (place_ref[b] == wanted)
        block = got_ref[:, slot * BLOCK : (slot + 1) * BLOCK]
        block = jnp.where(used, block, jnp.zeros_like(block))
        blocks.append(block)
        turneds.append(block.T)

    norms = {}
    for slot, side in both:
        block, turned = blocks[slot], turneds[slot]
        gram = dot(block, turned) if side == 0 else dot(turned, block)
        fetch(slot, side).wait()
        stat = BETA * prev_ref[slot, side] + gram
        new_ref[slot, side] = stat
        write(slot, side).start()
        damped = stat + eye(ALL, ALL, EPS_DAMP)
        norm = jnp.sqrt(jnp.sum(damped * damped, keepdims=True))
        n = damped * (1.0 / norm)
        n_ref[slot, side] = n
        put(pair(n_parts_ref, slot, side), ALL, ALL, n)
        norms[slot, side] = norm

    steps = [(rows, columns, k, s) for rows, columns in ((ALL, LOW), (HIGH, HIGH)) for k, s in both]
    for rows, columns, slot, side in steps:
        n = n_ref[slot, side, rows, columns]
        n_parts, q_parts = pair(n_parts_ref, slot, side), pair(q_parts_ref, slot, side)
        h_parts = pair(h_parts_ref, slot, side)
        n2 = dot3(n_parts, n_parts, rows, columns)
        put(q_parts, rows, columns, eye(rows, columns, 1.5625) - 2.5 * n + n2)
        put(h_parts, rows, columns, 1.25 * n - n2)
        if columns == LOW:
            mirror(q_parts)
            mirror(h_parts)
    for rows, columns, slot, side in steps:
        q_parts, r_parts = pair(q_parts_ref, slot, side), pair(r_parts_ref, slot, side)
        put(r_parts, rows, columns, dot3(q_parts, q_parts, rows, columns))
        if columns == LOW:
            mirror(r_parts)
    for rows, columns, slot, side in steps:
        product = dot3(pair(h_parts_ref, slot, side), pair(r_parts_ref, slot, side), rows, columns)
        product = eye(rows, columns, 1.5625) - 1.25 * n_ref[slot, side, rows, columns] - product
        product = product * lax.rsqrt(jnp.sqrt(0.25 * norms[slot, side]))
        put(pair(n_parts_ref, slot, side), rows, columns, product)
        if columns == LOW:
            mirror(pair(n_parts_ref, slot, side))
    for columns in (LOW, HIGH):
        for slot in slots:
            high, low = pair(n_parts_ref, slot, 0)
            half = dot(jnp.concatenate([high[...], low[...]], axis=0), blocks[slot][:, columns])
            put(pair(q_parts_ref, slot, 0), ALL, columns, half[:BLOCK] + half[BLOCK:])
    grad_sq = jnp.zeros((1, 1), jnp.float32)
    update_sq = jnp.zeros((1, 1), jnp.float32)
    for slot in slots:
        for columns in (LOW, HIGH):
            raw = dot3(pair(q_parts_ref, slot, 0), pair(n_parts_ref, slot, 1), ALL, columns)
            raw_ref[slot, :, columns] = raw
            update_sq += jnp.sum(raw * raw, keepdims=True)
        wide = blocks[slot].astype(jnp.float32)
        grad_sq += jnp.sum(wide * wide, keepdims=True)

    row_powers = []
    for slot in slots:
        raw = raw_ref[slot]
        largest = jnp.max(jnp.abs(raw), axis=1, keepdims=True)
        power = jnp.ceil(jnp.log2(jnp.maximum(largest, 1e-30)) + 0.001) - 15.0
        coded = jnp.round(raw * jnp.exp2(-power)).astype(jnp.int32)
        for p in range(OWNERS):
            staged_ref[p, :, pl.ds(slot * BLOCK, BLOCK)] = coded[p * LINES : (p + 1) * LINES].astype(jnp.int16)
        row_powers.append(power)
        if slot < SLOTS - 1:
            send(slot).start()

    lane = lax.broadcasted_iota(jnp.int32, (1, 128), 1)
    total = jnp.where(lane < UPDATE_LANE, grad_sq, update_sq)
    exponent = jnp.ceil(jnp.log2(jnp.maximum(total, 1e-30)))
    mantissa = total * jnp.exp2(12.0 - exponent)
    upper = jnp.floor(mantissa)
    lower = jnp.round((mantissa - upper) * 4096.0)
    start = jnp.where(lane < UPDATE_LANE, GRAD_LANE, UPDATE_LANE)
    digits = jnp.where(lane == start, exponent - 12.0, jnp.where(lane == start + 1, upper, lower))
    held = (lane >= GRAD_LANE) & (lane < UPDATE_LANE + 3)
    powers = jnp.where(lane < 64, row_powers[0], row_powers[1])
    powers = jnp.where(held, digits, powers).astype(jnp.int32)
    for p in range(OWNERS):
        staged_ref[p, :, pl.ds(SLOTS * BLOCK, 128)] = powers[p * LINES : (p + 1) * LINES].astype(jnp.int16)
    send(SLOTS - 1).start()
    for slot, side in both:
        write(slot, side).wait()
    for slot in slots:
        send(slot).wait()


def exchange(x, axes):
    return lax.all_to_all(x, axes, split_axis=0, concat_axis=0, tiled=True)


def add_permuted(x, axis, perms):
    return sum([lax.ppermute(x, axis, perm) for perm in perms], x)


def sum_mp(x):
    return add_permuted(x, "mp", [[(d, (d + s) % SHARDS) for d in range(SHARDS)] for s in range(1, 4)])


def shards(gradient, block_owner, prev_left, prev_right):
    shard = jnp.reshape(lax.axis_index("mp"), (1,)).astype(jnp.int32)
    me = jnp.reshape(lax.axis_index(("r", "g")), (1,)).astype(jnp.int32)
    spread_shape = (GROUPS, LINES, PER_SHARD * BLOCK)

    places = pl.pallas_call(
        place_table_kernel,
        out_shape=jax.ShapeDtypeStruct((BLOCKS,), jnp.int32),
        in_specs=[SMEM, SMEM],
        out_specs=SMEM,
        scratch_shapes=[pltpu.SMEM((OWNERS,), jnp.int32)],
        compiler_params=params(4),
        cost_estimate=pl.CostEstimate(flops=1000, bytes_accessed=1000, transcendentals=0),
        name="places",
    )(shard, block_owner)
    pieces = exchange(gradient.reshape(spread_shape), "g")
    routed = pl.pallas_call(
        route_kernel,
        out_shape=jax.ShapeDtypeStruct((OWNERS, LINES, SLOTS * BLOCK), jnp.bfloat16),
        in_specs=[SMEM, WHOLE],
        out_specs=pl.BlockSpec(memory_space=pl.ANY),
        scratch_shapes=[pltpu.SemaphoreType.DMA((GROUPS, PER_SHARD))],
        compiler_params=params(4),
        name="route",
    )(places, pieces)
    got = exchange(routed, ("r", "g")).reshape(BLOCK, SLOTS * BLOCK)

    stat_spec = pl.BlockSpec(memory_space=pl.ANY)
    stat_shape = jax.ShapeDtypeStruct((SLOTS, BLOCK, BLOCK), jnp.float32)
    coded_shape = (OWNERS, LINES, SLOTS * BLOCK + 128)
    wide = pltpu.VMEM((SLOTS, 2, BLOCK, BLOCK), jnp.float32)
    parts = pltpu.VMEM((SLOTS, 2, 2, BLOCK, BLOCK), jnp.bfloat16)
    new_left, new_right, coded = pl.pallas_call(
        owner_kernel,
        out_shape=[stat_shape, stat_shape, jax.ShapeDtypeStruct(coded_shape, jnp.int16)],
        in_specs=[SMEM, SMEM, WHOLE, stat_spec, stat_spec],
        out_specs=[stat_spec, stat_spec, stat_spec],
        scratch_shapes=[
            wide,
            wide,
            wide,
            pltpu.VMEM((SLOTS, BLOCK, BLOCK), jnp.float32),
            parts,
            parts,
            parts,
            parts,
            pltpu.VMEM(coded_shape, jnp.int16),
            pltpu.SemaphoreType.DMA((SLOTS, 2)),
            pltpu.SemaphoreType.DMA((SLOTS, 2)),
            pltpu.SemaphoreType.DMA((SLOTS,)),
        ],
        compiler_params=params(50),
        cost_estimate=pl.CostEstimate(
            flops=50 * 2 * BLOCK**3, bytes_accessed=12 * MIB, transcendentals=0
        ),
        name="owner",
    )(me, places, got, prev_left[0, 0], prev_right[0, 0])

    returned = exchange(coded, ("r", "g"))
    back, sums = pl.pallas_call(
        collect_kernel,
        out_shape=[
            jax.ShapeDtypeStruct((GROUPS, LINES, PER_SHARD * BLOCK + 128), jnp.int16),
            jax.ShapeDtypeStruct((LINES, 128), jnp.float32),
        ],
        in_specs=[SMEM, WHOLE],
        out_specs=[WHOLE, WHOLE],
        compiler_params=params(8),
        name="collect",
    )(places, returned)
    back = exchange(back, "g")
    update_out = pl.pallas_call(
        finish_kernel,
        out_shape=jax.ShapeDtypeStruct(spread_shape, jnp.bfloat16),
        in_specs=[WHOLE, WHOLE],
        out_specs=WHOLE,
        compiler_params=params(8),
        name="finish",
    )(sum_mp(sums), back).reshape(gradient.shape)
    return (update_out, new_left[None, None], new_right[None, None])


def solution(mesh):
    fine = Mesh(mesh.devices.reshape(GROUPS, MEMBERS, SHARDS), ("g", "r", "mp"))
    grad_spec = P(("g", "r"), "mp")
    stat_spec = P("mp", ("g", "r"), None, None, None)
    return jax.shard_map(
        shards,
        mesh=fine,
        in_specs=(grad_spec, P(), stat_spec, stat_spec),
        out_specs=(grad_spec, stat_spec, stat_spec),
        check_vma=False,
    )
```

```python
import jax
import jax.numpy as jnp
from jax import lax
from jax.experimental import pallas as pl
from jax.experimental.pallas import tpu as pltpu
from jax.sharding import Mesh
from jax.sharding import PartitionSpec as P

EPS_DAMP = 1.0
BETA = 0.95
BLOCK = 512
SHARDS = 4
GROUPS = 4
MEMBERS = 16
PER_SHARD = 8
BLOCKS = GROUPS * PER_SHARD
OWNERS = 64
SLOTS = 2
LINES = 8
CELLS = 2048 * 16384
MIB = 1024 * 1024
GRAD_LANE, UPDATE_LANE = 32, 36

WHOLE = pl.BlockSpec(memory_space=pltpu.VMEM)
SMEM = pl.BlockSpec(memory_space=pltpu.SMEM)


def params(mib):
    return pltpu.CompilerParams(vmem_limit_bytes=mib * MIB)


def place_table_kernel(shard_ref, owner_ref, place_ref, count_ref):
    base = shard_ref[0] * PER_SHARD

    def clear(o, _):
        count_ref[o] = 0
        return 0

    lax.fori_loop(0, OWNERS, clear, 0, unroll=8)
    for b in range(BLOCKS):
        owner = owner_ref[b // PER_SHARD, base + b % PER_SHARD]
        slot = count_ref[owner]
        count_ref[owner] = slot + 1
        place_ref[b] = (lax.rem(owner, MEMBERS) * GROUPS + owner // MEMBERS) * SLOTS + slot


def route_kernel(place_ref, in_ref, out_ref, sem):
    copies = []
    for row in range(GROUPS):
        for j in range(PER_SHARD):
            place = place_ref[row * PER_SHARD + j]
            columns = pl.ds(pl.multiple_of(lax.rem(place, SLOTS) * BLOCK, BLOCK), BLOCK)
            copy = pltpu.make_async_copy(
                in_ref.at[row, :, pl.ds(j * BLOCK, BLOCK)],
                out_ref.at[place // SLOTS, :, columns],
                sem.at[row, j],
            )
            copy.start()
            copies.append(copy)
    for copy in copies:
        copy.wait()


def collect_kernel(place_ref, in_ref, out_ref):
    lane = lax.broadcasted_iota(jnp.int32, (LINES, 128), 1)
    tile = pl.ds(SLOTS * BLOCK, 128)
    for row in range(GROUPS):
        powers = jnp.zeros((LINES, 128), jnp.int32)
        for j in range(PER_SHARD):
            place = place_ref[row * PER_SHARD + j]
            position, slot = place // SLOTS, lax.rem(place, SLOTS)
            columns = pl.ds(pl.multiple_of(slot * BLOCK, BLOCK), BLOCK)
            out_ref[row, :, pl.ds(j * BLOCK, BLOCK)] = in_ref[position, :, columns]
            powers = jnp.where(lane == j + 64 * slot, in_ref[position, :, tile].astype(jnp.int32), powers)
        out_ref[row, :, pl.ds(PER_SHARD * BLOCK, 128)] = powers.astype(jnp.int16)


def add_kernel(in_ref, sums_ref):
    lane = lax.broadcasted_iota(jnp.int32, (LINES, 128), 1)
    line = lax.broadcasted_iota(jnp.int32, (LINES, 128), 0)
    tile = pl.ds(SLOTS * BLOCK, 128)
    sums = jnp.zeros((LINES, 128), jnp.float32)
    for first in range(0, OWNERS, LINES):
        digits = jnp.zeros((LINES, 128), jnp.int32)
        for k in range(LINES):
            digits = jnp.where(line == k, in_ref[first + k, :, tile].astype(jnp.int32), digits)
        digits = digits.astype(jnp.float32)
        value = pltpu.roll(digits, 127, 1) + pltpu.roll(digits, 126, 1) * (1.0 / 4096.0)
        here = (lane == GRAD_LANE) | (lane == UPDATE_LANE)
        sums += jnp.where(here, value * jnp.exp2(jnp.where(here, digits, 0.0)), 0.0)
    sums_ref[...] = sums


def finish_kernel(sums_ref, in_ref, out_ref):
    totals = jnp.sum(sums_ref[...], axis=0, keepdims=True)
    grad_total = totals[:, GRAD_LANE : GRAD_LANE + 1]
    update_total = totals[:, UPDATE_LANE : UPDATE_LANE + 1]
    graft = jnp.sqrt(grad_total / CELLS) * lax.rsqrt(update_total / CELLS + 1e-06)
    for chunk in range(GROUPS):
        powers = in_ref[chunk, :, pl.ds(PER_SHARD * BLOCK, 128)].astype(jnp.int32).astype(jnp.float32)
        steps = jnp.exp2(powers + pltpu.roll(powers, 64, 1)) * graft
        for j in range(PER_SHARD):
            columns = pl.ds(j * BLOCK, BLOCK)
            coded = in_ref[chunk, :, columns].astype(jnp.int32).astype(jnp.float32)
            out_ref[chunk, :, columns] = (coded * steps[:, j : j + 1]).astype(jnp.bfloat16)


def dot(a, b):
    return jnp.dot(a, b, preferred_element_type=jnp.float32)


def split(x):
    high = x.astype(jnp.bfloat16)
    return high, (x - high.astype(jnp.float32)).astype(jnp.bfloat16)


HALF = BLOCK // 2
ALL = slice(0, BLOCK)
LOW = slice(0, HALF)
HIGH = slice(HALF, BLOCK)


def dot3(a, b, rows, columns):
    count = rows.stop - rows.start
    stacked = dot(jnp.concatenate([a[0][rows], a[1][rows]], axis=0), b[0][:, columns])
    return stacked[:count] + (stacked[count:] + dot(a[0][rows], b[1][:, columns]))


def put(pair, rows, columns, x):
    pair[0][rows, columns], pair[1][rows, columns] = split(x)


def mirror(pair):
    for part in pair:
        part[LOW, HIGH] = part[HIGH, LOW].T


def owner_kernel(me_ref, place_ref, got_ref, left_ref, right_ref, new_left_ref, new_right_ref, coded_ref,
                 prev_ref, new_ref, n_ref, raw_ref, n_parts_ref, q_parts_ref, h_parts_ref, r_parts_ref,
                 staged_ref, got_sem, new_sem, coded_sem):
    slots = range(SLOTS)
    both = [(slot, side) for slot in slots for side in range(2)]

    def fetch(slot, side):
        source = (left_ref, right_ref)[side]
        return pltpu.make_async_copy(source.at[slot], prev_ref.at[slot, side], got_sem.at[slot, side])

    def write(slot, side):
        target = (new_left_ref, new_right_ref)[side]
        return pltpu.make_async_copy(new_ref.at[slot, side], target.at[slot], new_sem.at[slot, side])

    def send(slot):
        last = BLOCK + 128 if slot == SLOTS - 1 else BLOCK
        columns = pl.ds(slot * BLOCK, last)
        return pltpu.make_async_copy(
            staged_ref.at[:, :, columns], coded_ref.at[:, :, columns], coded_sem.at[slot]
        )

    def eye(rows, columns, value):
        shape = (rows.stop - rows.start, columns.stop - columns.start)
        down = lax.broadcasted_iota(jnp.int32, shape, 0) + rows.start
        across = lax.broadcasted_iota(jnp.int32, shape, 1) + columns.start
        return jnp.where(down == across, jnp.float32(value), jnp.float32(0))

    def pair(ref, slot, side):
        return ref.at[slot, side, 0], ref.at[slot, side, 1]

    for slot, side in both:
        fetch(slot, side).start()
    blocks, turneds = [], []
    for slot in slots:
        wanted = me_ref[0] * SLOTS + slot
        used = place_ref[0] == wanted
        for b in range(1, BLOCKS):
            used = used | (place_ref[b] == wanted)
        block = got_ref[:, slot * BLOCK : (slot + 1) * BLOCK]
        block = jnp.where(used, block, jnp.zeros_like(block))
        blocks.append(block)
        turneds.append(block.T)

    norms = {}
    for slot, side in both:
        block, turned = blocks[slot], turneds[slot]
        gram = dot(block, turned) if side == 0 else dot(turned, block)
        fetch(slot, side).wait()
        stat = BETA * prev_ref[slot, side] + gram
        new_ref[slot, side] = stat
        write(slot, side).start()
        damped = stat + eye(ALL, ALL, EPS_DAMP)
        norm = jnp.sqrt(jnp.sum(damped * damped, keepdims=True))
        n = damped * (1.0 / norm)
        n_ref[slot, side] = n
        put(pair(n_parts_ref, slot, side), ALL, ALL, n)
        norms[slot, side] = norm

    steps = [(rows, columns, k, s) for rows, columns in ((ALL, LOW), (HIGH, HIGH)) for k, s in both]
    for rows, columns, slot, side in steps:
        n = n_ref[slot, side, rows, columns]
        n_parts, q_parts = pair(n_parts_ref, slot, side), pair(q_parts_ref, slot, side)
        h_parts = pair(h_parts_ref, slot, side)
        n2 = dot3(n_parts, n_parts, rows, columns)
        put(q_parts, rows, columns, eye(rows, columns, 1.5625) - 2.5 * n + n2)
        put(h_parts, rows, columns, 1.25 * n - n2)
        if columns == LOW:
            mirror(q_parts)
            mirror(h_parts)
    for rows, columns, slot, side in steps:
        q_parts, r_parts = pair(q_parts_ref, slot, side), pair(r_parts_ref, slot, side)
        put(r_parts, rows, columns, dot3(q_parts, q_parts, rows, columns))
        if columns == LOW:
            mirror(r_parts)
    for rows, columns, slot, side in steps:
        product = dot3(pair(h_parts_ref, slot, side), pair(r_parts_ref, slot, side), rows, columns)
        product = eye(rows, columns, 1.5625) - 1.25 * n_ref[slot, side, rows, columns] - product
        product = product * lax.rsqrt(jnp.sqrt(0.25 * norms[slot, side]))
        put(pair(n_parts_ref, slot, side), rows, columns, product)
        if columns == LOW:
            mirror(pair(n_parts_ref, slot, side))
    for columns in (LOW, HIGH):
        for slot in slots:
            high, low = pair(n_parts_ref, slot, 0)
            half = dot(jnp.concatenate([high[...], low[...]], axis=0), blocks[slot][:, columns])
            put(pair(q_parts_ref, slot, 0), ALL, columns, half[:BLOCK] + half[BLOCK:])
    grad_sq = jnp.zeros((1, 1), jnp.float32)
    update_sq = jnp.zeros((1, 1), jnp.float32)
    for slot in slots:
        for columns in (LOW, HIGH):
            raw = dot3(pair(q_parts_ref, slot, 0), pair(n_parts_ref, slot, 1), ALL, columns)
            raw_ref[slot, :, columns] = raw
            update_sq += jnp.sum(raw * raw, keepdims=True)
        wide = blocks[slot].astype(jnp.float32)
        grad_sq += jnp.sum(wide * wide, keepdims=True)

    row_powers = []
    for slot in slots:
        raw = raw_ref[slot]
        largest = jnp.max(jnp.abs(raw), axis=1, keepdims=True)
        power = jnp.ceil(jnp.log2(jnp.maximum(largest, 1e-30)) + 0.001) - 15.0
        coded = jnp.round(raw * jnp.exp2(-power)).astype(jnp.int32)
        for p in range(OWNERS):
            staged_ref[p, :, pl.ds(slot * BLOCK, BLOCK)] = coded[p * LINES : (p + 1) * LINES].astype(jnp.int16)
        row_powers.append(power)
        if slot < SLOTS - 1:
            send(slot).start()

    lane = lax.broadcasted_iota(jnp.int32, (1, 128), 1)
    total = jnp.where(lane < UPDATE_LANE, grad_sq, update_sq)
    exponent = jnp.ceil(jnp.log2(jnp.maximum(total, 1e-30)))
    mantissa = total * jnp.exp2(12.0 - exponent)
    upper = jnp.floor(mantissa)
    lower = jnp.round((mantissa - upper) * 4096.0)
    start = jnp.where(lane < UPDATE_LANE, GRAD_LANE, UPDATE_LANE)
    digits = jnp.where(lane == start, exponent - 12.0, jnp.where(lane == start + 1, upper, lower))
    held = (lane >= GRAD_LANE) & (lane < UPDATE_LANE + 3)
    powers = jnp.where(lane < 64, row_powers[0], row_powers[1])
    powers = jnp.where(held, digits, powers).astype(jnp.int32)
    for p in range(OWNERS):
        staged_ref[p, :, pl.ds(SLOTS * BLOCK, 128)] = powers[p * LINES : (p + 1) * LINES].astype(jnp.int16)
    send(SLOTS - 1).start()
    for slot, side in both:
        write(slot, side).wait()
    for slot in slots:
        send(slot).wait()


def exchange(x, axes):
    return lax.all_to_all(x, axes, split_axis=0, concat_axis=0, tiled=True)


def add_permuted(x, axis, perms):
    return sum([lax.ppermute(x, axis, perm) for perm in perms], x)


def sum_mp(x):
    return add_permuted(x, "mp", [[(d, (d + s) % SHARDS) for d in range(SHARDS)] for s in range(1, 4)])


def shards(gradient, block_owner, prev_left, prev_right):
    shard = jnp.reshape(lax.axis_index("mp"), (1,)).astype(jnp.int32)
    me = jnp.reshape(lax.axis_index(("r", "g")), (1,)).astype(jnp.int32)
    spread_shape = (GROUPS, LINES, PER_SHARD * BLOCK)

    places = pl.pallas_call(
        place_table_kernel,
        out_shape=jax.ShapeDtypeStruct((BLOCKS,), jnp.int32),
        in_specs=[SMEM, SMEM],
        out_specs=SMEM,
        scratch_shapes=[pltpu.SMEM((OWNERS,), jnp.int32)],
        compiler_params=params(4),
        cost_estimate=pl.CostEstimate(flops=1000, bytes_accessed=1000, transcendentals=0),
        name="places",
    )(shard, block_owner)
    pieces = exchange(gradient.reshape(spread_shape), "g")
    routed = pl.pallas_call(
        route_kernel,
        out_shape=jax.ShapeDtypeStruct((OWNERS, LINES, SLOTS * BLOCK), jnp.bfloat16),
        in_specs=[SMEM, WHOLE],
        out_specs=pl.BlockSpec(memory_space=pl.ANY),
        scratch_shapes=[pltpu.SemaphoreType.DMA((GROUPS, PER_SHARD))],
        compiler_params=params(4),
        name="route",
    )(places, pieces)
    got = exchange(routed, ("r", "g")).reshape(BLOCK, SLOTS * BLOCK)

    stat_spec = pl.BlockSpec(memory_space=pl.ANY)
    stat_shape = jax.ShapeDtypeStruct((SLOTS, BLOCK, BLOCK), jnp.float32)
    coded_shape = (OWNERS, LINES, SLOTS * BLOCK + 128)
    wide = pltpu.VMEM((SLOTS, 2, BLOCK, BLOCK), jnp.float32)
    parts = pltpu.VMEM((SLOTS, 2, 2, BLOCK, BLOCK), jnp.bfloat16)
    new_left, new_right, coded = pl.pallas_call(
        owner_kernel,
        out_shape=[stat_shape, stat_shape, jax.ShapeDtypeStruct(coded_shape, jnp.int16)],
        in_specs=[SMEM, SMEM, WHOLE, stat_spec, stat_spec],
        out_specs=[stat_spec, stat_spec, stat_spec],
        scratch_shapes=[
            wide,
            wide,
            wide,
            pltpu.VMEM((SLOTS, BLOCK, BLOCK), jnp.float32),
            parts,
            parts,
            parts,
            parts,
            pltpu.VMEM(coded_shape, jnp.int16),
            pltpu.SemaphoreType.DMA((SLOTS, 2)),
            pltpu.SemaphoreType.DMA((SLOTS, 2)),
            pltpu.SemaphoreType.DMA((SLOTS,)),
        ],
        compiler_params=params(50),
        cost_estimate=pl.CostEstimate(
            flops=50 * 2 * BLOCK**3, bytes_accessed=12 * MIB, transcendentals=0
        ),
        name="owner",
    )(me, places, got, prev_left[0, 0], prev_right[0, 0])

    returned = exchange(coded, ("r", "g"))
    sums = pl.pallas_call(
        add_kernel,
        out_shape=jax.ShapeDtypeStruct((LINES, 128), jnp.float32),
        in_specs=[WHOLE],
        out_specs=WHOLE,
        compiler_params=params(8),
        name="add",
    )(returned)
    sums, returned = lax.optimization_barrier((sums, returned))
    back = pl.pallas_call(
        collect_kernel,
        out_shape=jax.ShapeDtypeStruct((GROUPS, LINES, PER_SHARD * BLOCK + 128), jnp.int16),
        in_specs=[SMEM, WHOLE],
        out_specs=WHOLE,
        compiler_params=params(8),
        name="collect",
    )(places, returned)
    back = exchange(back, "g")
    update_out = pl.pallas_call(
        finish_kernel,
        out_shape=jax.ShapeDtypeStruct(spread_shape, jnp.bfloat16),
        in_specs=[WHOLE, WHOLE],
        out_specs=WHOLE,
        compiler_params=params(8),
        name="finish",
    )(sum_mp(sums), back).reshape(gradient.shape)
    return (update_out, new_left[None, None], new_right[None, None])


def solution(mesh):
    fine = Mesh(mesh.devices.reshape(GROUPS, MEMBERS, SHARDS), ("g", "r", "mp"))
    grad_spec = P(("g", "r"), "mp")
    stat_spec = P("mp", ("g", "r"), None, None, None)
    return jax.shard_map(
        shards,
        mesh=fine,
        in_specs=(grad_spec, P(), stat_spec, stat_spec),
        out_specs=(grad_spec, stat_spec, stat_spec),
        check_vma=False,
    )
```

```python
import jax
import jax.numpy as jnp
from jax import lax
from jax.experimental import pallas as pl
from jax.experimental.pallas import tpu as pltpu
from jax.sharding import Mesh
from jax.sharding import PartitionSpec as P

EPS_DAMP = 1.0
BETA = 0.95
BLOCK = 512
SHARDS = 4
GROUPS = 4
MEMBERS = 16
PER_SHARD = 8
BLOCKS = GROUPS * PER_SHARD
OWNERS = 64
SLOTS = 2
LINES = 8
CELLS = 2048 * 16384
MIB = 1024 * 1024
GRAD_LANE, UPDATE_LANE = 32, 36

WHOLE = pl.BlockSpec(memory_space=pltpu.VMEM)
SMEM = pl.BlockSpec(memory_space=pltpu.SMEM)


def params(mib):
    return pltpu.CompilerParams(vmem_limit_bytes=mib * MIB)


def place_table_kernel(shard_ref, owner_ref, place_ref, count_ref):
    base = shard_ref[0] * PER_SHARD

    def clear(o, _):
        count_ref[o] = 0
        return 0

    lax.fori_loop(0, OWNERS, clear, 0, unroll=8)
    for b in range(BLOCKS):
        owner = owner_ref[b // PER_SHARD, base + b % PER_SHARD]
        slot = count_ref[owner]
        count_ref[owner] = slot + 1
        place_ref[b] = (lax.rem(owner, MEMBERS) * GROUPS + owner // MEMBERS) * SLOTS + slot


def route_kernel(place_ref, in_ref, out_ref, sem):
    copies = []
    for row in range(GROUPS):
        for j in range(PER_SHARD):
            place = place_ref[row * PER_SHARD + j]
            columns = pl.ds(pl.multiple_of(lax.rem(place, SLOTS) * BLOCK, BLOCK), BLOCK)
            copy = pltpu.make_async_copy(
                in_ref.at[row, :, pl.ds(j * BLOCK, BLOCK)],
                out_ref.at[place // SLOTS, :, columns],
                sem.at[row, j],
            )
            copy.start()
            copies.append(copy)
    for copy in copies:
        copy.wait()


def collect_kernel(group_ref, place_ref, in_ref, *refs):
    out_refs, sums_ref = refs[:GROUPS], refs[GROUPS]
    lane = lax.broadcasted_iota(jnp.int32, (LINES, 128), 1)
    line = lax.broadcasted_iota(jnp.int32, (LINES, 128), 0)
    tile = pl.ds(SLOTS * BLOCK, 128)
    for shift, out_ref in enumerate(out_refs):
        row = lax.rem(group_ref[0] + shift, GROUPS)
        powers = jnp.zeros((LINES, 128), jnp.int32)
        for j in range(PER_SHARD):
            place = place_ref[row * PER_SHARD + j]
            position, slot = place // SLOTS, lax.rem(place, SLOTS)
            columns = pl.ds(pl.multiple_of(slot * BLOCK, BLOCK), BLOCK)
            out_ref[:, pl.ds(j * BLOCK, BLOCK)] = in_ref[position, :, columns]
            powers = jnp.where(lane == j + 64 * slot, in_ref[position, :, tile].astype(jnp.int32), powers)
        out_ref[:, pl.ds(PER_SHARD * BLOCK, 128)] = powers.astype(jnp.int16)
    sums = jnp.zeros((LINES, 128), jnp.float32)
    for first in range(0, OWNERS, LINES):
        digits = jnp.zeros((LINES, 128), jnp.int32)
        for k in range(LINES):
            digits = jnp.where(line == k, in_ref[first + k, :, tile].astype(jnp.int32), digits)
        digits = digits.astype(jnp.float32)
        value = pltpu.roll(digits, 127, 1) + pltpu.roll(digits, 126, 1) * (1.0 / 4096.0)
        here = (lane == GRAD_LANE) | (lane == UPDATE_LANE)
        sums += jnp.where(here, value * jnp.exp2(jnp.where(here, digits, 0.0)), 0.0)
    sums_ref[...] = sums


def finish_kernel(group_ref, sums_ref, *refs):
    in_refs, out_ref = refs[:GROUPS], refs[GROUPS]
    totals = jnp.sum(sums_ref[...], axis=0, keepdims=True)
    grad_total = totals[:, GRAD_LANE : GRAD_LANE + 1]
    update_total = totals[:, UPDATE_LANE : UPDATE_LANE + 1]
    graft = jnp.sqrt(grad_total / CELLS) * lax.rsqrt(update_total / CELLS + 1e-06)
    for shift, in_ref in enumerate(in_refs):
        chunk = lax.rem(group_ref[0] + GROUPS - shift, GROUPS)
        powers = in_ref[:, pl.ds(PER_SHARD * BLOCK, 128)].astype(jnp.int32).astype(jnp.float32)
        steps = jnp.exp2(powers + pltpu.roll(powers, 64, 1)) * graft
        for j in range(PER_SHARD):
            columns = pl.ds(j * BLOCK, BLOCK)
            coded = in_ref[:, columns].astype(jnp.int32).astype(jnp.float32)
            out_ref[chunk, :, columns] = (coded * steps[:, j : j + 1]).astype(jnp.bfloat16)


def dot(a, b):
    return jnp.dot(a, b, preferred_element_type=jnp.float32)


def split(x):
    high = x.astype(jnp.bfloat16)
    return high, (x - high.astype(jnp.float32)).astype(jnp.bfloat16)


HALF = BLOCK // 2
ALL = slice(0, BLOCK)
LOW = slice(0, HALF)
HIGH = slice(HALF, BLOCK)


def dot3(a, b, rows, columns):
    count = rows.stop - rows.start
    stacked = dot(jnp.concatenate([a[0][rows], a[1][rows]], axis=0), b[0][:, columns])
    return stacked[:count] + (stacked[count:] + dot(a[0][rows], b[1][:, columns]))


def put(pair, rows, columns, x):
    pair[0][rows, columns], pair[1][rows, columns] = split(x)


def mirror(pair):
    for part in pair:
        part[LOW, HIGH] = part[HIGH, LOW].T


def owner_kernel(me_ref, place_ref, got_ref, left_ref, right_ref, new_left_ref, new_right_ref, coded_ref,
                 prev_ref, new_ref, n_ref, raw_ref, n_parts_ref, q_parts_ref, h_parts_ref, r_parts_ref,
                 staged_ref, got_sem, new_sem, coded_sem):
    slots = range(SLOTS)
    both = [(slot, side) for slot in slots for side in range(2)]

    def fetch(slot, side):
        source = (left_ref, right_ref)[side]
        return pltpu.make_async_copy(source.at[slot], prev_ref.at[slot, side], got_sem.at[slot, side])

    def write(slot, side):
        target = (new_left_ref, new_right_ref)[side]
        return pltpu.make_async_copy(new_ref.at[slot, side], target.at[slot], new_sem.at[slot, side])

    def send(slot):
        last = BLOCK + 128 if slot == SLOTS - 1 else BLOCK
        columns = pl.ds(slot * BLOCK, last)
        return pltpu.make_async_copy(
            staged_ref.at[:, :, columns], coded_ref.at[:, :, columns], coded_sem.at[slot]
        )

    def eye(rows, columns, value):
        shape = (rows.stop - rows.start, columns.stop - columns.start)
        down = lax.broadcasted_iota(jnp.int32, shape, 0) + rows.start
        across = lax.broadcasted_iota(jnp.int32, shape, 1) + columns.start
        return jnp.where(down == across, jnp.float32(value), jnp.float32(0))

    def pair(ref, slot, side):
        return ref.at[slot, side, 0], ref.at[slot, side, 1]

    for slot, side in both:
        fetch(slot, side).start()
    blocks, turneds = [], []
    for slot in slots:
        wanted = me_ref[0] * SLOTS + slot
        used = place_ref[0] == wanted
        for b in range(1, BLOCKS):
            used = used | (place_ref[b] == wanted)
        block = got_ref[:, slot * BLOCK : (slot + 1) * BLOCK]
        block = jnp.where(used, block, jnp.zeros_like(block))
        blocks.append(block)
        turneds.append(block.T)

    norms = {}
    for slot, side in both:
        block, turned = blocks[slot], turneds[slot]
        gram = dot(block, turned) if side == 0 else dot(turned, block)
        fetch(slot, side).wait()
        stat = BETA * prev_ref[slot, side] + gram
        new_ref[slot, side] = stat
        write(slot, side).start()
        damped = stat + eye(ALL, ALL, EPS_DAMP)
        norm = jnp.sqrt(jnp.sum(damped * damped, keepdims=True))
        n = damped * (1.0 / norm)
        n_ref[slot, side] = n
        put(pair(n_parts_ref, slot, side), ALL, ALL, n)
        norms[slot, side] = norm

    steps = [(rows, columns, k, s) for rows, columns in ((ALL, LOW), (HIGH, HIGH)) for k, s in both]
    for rows, columns, slot, side in steps:
        n = n_ref[slot, side, rows, columns]
        n_parts, q_parts = pair(n_parts_ref, slot, side), pair(q_parts_ref, slot, side)
        h_parts = pair(h_parts_ref, slot, side)
        n2 = dot3(n_parts, n_parts, rows, columns)
        put(q_parts, rows, columns, eye(rows, columns, 1.5625) - 2.5 * n + n2)
        put(h_parts, rows, columns, 1.25 * n - n2)
        if columns == LOW:
            mirror(q_parts)
            mirror(h_parts)
    for rows, columns, slot, side in steps:
        q_parts, r_parts = pair(q_parts_ref, slot, side), pair(r_parts_ref, slot, side)
        put(r_parts, rows, columns, dot3(q_parts, q_parts, rows, columns))
        if columns == LOW:
            mirror(r_parts)
    for rows, columns, slot, side in steps:
        product = dot3(pair(h_parts_ref, slot, side), pair(r_parts_ref, slot, side), rows, columns)
        product = eye(rows, columns, 1.5625) - 1.25 * n_ref[slot, side, rows, columns] - product
        product = product * lax.rsqrt(jnp.sqrt(0.25 * norms[slot, side]))
        put(pair(n_parts_ref, slot, side), rows, columns, product)
        if columns == LOW:
            mirror(pair(n_parts_ref, slot, side))
    for columns in (LOW, HIGH):
        for slot in slots:
            high, low = pair(n_parts_ref, slot, 0)
            half = dot(jnp.concatenate([high[...], low[...]], axis=0), blocks[slot][:, columns])
            put(pair(q_parts_ref, slot, 0), ALL, columns, half[:BLOCK] + half[BLOCK:])
    grad_sq = jnp.zeros((1, 1), jnp.float32)
    update_sq = jnp.zeros((1, 1), jnp.float32)
    for slot in slots:
        for columns in (LOW, HIGH):
            raw = dot3(pair(q_parts_ref, slot, 0), pair(n_parts_ref, slot, 1), ALL, columns)
            raw_ref[slot, :, columns] = raw
            update_sq += jnp.sum(raw * raw, keepdims=True)
        wide = blocks[slot].astype(jnp.float32)
        grad_sq += jnp.sum(wide * wide, keepdims=True)

    row_powers = []
    for slot in slots:
        raw = raw_ref[slot]
        largest = jnp.max(jnp.abs(raw), axis=1, keepdims=True)
        power = jnp.ceil(jnp.log2(jnp.maximum(largest, 1e-30)) + 0.001) - 15.0
        coded = jnp.round(raw * jnp.exp2(-power)).astype(jnp.int32)
        for p in range(OWNERS):
            staged_ref[p, :, pl.ds(slot * BLOCK, BLOCK)] = coded[p * LINES : (p + 1) * LINES].astype(jnp.int16)
        row_powers.append(power)
        if slot < SLOTS - 1:
            send(slot).start()

    lane = lax.broadcasted_iota(jnp.int32, (1, 128), 1)
    total = jnp.where(lane < UPDATE_LANE, grad_sq, update_sq)
    exponent = jnp.ceil(jnp.log2(jnp.maximum(total, 1e-30)))
    mantissa = total * jnp.exp2(12.0 - exponent)
    upper = jnp.floor(mantissa)
    lower = jnp.round((mantissa - upper) * 4096.0)
    start = jnp.where(lane < UPDATE_LANE, GRAD_LANE, UPDATE_LANE)
    digits = jnp.where(lane == start, exponent - 12.0, jnp.where(lane == start + 1, upper, lower))
    held = (lane >= GRAD_LANE) & (lane < UPDATE_LANE + 3)
    powers = jnp.where(lane < 64, row_powers[0], row_powers[1])
    powers = jnp.where(held, digits, powers).astype(jnp.int32)
    for p in range(OWNERS):
        staged_ref[p, :, pl.ds(SLOTS * BLOCK, 128)] = powers[p * LINES : (p + 1) * LINES].astype(jnp.int16)
    send(SLOTS - 1).start()
    for slot, side in both:
        write(slot, side).wait()
    for slot in slots:
        send(slot).wait()


def exchange(x, axes):
    return lax.all_to_all(x, axes, split_axis=0, concat_axis=0, tiled=True)


def add_permuted(x, axis, perms):
    return sum([lax.ppermute(x, axis, perm) for perm in perms], x)


def sum_mp(x):
    return add_permuted(x, "mp", [[(d, (d + s) % SHARDS) for d in range(SHARDS)] for s in range(1, 4)])


def shards(gradient, block_owner, prev_left, prev_right):
    shard = jnp.reshape(lax.axis_index("mp"), (1,)).astype(jnp.int32)
    me = jnp.reshape(lax.axis_index(("r", "g")), (1,)).astype(jnp.int32)
    spread_shape = (GROUPS, LINES, PER_SHARD * BLOCK)

    places = pl.pallas_call(
        place_table_kernel,
        out_shape=jax.ShapeDtypeStruct((BLOCKS,), jnp.int32),
        in_specs=[SMEM, SMEM],
        out_specs=SMEM,
        scratch_shapes=[pltpu.SMEM((OWNERS,), jnp.int32)],
        compiler_params=params(4),
        cost_estimate=pl.CostEstimate(flops=1000, bytes_accessed=1000, transcendentals=0),
        name="places",
    )(shard, block_owner)
    pieces = exchange(gradient.reshape(spread_shape), "g")
    routed = pl.pallas_call(
        route_kernel,
        out_shape=jax.ShapeDtypeStruct((OWNERS, LINES, SLOTS * BLOCK), jnp.bfloat16),
        in_specs=[SMEM, WHOLE],
        out_specs=pl.BlockSpec(memory_space=pl.ANY),
        scratch_shapes=[pltpu.SemaphoreType.DMA((GROUPS, PER_SHARD))],
        compiler_params=params(4),
        name="route",
    )(places, pieces)
    got = exchange(routed, ("r", "g")).reshape(BLOCK, SLOTS * BLOCK)

    stat_spec = pl.BlockSpec(memory_space=pl.ANY)
    stat_shape = jax.ShapeDtypeStruct((SLOTS, BLOCK, BLOCK), jnp.float32)
    coded_shape = (OWNERS, LINES, SLOTS * BLOCK + 128)
    wide = pltpu.VMEM((SLOTS, 2, BLOCK, BLOCK), jnp.float32)
    parts = pltpu.VMEM((SLOTS, 2, 2, BLOCK, BLOCK), jnp.bfloat16)
    new_left, new_right, coded = pl.pallas_call(
        owner_kernel,
        out_shape=[stat_shape, stat_shape, jax.ShapeDtypeStruct(coded_shape, jnp.int16)],
        in_specs=[SMEM, SMEM, WHOLE, stat_spec, stat_spec],
        out_specs=[stat_spec, stat_spec, stat_spec],
        scratch_shapes=[
            wide,
            wide,
            wide,
            pltpu.VMEM((SLOTS, BLOCK, BLOCK), jnp.float32),
            parts,
            parts,
            parts,
            parts,
            pltpu.VMEM(coded_shape, jnp.int16),
            pltpu.SemaphoreType.DMA((SLOTS, 2)),
            pltpu.SemaphoreType.DMA((SLOTS, 2)),
            pltpu.SemaphoreType.DMA((SLOTS,)),
        ],
        compiler_params=params(50),
        cost_estimate=pl.CostEstimate(
            flops=50 * 2 * BLOCK**3, bytes_accessed=12 * MIB, transcendentals=0
        ),
        name="owner",
    )(me, places, got, prev_left[0, 0], prev_right[0, 0])

    returned = exchange(coded, ("r", "g"))
    group = jnp.reshape(lax.axis_index("g"), (1,)).astype(jnp.int32)
    *back, sums = pl.pallas_call(
        collect_kernel,
        out_shape=[jax.ShapeDtypeStruct((LINES, PER_SHARD * BLOCK + 128), jnp.int16)] * GROUPS
        + [jax.ShapeDtypeStruct((LINES, 128), jnp.float32)],
        in_specs=[SMEM, SMEM, WHOLE],
        out_specs=[WHOLE] * (GROUPS + 1),
        compiler_params=params(8),
        name="collect",
    )(group, places, returned)
    for shift in range(1, GROUPS):
        back[shift] = lax.ppermute(back[shift], "g", [(d, (d + shift) % GROUPS) for d in range(GROUPS)])
    update_out = pl.pallas_call(
        finish_kernel,
        out_shape=jax.ShapeDtypeStruct(spread_shape, jnp.bfloat16),
        in_specs=[SMEM] + [WHOLE] * (GROUPS + 1),
        out_specs=WHOLE,
        compiler_params=params(8),
        name="finish",
    )(group, sum_mp(sums), *back).reshape(gradient.shape)
    return (update_out, new_left[None, None], new_right[None, None])


def solution(mesh):
    fine = Mesh(mesh.devices.reshape(GROUPS, MEMBERS, SHARDS), ("g", "r", "mp"))
    grad_spec = P(("g", "r"), "mp")
    stat_spec = P("mp", ("g", "r"), None, None, None)
    return jax.shard_map(
        shards,
        mesh=fine,
        in_specs=(grad_spec, P(), stat_spec, stat_spec),
        out_specs=(grad_spec, stat_spec, stat_spec),
        check_vma=False,
    )
```
